128 devices in a mesh: section: 2 (over y_lo), dp: 64 (over z, x, y_hi, core).
Axes of the slice: x: 4, y: 4 (y_hi: 2, y_lo: 2; y = y_hi * 2 + y_lo), z: 4, core: 2. Of those that a mesh axis runs over, the one named last changes fastest.
Arguments:
- boundary: bfloat16 [2, 65536, 512], P('section', 'dp'), may hold values from -6 to 6
- in_weights: bfloat16 [2, 512, 4096], P('section'), as said below
- down_weight: bfloat16 [2, 2048, 512], P('section'), may hold values from -0.25 to 0.25
- gains: bfloat16 [2, 2, 512], P('section'), may hold values from 0.5 to 1.5
- proj: bfloat16 [2, 512, 8], P('section'), as said below
- codebook: bfloat16 [8, 8192], P(None, ('section', 'dp')), may hold values from -4 to 4
- codes: int32 [65536], P('dp'), may hold values from 0 to 8191
- grids: int32 [128], P('dp'), may hold values from 0 to 2
- orders: int32 [128, 2], P('dp'), may hold values from 0 to 1, each once within a row
- avg_in: float32 [2, 512, 4096], P('section', 'dp'), may hold values from -0.3 to 0.3
- avg_down: float32 [2, 2048, 512], P('section', 'dp'), may hold values from -0.3 to 0.3
Outputs:
- boundary_out: bfloat16 [2, 65536, 512], P('section', 'dp')
- grad_in_weights: float32 [2, 512, 4096], P('section', 'dp')
- grad_down: float32 [2, 2048, 512], P('section', 'dp')
- grad_gains: float32 [2, 2, 512], P('section', None, 'dp')
- grad_proj: float32 [2, 512, 8], P('section', 'dp')
- grad_codebook: float32 [8, 8192], P(None, ('section', 'dp'))
- avg_in_new: float32 [2, 512, 4096], P('section', 'dp')
- avg_down_new: float32 [2, 2048, 512], P('section', 'dp')
The draws below stay inside these ranges and needn't reach their ends.
Inputs may be any that keep to these rules, and one draw needn't show every extreme that they name: grids: 0, 1 and 2 name the grids of 16 x 16, 8 x 32 and 32 x 8 patches (rows x columns). in_weights: independent entries, fan-in scaled. proj: independent entries, fan-in scaled.
All inputs are finite; a program needn't handle non-finite values.
Results may differ from the reference program's by a relative error of at most 0.025.
Values may be sent and summed in bfloat16 or wider, within the bound.
A program may use at most 192 MiB of HBM per device.

```python
import jax
import jax.numpy as jnp
from jax import lax

D = 512
HEADS = 8
HEAD = 64
FF = 2048
CODES = 8192
CODE_DIM = 8
WINDOW = 64
GRID = 256
FRAMES = 2
CLIP = 512
TOKENS = 65536
CLIPS = 128
HALF = 4096


def draw_in_weights(key, part):
    key = jax.random.fold_in(key, 11)
    dims_all = (2, D, 4 * D + FF)
    normal_draw = jnp.clip(jax.random.normal(key, dims_all, jnp.float32), -6.0, 6.0)
    column = lax.broadcasted_iota(jnp.int32, dims_all, 2)
    col_scale = jnp.where((column >= 3 * D) & (column < 4 * D), (D / 8.0) ** (-0.5), D ** (-0.5))
    return (normal_draw * col_scale).astype(jnp.bfloat16)


def draw_proj(key, part):
    key = jax.random.fold_in(key, 23)
    dims_all = (2, D, CODE_DIM)
    normal_draw = jnp.clip(jax.random.normal(key, dims_all, jnp.float32), -6.0, 6.0)
    section_no = lax.broadcasted_iota(jnp.int32, dims_all, 0)
    row_scale = jnp.where(section_no == 0, D ** (-0.5), CODE_DIM ** (-0.5))
    return (normal_draw * row_scale).astype(jnp.bfloat16)


def plant(values, own_key, low, largest):
    place = [jax.random.randint(jax.random.fold_in(own_key, axis), (), 0, length) for axis, length in enumerate(values.shape)]
    longest = values.shape.index(max(values.shape))
    beside = place[:longest] + [(place[longest] + 1) % values.shape[longest]] + place[longest + 1:]
    return values.at[tuple(place)].set(low).at[tuple(beside)].set(largest)


def block_levels(own_key, shape, shards, low, high):
    def one(position, blocks):
        heights = jax.random.uniform(jax.random.fold_in(jax.random.fold_in(own_key, 6), position), (blocks,), jnp.float32, low / len(shards), high / len(shards))
        return jnp.repeat(jnp.exp(heights), shape[position] // blocks).reshape((-1,) + (1,) * (len(shape) - position - 1))

    level = one(*shards[0])
    for cut in shards[1:]:
        level = level * one(*cut)
    return level


def gaussian(key, dims, scale, reach, split=(), held_as=jnp.bfloat16):
    drawn = scale * jax.random.normal(key, dims, jnp.float32)
    if split:
        drawn = drawn * block_levels(key, dims, split, -0.22, 0.18)
    return jnp.clip(drawn, -reach, reach).astype(held_as)


def setup_inputs(seed: int = 0) -> dict:
    arg_keys = jax.random.split(jax.random.key(seed), 12)
    return {
        "boundary": gaussian(arg_keys[0], (2, TOKENS, D), 1.0, 6.0, ((0, 2), (1, 64))),
        "in_weights": draw_in_weights(jax.random.fold_in(arg_keys[11], 71), 0),
        "down_weight": gaussian(arg_keys[2], (2, FF, D), (FF // 4) ** -0.5, 0.25, ((0, 2),)),
        "gains": jnp.clip(1.0 + 0.1 * jax.random.normal(arg_keys[3], (2, 2, D), jnp.float32), 0.5, 1.5).astype(jnp.bfloat16),
        "proj": draw_proj(jax.random.fold_in(arg_keys[11], 71), 0),
        "codebook": gaussian(arg_keys[5], (CODE_DIM, CODES), 1.0, 4.0, ((1, 128),)),
        "codes": plant(jax.random.randint(arg_keys[6], (TOKENS,), 0, CODES), jax.random.fold_in(arg_keys[6], 1), 0, CODES - 1).astype(jnp.int32),
        "grids": plant(jax.random.randint(arg_keys[7], (CLIPS,), 0, 3), jax.random.fold_in(arg_keys[7], 1), 0, 2).astype(jnp.int32),
        "orders": jax.vmap(lambda own: jax.random.permutation(own, FRAMES))(jax.random.split(arg_keys[8], CLIPS)).reshape((CLIPS, FRAMES)).astype(jnp.int32),
        "avg_in": gaussian(arg_keys[9], (2, D, 4 * D + FF), 0.05, 0.3, ((0, 2), (1, 64)), jnp.float32),
        "avg_down": gaussian(arg_keys[10], (2, FF, D), 0.05, 0.3, ((0, 2), (1, 64)), jnp.float32),
    }


@jax.custom_vjp
def low(v):
    return lax.optimization_barrier(v.astype(jnp.bfloat16)).astype(jnp.float32)

@jax.custom_vjp
def low_back(v):
    return v

def low_keep(v):
    return (low(v), None)

def low_pass(kept, grad):
    return (grad,)

def back_keep(v):
    return (v, None)

def back_low(kept, grad):
    return (low(grad),)
low.defvjp(low_keep, low_pass)
low_back.defvjp(back_keep, back_low)
MASKED_SCORE = -1e+30
NORM_EPS = 1e-05
AVG_DECAY = 0.9
LEARN_RATE = 0.0005

def matmul(left, right):
    return jnp.dot(left, right, precision=lax.Precision.HIGHEST)

def layer_norm(values, gain):
    row_mean = lax.optimization_barrier(jnp.mean(values, axis=-1, keepdims=True))
    centred = values - row_mean
    spread = lax.optimization_barrier(jnp.mean(centred * centred, axis=-1, keepdims=True))
    return centred * lax.rsqrt(spread + NORM_EPS) * gain

def gelu_tanh(values):
    return jax.nn.gelu(values, approximate=True)

def window_tables(grid_id):
    row_ids = jnp.arange(CLIP, dtype=jnp.int32)
    frame_no = row_ids // GRID
    cell_no = row_ids % GRID
    inner_no = row_ids % WINDOW
    window_no = cell_no // WINDOW
    width_cells = jnp.where(grid_id == 0, 16, jnp.where(grid_id == 1, 32, 8)).astype(jnp.int32)
    across = width_cells // 8
    source = frame_no * GRID + (window_no // across * 8 + inner_no // 8) * width_cells + window_no % across * 8 + inner_no % 8
    row_no = cell_no // width_cells
    col_no = cell_no % width_cells
    target = frame_no * GRID + (row_no // 8 * across + col_no // 8) * WINDOW + row_no % 8 * 8 + col_no % 8
    return (source, target)

def frame_tables(order_row):
    row_ids = jnp.arange(CLIP, dtype=jnp.int32)
    frame_no = row_ids // GRID
    cell_no = row_ids % GRID
    inner_no = row_ids % WINDOW
    group_no = row_ids // WINDOW
    span_cells = WINDOW // FRAMES
    source = inner_no % FRAMES * GRID + group_no * span_cells + inner_no // FRAMES
    target = cell_no // span_cells * WINDOW + cell_no % span_cells * FRAMES + frame_no
    slot_no = jnp.arange(WINDOW, dtype=jnp.int32)
    time_of = order_row[slot_no % FRAMES]
    allowed = (slot_no[:, None] // FRAMES == slot_no[None, :] // FRAMES) & (time_of[None, :] <= time_of[:, None])
    return (source, target, allowed)

def block_pass(hidden, gain_pair, w_in, w_down, allowed):
    norm_one = low(layer_norm(hidden, gain_pair[0]))
    packed = low_back(matmul(norm_one, w_in[:, :3 * D]))
    queries = low(packed[:, :D]).reshape(-1, WINDOW, HEADS, HEAD)
    keys_now = low(packed[:, D:2 * D]).reshape(-1, WINDOW, HEADS, HEAD)
    values_now = low(packed[:, 2 * D:]).reshape(-1, WINDOW, HEADS, HEAD)
    scores = jnp.einsum('gqhd,gkhd->ghqk', queries, keys_now, precision=lax.Precision.HIGHEST)
    scores = low_back(scores * HEAD ** (-0.5))
    scores = jnp.where(allowed[None, None], scores, MASKED_SCORE)
    top_row = lax.optimization_barrier(jnp.max(scores, axis=-1, keepdims=True))
    expo_rows = jnp.exp(scores - top_row)
    prob_rows = expo_rows / lax.optimization_barrier(jnp.sum(expo_rows, axis=-1, keepdims=True))
    mixed_heads = jnp.einsum('ghqk,gkhd->gqhd', low(prob_rows), values_now, precision=lax.Precision.HIGHEST)
    attended = low(low_back(mixed_heads)).reshape(-1, D)
    mixed_rows = hidden + low_back(matmul(attended, w_in[:, 3 * D:4 * D]))
    norm_two = low(layer_norm(mixed_rows, gain_pair[1]))
    up_proj = low_back(matmul(norm_two, w_in[:, 4 * D:]))
    activated = low(gelu_tanh(up_proj))
    return mixed_rows + low_back(matmul(activated, w_down))

def clip_pass(params, clip_patches, clip_codes, grid_id, order_row):
    w_in, w_down, gains, proj, book = params
    enc_source, enc_target = window_tables(grid_id)
    dec_source, dec_target, dec_allowed = frame_tables(order_row)
    every_pair = jnp.ones((WINDOW, WINDOW), dtype=jnp.bool_)
    encoded = block_pass(clip_patches[enc_source], gains[0], w_in[0], w_down[0], every_pair)[enc_target]
    code_vec = matmul(low(encoded), proj[0])
    entry = jnp.take(book, clip_codes, axis=1).T
    lower = (clip_codes < HALF)[:, None]
    sent = low(code_vec + jnp.where(lower, entry, 0.0))
    quantized = low_back(sent + jnp.where(lower, 0.0, entry))
    dec_start = low_back(matmul(low(quantized), proj[1].T))
    return block_pass(dec_start[dec_source], gains[1], w_in[1], w_down[1], dec_allowed)[dec_target]

def reference(boundary, in_weights, down_weight, gains, proj, codebook, codes, grids, orders, avg_in, avg_down):
    patches = boundary[0].astype(jnp.float32).reshape(CLIPS, CLIP, D)
    cotangent = boundary[1].astype(jnp.float32).reshape(CLIPS, CLIP, D)
    params = (in_weights.astype(jnp.float32), down_weight.astype(jnp.float32), gains.astype(jnp.float32), proj.astype(jnp.float32), codebook.astype(jnp.float32))
    clip_codes = codes.reshape(CLIPS, CLIP)

    def forward_all(weights_now, patch_rows):

        def one_clip(item):
            return jax.checkpoint(clip_pass)(weights_now, item[0], item[1], item[2], item[3])
        return lax.map(one_clip, (patch_rows, clip_codes, grids, orders))
    decoded, pull_back = jax.vjp(forward_all, params, patches)
    grad_params, grad_patches = pull_back(cotangent)
    boundary_out = jnp.stack([grad_patches.reshape(TOKENS, D), decoded.reshape(TOKENS, D)]).astype(jnp.bfloat16)
    grad_in, grad_dn, grad_gn, grad_pj, grad_bk = grad_params
    avg_in_new = AVG_DECAY * avg_in + (1.0 - AVG_DECAY) * (params[0] - LEARN_RATE * grad_in)
    avg_down_new = AVG_DECAY * avg_down + (1.0 - AVG_DECAY) * (params[1] - LEARN_RATE * grad_dn)
    return (boundary_out, grad_in, grad_dn, grad_gn, grad_pj, grad_bk, avg_in_new, avg_down_new)
```

```python
import functools

import jax
import jax.numpy as jnp
from jax import lax
from jax.experimental import pallas as pl
from jax.experimental.pallas import tpu as pltpu
from jax.sharding import PartitionSpec as P

BF = jnp.bfloat16
F32 = jnp.float32
I32 = jnp.int32
MESH = pl.DeviceIdType.MESH

D = 512
FF = 2048
CLIP = 512
GRID = 256
WINDOW = 64
HALF = 4096
NORM_EPS = 1e-05
AVG_DECAY = 0.9
LEARN_RATE = 0.0005
SCALE = 0.125
RC = 256

CHUNKS = {"a": (128, 256), "b": (32, 1024), "c": (32, 1024)}


def nn(left, right):
    return lax.dot_general(left, right, (((1,), (0,)), ((), ())), preferred_element_type=F32)


def nt(left, right):
    return lax.dot_general(left, right, (((1,), (1,)), ((), ())), preferred_element_type=F32)


def tn(left, right):
    return lax.dot_general(left, right, (((0,), (0,)), ((), ())), preferred_element_type=F32)


def tt(left, right):
    return lax.dot_general(left, right, (((0,), (1,)), ((), ())), preferred_element_type=F32)


def iota(shape, axis):
    return lax.broadcasted_iota(I32, shape, axis)


def normed(h):
    mean = jnp.mean(h, axis=-1, keepdims=True)
    c = h - mean
    var = jnp.mean(c * c, axis=-1, keepdims=True)
    r = lax.rsqrt(var + NORM_EPS)
    return c * r, r


def normed_back(grad, xhat, r, gain):
    t = grad * gain
    m1 = jnp.mean(t, axis=-1, keepdims=True)
    m2 = jnp.mean(t * xhat, axis=-1, keepdims=True)
    return r * (t - m1 - xhat * m2)


def gelu_pair(u):
    c0 = 0.7978845608028654
    c1 = 0.7978845608028654 * 0.044715
    u2 = u * u
    t = jnp.tanh(u * (c0 + c1 * u2))
    hu = 0.5 * u
    ht = 0.5 + 0.5 * t
    value = hu + hu * t
    slope = ht + hu * (1.0 - t * t) * (c0 + (3.0 * c1) * u2)
    return value, slope


def ten_shapes():
    shapes = {
        "xs": ((2, CLIP, D), BF),
        "win": ((D, 4 * D + FF), BF),
        "wdn": ((FF, D), BF),
        "perm": ((2, GRID, GRID), BF),
        "bd1": ((256, 256), BF),
        "bds": ((256, 256), BF),
        "bdf": ((256, 256), F32),
        "tbl": ((64, 8, 128), F32),
        "cds": ((2, 8, CLIP), I32),
        "cxs": ((2, 16, CLIP), BF),
        "cxr": ((2, 16, CLIP), BF),
        "ent": ((2, 8, CLIP), F32),
        "cvec": ((2, 16, CLIP), BF),
        "hb": ((CLIP, D), F32),
        "gg": ((CLIP, D), F32),
        "gob": ((CLIP, D), BF),
        "xh1": ((2, CLIP, D), F32),
        "xh2": ((2, CLIP, D), F32),
        "r1": ((2, CLIP, 1), F32),
        "r2": ((2, CLIP, 1), F32),
        "a1": ((2, CLIP, D), BF),
        "a2": ((2, CLIP, D), BF),
        "qkv": ((2, CLIP, 3 * D), BF),
        "prob": ((2, CLIP, D), F32),
        "att": ((2, CLIP, D), BF),
        "act": ((2, CLIP, FF), BF),
        "gel": ((2, CLIP, FF), BF),
        "gy": ((2, CLIP, D), BF),
        "eb": ((2, CLIP, D), BF),
        "acc_dn": ((FF, D), F32),
        "acc_up": ((D, FF), F32),
        "acc_qkv": ((D, 3 * D), F32),
        "acc_out": ((D, D), F32),
        "s_acc": ((4, 8, 2, 8, 128), F32),
        "gacc": ((2, 8, D), F32),
        "s0": ((4, 8, 8, 128), F32),
        "s1": ((3, 8, 8, 128), F32),
        "s2": ((3, 2, 8, 128), F32),
        "s3": ((8, 128), F32),
    }
    for k, (rows, w) in CHUNKS.items():
        h = w // 2
        shapes["sb0" + k] = ((4, 4, rows, w), BF)
        shapes["r0" + k] = ((4, 4, rows, w), BF)
        shapes["r1z" + k] = ((3, 4, rows, h), BF)
        shapes["r1x" + k] = ((3, 4, rows, h), BF)
        shapes["r2a" + k] = ((3, rows, h), BF)
        shapes["r2b" + k] = ((3, rows, h), BF)
        shapes["t3" + k] = ((rows, w), F32)
        shapes["sb3" + k] = ((rows // 2, w), BF)
        shapes["r3" + k] = ((rows // 2, w), BF)
        shapes["t4" + k] = ((rows // 2, w), F32)
        shapes["r4" + k] = ((rows // 4, w), F32)
    return shapes


SHAPES = ten_shapes()
N_SEM = 80


class Refs:
    pass


def mega(
    x_hbm, win_hbm, wdn_hbm, gains_ref, proj_ref, book_ref, codes_ref, grids_ref, orders_ref,
    avgin_ref, avgdn_ref,
    bout_ref, gin_ref, gdn_ref, ggain_ref, gproj_ref, gbook_ref, ain_ref, adn_ref,
    *scratch,
):
    s = Refs()
    for name, ref in zip(SHAPES, scratch):
        setattr(s, name, ref)
    send_sems, recv_sems, load_sems = scratch[len(SHAPES):]

    sec = lax.axis_index("section")
    dp = lax.axis_index("dp")
    core = dp % 2
    yh = (dp // 2) % 2
    x = (dp // 4) % 4
    z = dp // 16
    is_e = sec == 0
    is_d = sec == 1

    def place(zz, xx, yy, cc):
        return (sec, ((zz * 4 + xx) * 2 + yy) * 2 + cc)

    core_dev = place(z, x, yh, 1 - core)
    y_dev = place(z, x, 1 - yh, core)
    z_dev = [place((z + d) % 4, x, yh, core) for d in (1, 2, 3)]
    x_dev = [place(z, (x + d) % 4, yh, core) for d in (1, 2, 3)]
    sec_dev = (1 - sec, dp)

    counter = [0]
    slots = {}

    def rcopy(key, src, dst, dev):
        if key not in slots:
            slots[key] = counter[0]
            counter[0] += 1
        i = slots[key]
        return pltpu.make_async_remote_copy(
            src_ref=src, dst_ref=dst, send_sem=send_sems.at[i], recv_sem=recv_sems.at[i],
            device_id=dev, device_id_type=MESH,
        )

    loads = [
        pltpu.make_async_copy(x_hbm.at[0, pl.ds(0, CLIP)], s.xs.at[0], load_sems.at[0]),
        pltpu.make_async_copy(x_hbm.at[0, pl.ds(CLIP, CLIP)], s.xs.at[1], load_sems.at[1]),
        pltpu.make_async_copy(win_hbm.at[0], s.win, load_sems.at[2]),
        pltpu.make_async_copy(wdn_hbm.at[0], s.wdn, load_sems.at[3]),
    ]
    for load in loads:
        load.start()

    barrier = pltpu.get_barrier_semaphore()
    peers = [core_dev, y_dev, sec_dev] + z_dev + x_dev
    for dev in peers:
        pl.semaphore_signal(barrier, inc=1, device_id=dev, device_id_type=MESH)

    rows_i = iota((256, 256), 0)
    cols_i = iota((256, 256), 1)
    same = ((rows_i >> 6) == (cols_i >> 6)).astype(F32)
    s.bdf[...] = same * SCALE
    s.bd1[...] = same.astype(BF)
    s.bds[...] = (same * SCALE).astype(BF)
    for c in range(2):
        code_row = jnp.concatenate([codes_ref[4 * c + k : 4 * c + k + 1, :] for k in range(4)], axis=1)
        s.cds[c] = jnp.broadcast_to(code_row - sec * HALF, (8, CLIP))

    gain_one = gains_ref[0, 0:1, :].astype(F32)
    gain_two = gains_ref[0, 1:2, :].astype(F32)
    book = book_ref[...].astype(F32)
    s.tbl[dp] = jnp.concatenate([book, jnp.zeros((8, 64), F32)], axis=1)
    s.gacc[...] = jnp.zeros((2, 8, D), F32)
    s.s_acc[...] = jnp.zeros((4, 8, 2, 8, 128), F32)

    pl.semaphore_wait(barrier, len(peers))

    def ag_copies(step):
        if step == 0:
            part = s.tbl.at[dp]
            return [rcopy("ag0", part, part, core_dev)]
        if step == 1:
            part = s.tbl.at[pl.ds((dp // 2) * 2, 2)]
            return [rcopy("ag1", part, part, y_dev)]
        if step == 2:
            part = s.tbl.at[pl.ds((dp // 4) * 4, 4)]
            return [rcopy("ag2%d" % i, part, part, x_dev[i]) for i in range(3)]
        part = s.tbl.at[pl.ds((dp // 16) * 16, 16)]
        return [rcopy("ag3%d" % i, part, part, z_dev[i]) for i in range(3)]

    def ag_arrivals(step):
        if step == 0:
            part = s.tbl.at[dp + 1 - 2 * core]
            return [rcopy("ag0", part, part, core_dev)]
        if step == 1:
            part = s.tbl.at[pl.ds((dp // 4) * 4 + (1 - yh) * 2, 2)]
            return [rcopy("ag1", part, part, y_dev)]
        if step == 2:
            parts = [s.tbl.at[pl.ds(z * 16 + ((x + 3 - i) % 4) * 4, 4)] for i in range(3)]
            return [rcopy("ag2%d" % i, parts[i], parts[i], x_dev[i]) for i in range(3)]
        parts = [s.tbl.at[pl.ds(((z + 3 - i) % 4) * 16, 16)] for i in range(3)]
        return [rcopy("ag3%d" % i, parts[i], parts[i], z_dev[i]) for i in range(3)]

    def ag_start(step):
        for cp in ag_copies(step):
            cp.start()

    def ag_wait(step):
        for cp in ag_arrivals(step):
            cp.wait_recv()
        for cp in ag_copies(step):
            cp.wait_send()

    def onehots(c):
        code_row = s.cds[c][0:1, :]
        hi = code_row >> 6
        lo = code_row & 63
        lo_one = (iota((128, CLIP), 0) == lo).astype(F32).astype(BF)
        hi_mask = (iota((CLIP, CLIP), 0) >> 3) == hi
        return lo_one, hi_mask

    def entries(c):
        lo_one, hi_mask = onehots(c)
        table = s.tbl[...].reshape(CLIP, 128).astype(BF)
        picked = jnp.where(hi_mask, nn(table, lo_one), 0.0)
        s.ent[c] = jnp.sum(picked.reshape(64, 8, CLIP), axis=0)

    def pad16(v):
        return jnp.concatenate([v, jnp.zeros((8, v.shape[1]), F32)], axis=0).astype(BF)

    def book_proj_terms(c, code_grad, wide_rows, narrow):
        lo_one, hi_mask = onehots(c)
        spread = jnp.broadcast_to(code_grad[None], (64, 8, CLIP)).reshape(CLIP, CLIP)
        left = jnp.where(hi_mask, spread, 0.0).astype(BF)
        total = nt(left, lo_one)
        narrow_wide = jnp.concatenate(
            [jnp.zeros((64, CLIP), F32), narrow, jnp.zeros((56, CLIP), F32)], axis=0
        ).astype(BF)
        total = total + tt(wide_rows, narrow_wide)
        s.s_acc[...] += total.reshape(4, 8, 2, 8, 128)

    def norm_qkv(c, rows, h):
        s.hb[rows] = h
        xh, r = normed(h)
        s.xh1[c, rows] = xh
        s.r1[c, rows] = r
        a = (xh * gain_one).astype(BF)
        s.a1[c, rows] = a
        for j in range(3):
            s.qkv[c, rows, 512 * j : 512 * j + 512] = nn(a, s.win[:, 512 * j : 512 * j + 512]).astype(BF)

    def feed_forward(c, put):
        def step(i, carry):
            rows = pl.ds(i * RC, RC)
            m = s.hb[rows] + nn(s.att[c, rows], s.win[:, 1536:2048])
            xh, r = normed(m)
            s.xh2[c, rows] = xh
            s.r2[c, rows] = r
            a = (xh * gain_two).astype(BF)
            s.a2[c, rows] = a
            acc = m
            for j in range(4):
                cols = slice(512 * j, 512 * j + 512)
                u = nn(a, s.win[:, 2048 + 512 * j : 2560 + 512 * j])
                value, slope = gelu_pair(u)
                value = value.astype(BF)
                s.act[c, rows, cols] = value
                s.gel[c, rows, cols] = slope.astype(BF)
                acc = acc + nn(value, s.wdn[cols, :])
            put(rows, acc)
            return carry

        lax.fori_loop(0, CLIP // RC, step, 0)

    def window_forward(c):
        def step(w, carry):
            rows = pl.ds(w * WINDOW, WINDOW)
            for quad in range(2):
                cols = slice(256 * quad, 256 * quad + 256)
                q4 = s.qkv[c, rows, 256 * quad : 256 * quad + 256]
                k4 = s.qkv[c, rows, 512 + 256 * quad : 768 + 256 * quad]
                v4 = s.qkv[c, rows, 1024 + 256 * quad : 1280 + 256 * quad]
                q_wide = jnp.concatenate([q4] * 4, axis=0) * s.bds[...]
                scores = nt(k4, q_wide)
                top = jnp.max(scores, axis=0, keepdims=True)
                e = jnp.exp(scores - top)
                p = e * (1.0 / jnp.sum(e, axis=0, keepdims=True))
                s.prob[c, rows, cols] = p
                wide = tn(p.astype(BF), v4) * s.bdf[...]
                out = (wide[0:64] + wide[64:128]) + (wide[128:192] + wide[192:256])
                s.att[c, rows, cols] = (out * (1.0 / SCALE)).astype(BF)
            return carry

        lax.fori_loop(0, CLIP // WINDOW, step, 0)

    def window_backward(c):
        def step(w, carry):
            rows = pl.ds(w * WINDOW, WINDOW)
            for quad in range(2):
                cols = slice(256 * quad, 256 * quad + 256)
                qc = slice(256 * quad, 256 * quad + 256)
                kc = slice(512 + 256 * quad, 768 + 256 * quad)
                vc = slice(1024 + 256 * quad, 1280 + 256 * quad)
                q4 = s.qkv[c, rows, qc]
                k4 = s.qkv[c, rows, kc]
                v4 = s.qkv[c, rows, vc]
                go = s.gob[rows, cols]
                p = s.prob[c, rows, cols]
                go_wide = jnp.concatenate([go] * 4, axis=0) * s.bd1[...]
                q_wide = jnp.concatenate([q4] * 4, axis=0) * s.bds[...]
                gp = nt(v4, go_wide)
                gs = (p * (gp - jnp.sum(gp * p, axis=0, keepdims=True))).astype(BF)
                s.qkv[c, rows, vc] = nn(p.astype(BF), go_wide).astype(BF)
                s.qkv[c, rows, kc] = nn(gs, q_wide).astype(BF)
                wide = tn(gs, k4) * s.bdf[...]
                out = (wide[0:64] + wide[64:128]) + (wide[128:192] + wide[192:256])
                s.qkv[c, rows, qc] = out.astype(BF)
            return carry

        lax.fori_loop(0, CLIP // WINDOW, step, 0)

    def head_sums(v):
        hi = v.astype(BF)
        lo = (v - hi.astype(F32)).astype(BF)
        return nn(hi, s.bd1[...]) + nn(lo, s.bd1[...])

    CR = 128

    def frames_forward(c):
        late0 = orders_ref[c, 0] > orders_ref[c, 1]
        sign = jnp.where(late0, 1.0, -1.0).astype(F32)

        def step(i, carry):
            r0 = pl.ds(i * CR, CR)
            r1 = pl.ds(GRID + i * CR, CR)
            for quad in range(2):
                qc = slice(256 * quad, 256 * quad + 256)
                kc = slice(512 + 256 * quad, 768 + 256 * quad)
                vc = slice(1024 + 256 * quad, 1280 + 256 * quad)
                q_late = jnp.where(late0, s.qkv[c, r0, qc].astype(F32), s.qkv[c, r1, qc].astype(F32))
                k_diff = sign * (s.qkv[c, r1, kc].astype(F32) - s.qkv[c, r0, kc].astype(F32))
                v0 = s.qkv[c, r0, vc].astype(F32)
                v1 = s.qkv[c, r1, vc].astype(F32)
                d = head_sums(q_late * k_diff) * SCALE
                e = jnp.exp(-jnp.abs(d))
                big = 1.0 / (1.0 + e)
                small = e * big
                p_other = jnp.where(d > 0.0, big, small)
                p_self = jnp.where(d > 0.0, small, big)
                s.prob[c, r0, qc] = p_other
                s.prob[c, r1, qc] = p_self
                po = p_other.astype(BF).astype(F32)
                ps = p_self.astype(BF).astype(F32)
                v_late = jnp.where(late0, v0, v1)
                v_early = jnp.where(late0, v1, v0)
                mix = ps * v_late + po * v_early
                s.att[c, r0, qc] = jnp.where(late0, mix, v0).astype(BF)
                s.att[c, r1, qc] = jnp.where(late0, v1, mix).astype(BF)
            return carry

        lax.fori_loop(0, GRID // CR, step, 0)

    def frames_backward(c):
        late0 = orders_ref[c, 0] > orders_ref[c, 1]
        sign = jnp.where(late0, 1.0, -1.0).astype(F32)

        def step(i, carry):
            r0 = pl.ds(i * CR, CR)
            r1 = pl.ds(GRID + i * CR, CR)
            for quad in range(2):
                qc = slice(256 * quad, 256 * quad + 256)
                kc = slice(512 + 256 * quad, 768 + 256 * quad)
                vc = slice(1024 + 256 * quad, 1280 + 256 * quad)
                q_late = jnp.where(late0, s.qkv[c, r0, qc].astype(F32), s.qkv[c, r1, qc].astype(F32))
                k_diff = sign * (s.qkv[c, r1, kc].astype(F32) - s.qkv[c, r0, kc].astype(F32))
                v_diff = sign * (s.qkv[c, r1, vc].astype(F32) - s.qkv[c, r0, vc].astype(F32))
                go0 = s.gob[r0, qc].astype(F32)
                go1 = s.gob[r1, qc].astype(F32)
                go_late = jnp.where(late0, go0, go1)
                go_early = jnp.where(late0, go1, go0)
                p_other = s.prob[c, r0, qc]
                p_self = s.prob[c, r1, qc]
                gs = p_other * p_self * head_sums(go_late * v_diff)
                gs = gs.astype(BF).astype(F32) * SCALE
                gq = gs * k_diff
                gk = gs * q_late
                gv_late = p_self.astype(BF).astype(F32) * go_late
                gv_early = go_early + p_other.astype(BF).astype(F32) * go_late
                s.qkv[c, r0, qc] = jnp.where(late0, gq, 0.0).astype(BF)
                s.qkv[c, r1, qc] = jnp.where(late0, 0.0, gq).astype(BF)
                s.qkv[c, r0, kc] = (-sign * gk).astype(BF)
                s.qkv[c, r1, kc] = (sign * gk).astype(BF)
                s.qkv[c, r0, vc] = jnp.where(late0, gv_late, gv_early).astype(BF)
                s.qkv[c, r1, vc] = jnp.where(late0, gv_early, gv_late).astype(BF)
            return carry

        lax.fori_loop(0, GRID // CR, step, 0)

    def gain_terms(which, grad, xhat):
        part = jnp.sum((grad * xhat).reshape(-1, 8, D), axis=0)
        s.gacc[which] += part

    def back_ff(c, grad_of):
        def step(i, carry):
            rows = pl.ds(i * RC, RC)
            gz = s.xs[c, rows]
            acc = None
            for j in range(4):
                cols = slice(512 * j, 512 * j + 512)
                gu = (nt(gz, s.wdn[cols, :]) * s.gel[c, rows, cols].astype(F32)).astype(BF)
                s.gel[c, rows, cols] = gu
                term = nt(gu, s.win[:, 2048 + 512 * j : 2560 + 512 * j])
                acc = term if acc is None else acc + term
            xh = s.xh2[c, rows]
            gain_terms(1, acc, xh)
            gm = grad_of(rows) + normed_back(acc, xh, s.r2[c, rows], gain_two)
            s.hb[rows] = gm
            gy = gm.astype(BF)
            s.gy[c, rows] = gy
            s.gob[rows] = nt(gy, s.win[:, 1536:2048]).astype(BF)
            return carry

        lax.fori_loop(0, CLIP // RC, step, 0)

    def back_in(c, put):
        def step(i, carry):
            rows = pl.ds(i * RC, RC)
            acc = None
            for j in range(3):
                cols = slice(512 * j, 512 * j + 512)
                term = nt(s.qkv[c, rows, cols], s.win[:, cols])
                acc = term if acc is None else acc + term
            xh = s.xh1[c, rows]
            gain_terms(0, acc, xh)
            put(rows, s.hb[rows] + normed_back(acc, xh, s.r1[c, rows], gain_one))
            return carry

        lax.fori_loop(0, CLIP // RC, step, 0)

    def add_into(ref, rows, cols, c, value):
        ref[rows, cols] = jnp.where(c == 0, value, ref[rows, cols] + value)

    def grad_down(c):
        for j in range(4):
            cols = slice(512 * j, 512 * j + 512)
            add_into(s.acc_dn, cols, slice(None), c, tn(s.act[c, :, cols], s.xs[c]))

    def grad_up(c):
        for j in range(4):
            cols = slice(512 * j, 512 * j + 512)
            add_into(s.acc_up, slice(None), cols, c, tn(s.a2[c], s.gel[c, :, cols]))

    def grad_attn(c):
        for j in range(3):
            cols = slice(512 * j, 512 * j + 512)
            add_into(s.acc_qkv, slice(None), cols, c, tn(s.a1[c], s.qkv[c, :, cols]))
        add_into(s.acc_out, slice(None), slice(None), c, tn(s.att[c], s.gy[c]))

    def load_half(k, i, half):
        if k == "a":
            return s.acc_dn[pl.ds(i * 128, 128), pl.ds(pl.multiple_of(half * 256, 128), 256)]
        rows = pl.ds(i * 32, 32)
        if k == "b":
            return s.acc_up[rows, pl.ds(pl.multiple_of(half * 1024, 128), 1024)]
        return jnp.concatenate(
            [
                s.acc_qkv[rows, pl.ds(pl.multiple_of(half * 768, 128), 768)],
                s.acc_out[rows, pl.ds(pl.multiple_of(half * 256, 128), 256)],
            ],
            axis=1,
        )

    def buf(name, k):
        return getattr(s, name + k)

    def copies(k, step):
        if k == "s":
            if step == 0:
                return [rcopy("s0", s.s_acc.at[:, :, 1 - core], s.s0, core_dev)]
            if step == 1:
                return [rcopy("s1%d" % i, s.s0.at[(z + 1 + i) % 4], s.s1.at[i], z_dev[i]) for i in range(3)]
            if step == 2:
                return [
                    rcopy("s2%d" % i, s.s0.at[z, pl.ds(2 * ((x + 1 + i) % 4), 2)], s.s2.at[i], x_dev[i])
                    for i in range(3)
                ]
            if step == 3:
                return [rcopy("s3", s.s0.at[z, 2 * x + 1 - yh], s.s3, y_dev)]
            return []
        rows, w = CHUNKS[k]
        h = w // 2
        r0 = buf("r0", k)
        if step == 0:
            return [rcopy(k + "0", buf("sb0", k), r0, core_dev)]
        if step == 1:
            return [
                rcopy(k + "1z%d" % i, r0.at[(z + 1 + i) % 4, :, :, pl.ds(0, h)], buf("r1z", k).at[i], z_dev[i])
                for i in range(3)
            ] + [
                rcopy(k + "1x%d" % i, r0.at[:, (x + 1 + i) % 4, :, pl.ds(h, h)], buf("r1x", k).at[i], x_dev[i])
                for i in range(3)
            ]
        if step == 2:
            return [
                rcopy(k + "2x%d" % i, r0.at[z, (x + 1 + i) % 4, :, pl.ds(0, h)], buf("r2a", k).at[i], x_dev[i])
                for i in range(3)
            ] + [
                rcopy(k + "2z%d" % i, r0.at[(z + 1 + i) % 4, x, :, pl.ds(h, h)], buf("r2b", k).at[i], z_dev[i])
                for i in range(3)
            ]
        if step == 3:
            return [rcopy(k + "3", buf("sb3", k), buf("r3", k), y_dev)]
        quarter = rows // 4
        return [rcopy(k + "4", buf("t4", k).at[pl.ds((1 - core) * quarter, quarter)], buf("r4", k), core_dev)]

    def arrived(k, step):
        for cp in copies(k, step):
            cp.wait_recv()

    def send(k, step):
        for cp in copies(k, step):
            cp.start()

    def reduce_step(k, step):
        if step > 0:
            arrived(k, step - 1)
        if k == "s":
            if step == 1:
                s.s0[...] += s.s_acc[:, :, core]
            elif step == 2:
                s.s0[z] += (s.s1[0] + s.s1[1]) + s.s1[2]
            elif step == 3:
                here = pl.ds(2 * x, 2)
                s.s0[z, here] += (s.s2[0] + s.s2[1]) + s.s2[2]
            elif step == 4:
                final = s.s0[z, 2 * x + yh] + s.s3[...]
                gbook_ref[...] = final[:, 0:64]
                gproj_ref[0] = final[:, 64:72]
                ggain_ref[0] = jnp.transpose(jnp.concatenate([final] * 16, axis=0))[72:74, 0:8]
                return
            send(k, step)
            return
        rows, w = CHUNKS[k]
        h = w // 2
        r0 = buf("r0", k)
        if step == 0:
            sb0 = buf("sb0", k)

            def body(i, carry):
                sb0[i // 4, i % 4] = load_half(k, i, 1 - core).astype(BF)
                return carry

            lax.fori_loop(0, 16, body, 0)
        elif step == 1:

            def body(i, carry):
                r0[i // 4, i % 4] = (load_half(k, i, core) + r0[i // 4, i % 4].astype(F32)).astype(BF)
                return carry

            lax.fori_loop(0, 16, body, 0)
        elif step == 2:
            rz = buf("r1z", k)
            rx = buf("r1x", k)

            def body(i, carry):
                r0[z, i, :, pl.ds(0, h)] = (
                    (r0[z, i, :, pl.ds(0, h)].astype(F32) + rz[0, i].astype(F32))
                    + (rz[1, i].astype(F32) + rz[2, i].astype(F32))
                ).astype(BF)
                r0[i, x, :, pl.ds(h, h)] = (
                    (r0[i, x, :, pl.ds(h, h)].astype(F32) + rx[0, i].astype(F32))
                    + (rx[1, i].astype(F32) + rx[2, i].astype(F32))
                ).astype(BF)
                return carry

            lax.fori_loop(0, 4, body, 0)
        elif step == 3:
            ra = buf("r2a", k)
            rb = buf("r2b", k)
            t3 = buf("t3", k)
            t3[:, :h] = (r0[z, x, :, pl.ds(0, h)].astype(F32) + ra[0].astype(F32)) + (
                ra[1].astype(F32) + ra[2].astype(F32)
            )
            t3[:, h:] = (r0[z, x, :, pl.ds(h, h)].astype(F32) + rb[0].astype(F32)) + (
                rb[1].astype(F32) + rb[2].astype(F32)
            )
            buf("sb3", k)[...] = t3[pl.ds((1 - yh) * (rows // 2), rows // 2), :].astype(BF)
        elif step == 4:
            t3 = buf("t3", k)
            buf("t4", k)[...] = t3[pl.ds(yh * (rows // 2), rows // 2), :] + buf("r3", k)[...].astype(F32)
        else:
            quarter = rows // 4
            mine = buf("t4", k)[pl.ds(core * quarter, quarter), :]
            other = buf("r4", k)[...]
            if k == "a":
                gdn_ref[0, :, pl.ds(pl.multiple_of(core * 256, 128), 256)] = mine
                gdn_ref[0, :, pl.ds(pl.multiple_of((1 - core) * 256, 128), 256)] = other
                piece = s.wdn[pl.ds(dp * 32, 32), :].astype(F32)
                adn_ref[0] = AVG_DECAY * avgdn_ref[0] + (1.0 - AVG_DECAY) * (
                    piece - LEARN_RATE * gdn_ref[0]
                )
            elif k == "b":
                gin_ref[0, :, pl.ds(pl.multiple_of(2048 + core * 1024, 128), 1024)] = mine
                gin_ref[0, :, pl.ds(pl.multiple_of(2048 + (1 - core) * 1024, 128), 1024)] = other
            else:
                gin_ref[0, :, pl.ds(pl.multiple_of(core * 768, 128), 768)] = mine[:, :768]
                gin_ref[0, :, pl.ds(pl.multiple_of((1 - core) * 768, 128), 768)] = other[:, :768]
                gin_ref[0, :, pl.ds(pl.multiple_of(1536 + core * 256, 128), 256)] = mine[:, 768:]
                gin_ref[0, :, pl.ds(pl.multiple_of(1536 + (1 - core) * 256, 128), 256)] = other[:, 768:]
            return
        send(k, step)

    def code_copy(c):
        return pltpu.make_async_remote_copy(
            src_ref=s.cxs.at[c], dst_ref=s.cxr.at[c], send_sem=send_sems.at[N_SEM - 2 + c],
            recv_sem=recv_sems.at[N_SEM - 2 + c], device_id=sec_dev, device_id_type=MESH,
        )

    for load in loads:
        load.wait()
    ag_start(0)

    @pl.when(is_e)
    def _():
        for c in range(2):
            grid_now = grids_ref[c]
            width = jnp.where(grid_now == 0, 16, jnp.where(grid_now == 1, 32, 8)).astype(I32)
            log_across = jnp.where(grid_now == 0, 1, jnp.where(grid_now == 1, 2, 0)).astype(I32)
            across_mask = jnp.where(grid_now == 0, 1, jnp.where(grid_now == 1, 3, 0)).astype(I32)
            window_no = rows_i >> 6
            inner = rows_i & 63
            source = (
                ((window_no >> log_across) * 8 + (inner >> 3)) * width
                + (window_no & across_mask) * 8
                + (inner & 7)
            )
            s.perm[c] = (source == cols_i).astype(F32).astype(BF)

        def forward(c, carry):
            for f in range(2):
                rows = slice(GRID * f, GRID * f + GRID)
                norm_qkv(c, rows, nn(s.perm[c], s.xs[c, rows]))

            @pl.when(c == 0)
            def _():
                ag_wait(0)
                ag_start(1)

            window_forward(c)

            @pl.when(c == 0)
            def _():
                ag_wait(1)
                ag_start(2)

            def put(rows, acc):
                s.eb[c, rows] = acc.astype(BF)

            feed_forward(c, put)

            @pl.when(c == 0)
            def _():
                ag_wait(2)
                ag_start(3)
                ag_wait(3)

            entries(c)
            entry = s.ent[c]
            vec = tt(proj_ref[0], s.eb[c])
            for f in range(2):
                cols = slice(GRID * f, GRID * f + GRID)
                entry_enc = nt(pad16(entry[:, cols]), s.perm[c])[0:8]
                sent = pad16(vec[:, cols] + entry_enc)
                s.cxs[c, :, cols] = nn(sent, s.perm[c]).astype(BF)
            code_copy(c).start()
            return carry

        lax.fori_loop(0, 2, forward, 0)

    @pl.when(is_d)
    def _():
        for step in range(4):
            ag_wait(step)
            if step < 3:
                ag_start(step + 1)
        for c in range(2):
            entries(c)

        def both(c, carry):
            code_copy(c).wait_recv()
            quant = s.cxr[c][0:8].astype(F32) + s.ent[c]
            s.cvec[c] = pad16(quant)
            for f in range(2):
                rows = slice(GRID * f, GRID * f + GRID)
                h = tt(s.cvec[c][0:8, rows], proj_ref[0])
                norm_qkv(c, rows, h)
            frames_forward(c)

            def put(rows, acc):
                bout_ref[0, pl.ds(c * CLIP + rows.start, rows.size), :] = acc.astype(BF)

            feed_forward(c, put)
            back_ff(c, lambda rows: s.xs[c, rows].astype(F32))
            frames_backward(c)

            def put_back(rows, acc):
                s.eb[c, rows] = acc.astype(BF)

            back_in(c, put_back)
            grad_code = tt(proj_ref[0], s.eb[c])
            s.cxs[c] = pad16(grad_code)
            code_copy(c).start()
            book_proj_terms(
                c, s.cxs[c][0:8].astype(F32), s.eb[c], s.cvec[c][0:8].astype(F32)
            )
            return carry

        lax.fori_loop(0, 2, both, 0)

    def last(c, carry):
        @pl.when(is_e)
        def _():
            code_copy(c).wait_recv()
            for f in range(2):
                cols = slice(GRID * f, GRID * f + GRID)
                s.cvec[c, :, cols] = nt(s.cxr[c, :, cols], s.perm[c]).astype(BF)
            g = tt(s.cvec[c][0:8], proj_ref[0])
            s.gg[...] = g
            s.xs[c] = g.astype(BF)
            book_proj_terms(
                c, s.cxr[c][0:8].astype(F32), s.eb[c], s.cvec[c][0:8].astype(F32)
            )

        grad_down(c)

        @pl.when(c == 1)
        def _():
            reduce_step("a", 0)

        @pl.when(is_e)
        def _():
            back_ff(c, lambda rows: s.gg[rows])

        grad_up(c)

        @pl.when(c == 1)
        def _():
            reduce_step("b", 0)
            reduce_step("a", 1)

        @pl.when(is_e)
        def _():
            window_backward(c)

            def put_back(rows, acc):
                s.gob[rows] = acc.astype(BF)

            back_in(c, put_back)
            for f in range(2):
                back = tn(s.perm[c], s.gob[GRID * f : GRID * f + GRID])
                bout_ref[0, pl.ds(c * CLIP + GRID * f, GRID), :] = back.astype(BF)

        grad_attn(c)
        return carry

    lax.fori_loop(0, 2, last, 0)

    reduce_step("c", 0)
    sums = jnp.concatenate(
        [
            jnp.sum(s.gacc[0], axis=0, keepdims=True),
            jnp.sum(s.gacc[1], axis=0, keepdims=True),
            jnp.zeros((6, D), F32),
        ],
        axis=0,
    )
    wide_sums = jnp.concatenate([jnp.zeros((72, D), F32), sums, jnp.zeros((48, D), F32)], axis=0)
    s.s_acc[...] += jnp.transpose(wide_sums).reshape(4, 8, 2, 8, 128)
    order = [
        "s0", "b1", "c1", "s1", "a2", "b2", "s2", "c2", "a3", "s3", "b3", "c3", "a4", "b4", "s4", "c4",
        "a5", "b5", "c5",
    ]
    for item in order:
        reduce_step(item[0], int(item[1]))

    half_rows = s.win[pl.ds(16 * (dp // 2), 16), :].astype(F32)
    piece = jnp.where(core == 0, half_rows[0:8], half_rows[8:16])
    ain_ref[0] = AVG_DECAY * avgin_ref[0] + (1.0 - AVG_DECAY) * (piece - LEARN_RATE * gin_ref[0])

    for c in range(2):
        code_copy(c).wait_send()
    for k in ("a", "b", "c", "s"):
        for step in range(5):
            for cp in copies(k, step):
                cp.wait_send()


def body(
    boundary, in_weights, down_weight, gains, proj, codebook, codes, grids, orders, avg_in, avg_down
):
    vmem = pl.BlockSpec(memory_space=pltpu.VMEM)
    smem = pl.BlockSpec(memory_space=pltpu.SMEM)
    hbm = pl.BlockSpec(memory_space=pl.ANY)
    outs = (
        jax.ShapeDtypeStruct(boundary.shape, BF),
        jax.ShapeDtypeStruct(avg_in.shape, F32),
        jax.ShapeDtypeStruct(avg_down.shape, F32),
        jax.ShapeDtypeStruct((1, 2, 8), F32),
        jax.ShapeDtypeStruct((1, 8, 8), F32),
        jax.ShapeDtypeStruct(codebook.shape, F32),
        jax.ShapeDtypeStruct(avg_in.shape, F32),
        jax.ShapeDtypeStruct(avg_down.shape, F32),
    )
    scratch = [pltpu.VMEM(shape, dtype) for shape, dtype in SHAPES.values()]
    scratch += [pltpu.SemaphoreType.DMA((N_SEM,)), pltpu.SemaphoreType.DMA((N_SEM,)), pltpu.SemaphoreType.DMA((4,))]
    return pl.pallas_call(
        mega,
        out_shape=outs,
        in_specs=[hbm, hbm, hbm, vmem, vmem, vmem, vmem, smem, smem, vmem, vmem],
        out_specs=[vmem] * 8,
        scratch_shapes=scratch,
        compiler_params=pltpu.CompilerParams(
            collective_id=0, has_side_effects=True, vmem_limit_bytes=63 << 20
        ),
        name="both_sections",
    )(
        boundary, in_weights, down_weight, gains, proj, codebook, codes.reshape(8, 128), grids, orders,
        avg_in, avg_down,
    )


def solution(mesh):
    placed = (
        P("section", "dp", None),
        P("section", None, None),
        P("section", None, None),
        P("section", None, None),
        P("section", None, None),
        P(None, ("section", "dp")),
        P("dp"),
        P("dp"),
        P("dp", None),
        P("section", "dp", None),
        P("section", "dp", None),
    )
    return jax.shard_map(
        body,
        mesh=mesh,
        in_specs=placed,
        out_specs=(
            P("section", "dp", None),
            P("section", "dp", None),
            P("section", "dp", None),
            P("section", None, "dp"),
            P("section", "dp", None),
            P(None, ("section", "dp")),
            P("section", "dp", None),
            P("section", "dp", None),
        ),
        check_vma=False,
    )
```

```python
import functools

import jax
import jax.numpy as jnp
from jax import lax
from jax.experimental import pallas as pl
from jax.experimental.pallas import tpu as pltpu
from jax.sharding import PartitionSpec as P

BF = jnp.bfloat16
F32 = jnp.float32
I32 = jnp.int32
MESH = pl.DeviceIdType.MESH

D = 512
FF = 2048
CLIP = 512
GRID = 256
WINDOW = 64
HALF = 4096
NORM_EPS = 1e-05
AVG_DECAY = 0.9
LEARN_RATE = 0.0005
SCALE = 0.125
RC = 512
WB = 4

CHUNKS = {"a": (128, 256), "b": (32, 1280), "c": (32, 768)}


def nn(left, right):
    return lax.dot_general(left, right, (((1,), (0,)), ((), ())), preferred_element_type=F32)


def nt(left, right):
    return lax.dot_general(left, right, (((1,), (1,)), ((), ())), preferred_element_type=F32)


def tn(left, right):
    return lax.dot_general(left, right, (((0,), (0,)), ((), ())), preferred_element_type=F32)


def tt(left, right):
    return lax.dot_general(left, right, (((0,), (1,)), ((), ())), preferred_element_type=F32)


def iota(shape, axis):
    return lax.broadcasted_iota(I32, shape, axis)


def normed(h):
    mean = jnp.mean(h, axis=-1, keepdims=True)
    c = h - mean
    var = jnp.mean(c * c, axis=-1, keepdims=True)
    r = lax.rsqrt(var + NORM_EPS)
    return c * r, r


def normed_back(grad, xhat, r, gain):
    t = grad * gain
    m1 = jnp.mean(t, axis=-1, keepdims=True)
    m2 = jnp.mean(t * xhat, axis=-1, keepdims=True)
    return r * (t - m1 - xhat * m2)


def gelu_pair(u):
    c0 = 0.7978845608028654
    c1 = 0.7978845608028654 * 0.044715
    m = c1 * (u * u)
    half = 0.5 + 0.5 * jnp.tanh(u * (c0 + m))
    value = u * half
    slope = half + (value - value * half) * (2.0 * c0 + 6.0 * m)
    return value, slope


def ten_shapes():
    shapes = {
        "xs": ((2, CLIP, D), BF),
        "win": ((D, 4 * D + FF), BF),
        "wdn": ((FF, D), BF),
        "perm": ((2, GRID, GRID), BF),
        "bd1": ((256, 256), BF),
        "bds": ((256, 256), BF),
        "bdf": ((256, 256), F32),
        "tbl": ((64, 8, 128), F32),
        "cds": ((2, 8, CLIP), I32),
        "cxs": ((2, 16, CLIP), BF),
        "cxr": ((2, 16, CLIP), BF),
        "ent": ((2, 8, CLIP), F32),
        "cvec": ((2, 16, CLIP), BF),
        "hb": ((CLIP, D), F32),
        "bo": ((2 * CLIP, D), BF),
        "gob": ((CLIP, D), BF),
        "xh1": ((2, CLIP, D), F32),
        "xh2": ((2, CLIP, D), F32),
        "r1": ((2, CLIP, 1), F32),
        "r2": ((2, CLIP, 1), F32),
        "a1": ((2, CLIP, D), BF),
        "a2": ((2, CLIP, D), BF),
        "qkv": ((2, CLIP, 3 * D), BF),
        "prob": ((2, CLIP, D), F32),
        "att": ((2, CLIP, D), BF),
        "act": ((2, CLIP, FF), BF),
        "gel": ((2, CLIP, FF), BF),
        "gy": ((2, CLIP, D), BF),
        "eb": ((2, CLIP, D), BF),
        "acc_dn": ((FF, D), F32),
        "acc_up": ((D, FF), F32),
        "acc_qkv": ((D, 3 * D), F32),
        "acc_out": ((D, D), F32),
        "s_acc": ((4, 8, 2, 8, 128), F32),
        "gacc": ((2, 8, D), F32),
        "s0": ((4, 8, 8, 128), F32),
        "s1": ((3, 8, 8, 128), F32),
        "s2": ((3, 2, 8, 128), F32),
        "s3": ((8, 128), F32),
    }
    for k, (rows, w) in CHUNKS.items():
        h = w // 2
        half = rows // 2
        shapes["sb0" + k] = ((4, 4, 2, half, w), BF)
        shapes["r0" + k] = ((4, 4, 2, half, w), BF)
        for ax in "zx":
            for slot in "012":
                shapes["q" + slot + ax + k] = ((2, 4, half, h), BF)
            shapes["r2" + ax + k] = ((3, 2, half, h), BF)
        shapes["t3" + k] = ((2, half, w), F32)
        shapes["sb3" + k] = ((half, w), BF)
        shapes["r3" + k] = ((half, w), BF)
        shapes["t4" + k] = ((half, w), F32)
        shapes["r4" + k] = ((half // 2, w), F32)
    return shapes


SHAPES = ten_shapes()
N_SEM = 120


class Refs:
    pass


def mega(
    x_hbm, win_hbm, wdn_hbm, gains_ref, proj_ref, book_ref, codes_ref, grids_ref, orders_ref,
    avgin_ref, avgdn_ref,
    bout_hbm, gin_ref, gdn_ref, small_ref, ain_ref, adn_ref,
    *scratch,
):
    s = Refs()
    for name, ref in zip(SHAPES, scratch):
        setattr(s, name, ref)
    send_sems, recv_sems, load_sems = scratch[len(SHAPES):]

    sec = lax.axis_index("section")
    dp = lax.axis_index("dp")
    core = dp % 2
    yh = (dp // 2) % 2
    x = (dp // 4) % 4
    z = dp // 16
    is_e = sec == 0
    is_d = sec == 1

    def place(zz, xx, yy, cc):
        return (sec, ((zz * 4 + xx) * 2 + yy) * 2 + cc)

    core_dev = place(z, x, yh, 1 - core)
    y_dev = place(z, x, 1 - yh, core)
    def flips(v):
        return {1: v + 1 - 2 * (v % 2), 2: (v + 2) % 4, 3: 3 - v}

    z_flip, x_flip = flips(z), flips(x)
    z_dev = [place((z + d) % 4, x, yh, core) for d in (1, 2, 3)]
    x_dev = [place(z, (x + d) % 4, yh, core) for d in (1, 2, 3)]
    sec_dev = (1 - sec, dp)

    counter = [0]
    slots = {}

    def rcopy(key, src, dst, dev):
        if key not in slots:
            slots[key] = counter[0]
            counter[0] += 1
        i = slots[key]
        return pltpu.make_async_remote_copy(
            src_ref=src, dst_ref=dst, send_sem=send_sems.at[i], recv_sem=recv_sems.at[i],
            device_id=dev, device_id_type=MESH,
        )

    loads = [
        pltpu.make_async_copy(x_hbm.at[0, pl.ds(0, CLIP)], s.xs.at[0], load_sems.at[0]),
        pltpu.make_async_copy(win_hbm.at[0, :, pl.ds(0, 3 * D)], s.win.at[:, pl.ds(0, 3 * D)], load_sems.at[1]),
        pltpu.make_async_copy(
            win_hbm.at[0, :, pl.ds(3 * D, D + FF)], s.win.at[:, pl.ds(3 * D, D + FF)], load_sems.at[2]
        ),
        pltpu.make_async_copy(wdn_hbm.at[0], s.wdn, load_sems.at[3]),
        pltpu.make_async_copy(x_hbm.at[0, pl.ds(CLIP, CLIP)], s.xs.at[1], load_sems.at[4]),
    ]
    for load in loads:
        load.start()

    def bout_copy(c):
        rows = pl.ds(c * CLIP, CLIP)
        return pltpu.make_async_copy(s.bo.at[rows], bout_hbm.at[0, rows], load_sems.at[5 + c])

    barrier = pltpu.get_barrier_semaphore()
    peers = [core_dev, y_dev, sec_dev] + z_dev + x_dev
    for dev in peers:
        pl.semaphore_signal(barrier, inc=1, device_id=dev, device_id_type=MESH)

    rows_i = iota((256, 256), 0)
    cols_i = iota((256, 256), 1)
    same = ((rows_i >> 6) == (cols_i >> 6)).astype(F32)
    s.bdf[...] = same * SCALE
    s.bd1[...] = same.astype(BF)
    s.bds[...] = (same * SCALE).astype(BF)
    for c in range(2):
        code_row = jnp.concatenate([codes_ref[4 * c + k : 4 * c + k + 1, :] for k in range(4)], axis=1)
        s.cds[c] = jnp.broadcast_to(code_row - sec * HALF, (8, CLIP))

    proj_t = proj_ref[...]
    gain_one = gains_ref[0, 0:1, :].astype(F32)
    gain_two = gains_ref[0, 1:2, :].astype(F32)
    book = book_ref[...].astype(F32)
    s.tbl[dp] = jnp.concatenate([book, jnp.zeros((8, 64), F32)], axis=1)
    s.gacc[...] = jnp.zeros((2, 8, D), F32)
    s.s_acc[...] = jnp.zeros((4, 8, 2, 8, 128), F32)

    pl.semaphore_wait(barrier, len(peers))

    def ag_copies(step):
        if step == 0:
            part = s.tbl.at[dp]
            return [rcopy("ag0", part, part, core_dev)]
        if step == 1:
            part = s.tbl.at[pl.ds((dp // 2) * 2, 2)]
            return [rcopy("ag1", part, part, y_dev)]
        if step == 2:
            part = s.tbl.at[pl.ds((dp // 4) * 4, 4)]
            return [rcopy("ag2%d" % i, part, part, x_dev[i]) for i in range(3)]
        part = s.tbl.at[pl.ds((dp // 16) * 16, 16)]
        return [rcopy("ag3%d" % i, part, part, z_dev[i]) for i in range(3)]

    def ag_arrivals(step):
        if step == 0:
            part = s.tbl.at[dp + 1 - 2 * core]
            return [rcopy("ag0", part, part, core_dev)]
        if step == 1:
            part = s.tbl.at[pl.ds((dp // 4) * 4 + (1 - yh) * 2, 2)]
            return [rcopy("ag1", part, part, y_dev)]
        if step == 2:
            parts = [s.tbl.at[pl.ds(z * 16 + ((x + 3 - i) % 4) * 4, 4)] for i in range(3)]
            return [rcopy("ag2%d" % i, parts[i], parts[i], x_dev[i]) for i in range(3)]
        parts = [s.tbl.at[pl.ds(((z + 3 - i) % 4) * 16, 16)] for i in range(3)]
        return [rcopy("ag3%d" % i, parts[i], parts[i], z_dev[i]) for i in range(3)]

    def ag_start(step):
        for cp in ag_copies(step):
            cp.start()

    def ag_wait(step):
        for cp in ag_arrivals(step):
            cp.wait_recv()
        for cp in ag_copies(step):
            cp.wait_send()

    def onehots(c):
        code_row = s.cds[c][0:1, :]
        hi = code_row >> 6
        lo = code_row & 63
        lo_one = (iota((128, CLIP), 0) == lo).astype(F32).astype(BF)
        hi_mask = (iota((CLIP, CLIP), 0) >> 3) == hi
        return lo_one, hi_mask

    def entries(c):
        lo_one, hi_mask = onehots(c)
        table = s.tbl[...].reshape(CLIP, 128).astype(BF)
        picked = jnp.where(hi_mask, nn(table, lo_one), 0.0)
        s.ent[c] = jnp.sum(picked.reshape(64, 8, CLIP), axis=0)

    def pad16(v):
        return jnp.concatenate([v, jnp.zeros((8, v.shape[1]), F32)], axis=0).astype(BF)

    def book_proj_terms(c, code_grad, wide_rows, narrow):
        lo_one, hi_mask = onehots(c)
        spread = jnp.broadcast_to(code_grad[None], (64, 8, CLIP)).reshape(CLIP, CLIP)
        left = jnp.where(hi_mask, spread, 0.0).astype(BF)
        total = nt(left, lo_one)
        narrow_wide = jnp.concatenate(
            [jnp.zeros((64, CLIP), F32), narrow, jnp.zeros((56, CLIP), F32)], axis=0
        ).astype(BF)
        total = total + tt(wide_rows, narrow_wide)
        s.s_acc[...] += total.reshape(4, 8, 2, 8, 128)

    def norm_qkv(c, rows, h):
        s.hb[rows] = h
        xh, r = normed(h)
        s.xh1[c, rows] = xh
        s.r1[c, rows] = r
        a = (xh * gain_one).astype(BF)
        s.a1[c, rows] = a
        for j in range(3):
            s.qkv[c, rows, 512 * j : 512 * j + 512] = nn(a, s.win[:, 512 * j : 512 * j + 512]).astype(BF)

    def feed_forward(c, put):
        def step(i, carry):
            rows = pl.ds(i * RC, RC)
            m = s.hb[rows] + nn(s.att[c, rows], s.win[:, 1536:2048])
            xh, r = normed(m)
            s.xh2[c, rows] = xh
            s.r2[c, rows] = r
            a = (xh * gain_two).astype(BF)
            s.a2[c, rows] = a
            acc = m
            nxt = nn(a, s.win[:, 2048:2304])
            for j in range(8):
                cols = slice(256 * j, 256 * j + 256)
                u = nxt
                if j < 7:
                    nxt = nn(a, s.win[:, 2304 + 256 * j : 2560 + 256 * j])
                value, slope = gelu_pair(u.astype(BF))
                s.act[c, rows, cols] = value
                s.gel[c, rows, cols] = slope
                acc = acc + nn(value, s.wdn[cols, :])
            put(rows, acc)
            return carry

        lax.fori_loop(0, CLIP // RC, step, 0)

    def units(c, w, count):
        out = []
        for n in range(count):
            rows = pl.ds((w * count + n) * WINDOW, WINDOW)
            for quad in range(2):
                out.append((rows, 256 * quad))
        return out

    def widened(v, mask):
        return jnp.concatenate([v] * 4, axis=0) * mask

    def heads_of(wide):
        return (wide[0:64] + wide[64:128]) + (wide[128:192] + wide[192:256])

    def window_forward(c, w):
        if True:
            us = units(c, w, WB)
            bds = s.bds[...]
            bdf = s.bdf[...]
            q = [s.qkv[c, r, o : o + 256] for r, o in us]
            k = [s.qkv[c, r, 512 + o : 768 + o] for r, o in us]
            v = [s.qkv[c, r, 1024 + o : 1280 + o] for r, o in us]
            scores = [nt(kk, widened(qq, bds)) for kk, qq in zip(k, q)]
            e = [jnp.exp(x - jnp.max(x, axis=0, keepdims=True)) for x in scores]
            p = [x * (1.0 / jnp.sum(x, axis=0, keepdims=True)) for x in e]
            wide = [tn(x.astype(BF), vv) for x, vv in zip(p, v)]
            att = [(heads_of(x * bdf) * (1.0 / SCALE)).astype(BF) for x in wide]
            for (r, o), pp, aa in zip(us, p, att):
                s.prob[c, r, o : o + 256] = pp
                s.att[c, r, o : o + 256] = aa

    def window_backward(c, w):
        if True:
            us = units(c, w, WB)
            bds = s.bds[...]
            bd1 = s.bd1[...]
            bdf = s.bdf[...]
            q = [s.qkv[c, r, o : o + 256] for r, o in us]
            k = [s.qkv[c, r, 512 + o : 768 + o] for r, o in us]
            v = [s.qkv[c, r, 1024 + o : 1280 + o] for r, o in us]
            go = [widened(s.gob[r, o : o + 256], bd1) for r, o in us]
            p = [s.prob[c, r, o : o + 256] for r, o in us]
            gp = [nt(vv, gg) for vv, gg in zip(v, go)]
            gv = [nn(pp.astype(BF), gg).astype(BF) for pp, gg in zip(p, go)]
            gs = [
                (pp * (x - jnp.sum(x * pp, axis=0, keepdims=True))).astype(BF)
                for pp, x in zip(p, gp)
            ]
            gk = [nn(x, widened(qq, bds)).astype(BF) for x, qq in zip(gs, q)]
            gq = [heads_of(tn(x, kk) * bdf).astype(BF) for x, kk in zip(gs, k)]
            for (r, o), a, b, d in zip(us, gq, gk, gv):
                s.qkv[c, r, o : o + 256] = a
                s.qkv[c, r, 512 + o : 768 + o] = b
                s.qkv[c, r, 1024 + o : 1280 + o] = d

    def head_sums(v):
        hi = v.astype(BF)
        lo = (v - hi.astype(F32)).astype(BF)
        return nn(hi, s.bd1[...]) + nn(lo, s.bd1[...])

    CR = 128

    def frames_forward(c):
        late0 = orders_ref[c, 0] > orders_ref[c, 1]
        sign = jnp.where(late0, 1.0, -1.0).astype(F32)

        def step(i, carry):
            r0 = pl.ds(i * CR, CR)
            r1 = pl.ds(GRID + i * CR, CR)
            for quad in range(2):
                qc = slice(256 * quad, 256 * quad + 256)
                kc = slice(512 + 256 * quad, 768 + 256 * quad)
                vc = slice(1024 + 256 * quad, 1280 + 256 * quad)
                q_late = jnp.where(late0, s.qkv[c, r0, qc].astype(F32), s.qkv[c, r1, qc].astype(F32))
                k_diff = sign * (s.qkv[c, r1, kc].astype(F32) - s.qkv[c, r0, kc].astype(F32))
                v0 = s.qkv[c, r0, vc].astype(F32)
                v1 = s.qkv[c, r1, vc].astype(F32)
                d = head_sums(q_late * k_diff) * SCALE
                e = jnp.exp(-jnp.abs(d))
                big = 1.0 / (1.0 + e)
                small = e * big
                p_other = jnp.where(d > 0.0, big, small)
                p_self = jnp.where(d > 0.0, small, big)
                s.prob[c, r0, qc] = p_other
                s.prob[c, r1, qc] = p_self
                po = p_other.astype(BF).astype(F32)
                ps = p_self.astype(BF).astype(F32)
                v_late = jnp.where(late0, v0, v1)
                v_early = jnp.where(late0, v1, v0)
                mix = ps * v_late + po * v_early
                s.att[c, r0, qc] = jnp.where(late0, mix, v0).astype(BF)
                s.att[c, r1, qc] = jnp.where(late0, v1, mix).astype(BF)
            return carry

        lax.fori_loop(0, GRID // CR, step, 0)

    def frames_backward(c):
        late0 = orders_ref[c, 0] > orders_ref[c, 1]
        sign = jnp.where(late0, 1.0, -1.0).astype(F32)

        def step(i, carry):
            r0 = pl.ds(i * CR, CR)
            r1 = pl.ds(GRID + i * CR, CR)
            for quad in range(2):
                qc = slice(256 * quad, 256 * quad + 256)
                kc = slice(512 + 256 * quad, 768 + 256 * quad)
                vc = slice(1024 + 256 * quad, 1280 + 256 * quad)
                q_late = jnp.where(late0, s.qkv[c, r0, qc].astype(F32), s.qkv[c, r1, qc].astype(F32))
                k_diff = sign * (s.qkv[c, r1, kc].astype(F32) - s.qkv[c, r0, kc].astype(F32))
                v_diff = sign * (s.qkv[c, r1, vc].astype(F32) - s.qkv[c, r0, vc].astype(F32))
                go0 = s.gob[r0, qc].astype(F32)
                go1 = s.gob[r1, qc].astype(F32)
                go_late = jnp.where(late0, go0, go1)
                go_early = jnp.where(late0, go1, go0)
                p_other = s.prob[c, r0, qc]
                p_self = s.prob[c, r1, qc]
                gs = p_other * p_self * head_sums(go_late * v_diff)
                gs = gs.astype(BF).astype(F32) * SCALE
                gq = gs * k_diff
                gk = gs * q_late
                gv_late = p_self.astype(BF).astype(F32) * go_late
                gv_early = go_early + p_other.astype(BF).astype(F32) * go_late
                s.qkv[c, r0, qc] = jnp.where(late0, gq, 0.0).astype(BF)
                s.qkv[c, r1, qc] = jnp.where(late0, 0.0, gq).astype(BF)
                s.qkv[c, r0, kc] = (-sign * gk).astype(BF)
                s.qkv[c, r1, kc] = (sign * gk).astype(BF)
                s.qkv[c, r0, vc] = jnp.where(late0, gv_late, gv_early).astype(BF)
                s.qkv[c, r1, vc] = jnp.where(late0, gv_early, gv_late).astype(BF)
            return carry

        lax.fori_loop(0, GRID // CR, step, 0)

    def gain_terms(which, grad, xhat):
        part = jnp.sum((grad * xhat).reshape(-1, 8, D), axis=0)
        s.gacc[which] += part

    def back_ff(c, grad_of):
        def step(i, carry):
            rows = pl.ds(i * RC, RC)
            gz = s.xs[c, rows]
            acc = None
            for j in range(4):
                cols = slice(512 * j, 512 * j + 512)
                gu = (nt(gz, s.wdn[cols, :]) * s.gel[c, rows, cols].astype(F32)).astype(BF)
                s.gel[c, rows, cols] = gu
                term = nt(gu, s.win[:, 2048 + 512 * j : 2560 + 512 * j])
                acc = term if acc is None else acc + term
            xh = s.xh2[c, rows]
            gain_terms(1, acc, xh)
            gm = grad_of(rows) + normed_back(acc, xh, s.r2[c, rows], gain_two)
            s.hb[rows] = gm
            gy = gm.astype(BF)
            s.gy[c, rows] = gy
            s.gob[rows] = nt(gy, s.win[:, 1536:2048]).astype(BF)
            return carry

        lax.fori_loop(0, CLIP // RC, step, 0)

    def back_in(c, put):
        def step(i, carry):
            rows = pl.ds(i * RC, RC)
            acc = None
            for j in range(3):
                cols = slice(512 * j, 512 * j + 512)
                term = nt(s.qkv[c, rows, cols], s.win[:, cols])
                acc = term if acc is None else acc + term
            xh = s.xh1[c, rows]
            gain_terms(0, acc, xh)
            put(rows, s.hb[rows] + normed_back(acc, xh, s.r1[c, rows], gain_one))
            return carry

        lax.fori_loop(0, CLIP // RC, step, 0)

    def add_into(ref, rows, cols, c, value):
        ref[rows, cols] = jnp.where(c == 0, value, ref[rows, cols] + value)

    def grad_down(c):
        for j in range(4):
            cols = slice(512 * j, 512 * j + 512)
            add_into(s.acc_dn, cols, slice(None), c, tn(s.act[c, :, cols], s.xs[c]))

    def grad_up(c):
        for j in range(4):
            cols = slice(512 * j, 512 * j + 512)
            add_into(s.acc_up, slice(None), cols, c, tn(s.a2[c], s.gel[c, :, cols]))

        add_into(s.acc_out, slice(None), slice(None), c, tn(s.att[c], s.gy[c]))

    def grad_attn(c):
        for j in range(3):
            cols = slice(512 * j, 512 * j + 512)
            add_into(s.acc_qkv, slice(None), cols, c, tn(s.a1[c], s.qkv[c, :, cols]))

    def load_half(k, i, half):
        if k == "a":
            v = s.acc_dn[pl.ds(i * 128, 128), pl.ds(pl.multiple_of(half * 256, 128), 256)]
            return v.reshape(2, 64, 256)
        rows = pl.ds(i * 32, 32)
        if k == "c":
            v = s.acc_qkv[rows, pl.ds(pl.multiple_of(half * 768, 128), 768)]
            return v.reshape(2, 16, 768)
        v = jnp.concatenate(
            [
                s.acc_up[rows, pl.ds(pl.multiple_of(half * 1024, 128), 1024)],
                s.acc_out[rows, pl.ds(pl.multiple_of(half * 256, 128), 256)],
            ],
            axis=1,
        )
        return v.reshape(2, 16, 1280)

    def buf(name, k):
        return getattr(s, name + k)

    def copies(k, step):
        if k == "s":
            if step == 0:
                return [rcopy("s0", s.s_acc.at[:, :, 1 - core], s.s0, core_dev)]
            if step == 1:
                return [rcopy("s1%d" % i, s.s0.at[(z + 1 + i) % 4], s.s1.at[i], z_dev[i]) for i in range(3)]
            if step == 2:
                return [
                    rcopy("s2%d" % i, s.s0.at[z, pl.ds(2 * ((x + 1 + i) % 4), 2)], s.s2.at[i], x_dev[i])
                    for i in range(3)
                ]
            if step == 3:
                return [rcopy("s3", s.s0.at[z, 2 * x + 1 - yh], s.s3, y_dev)]
            return []
        rows, w = CHUNKS[k]
        h = w // 2
        r0 = buf("r0", k)
        if step == 0:
            return [rcopy(k + "0", buf("sb0", k), r0, core_dev)]
        lo, hi = pl.ds(0, h), pl.ds(h, h)
        out = []
        if step in (1, 2, 3):
            for y in range(2):
                first, second = ((1, 3), (3, 1))[y]
                hop = second if step == 3 else first
                block = {1: 2, 2: first, 3: second}[step]
                slot = {1: "q1", 2: "q0", 3: "q2"}[step]
                out.append(
                    rcopy(
                        "%s%dz%d" % (k, step, y), r0.at[z_flip[block], :, y, :, lo],
                        buf(slot + "z", k).at[y], place(z_flip[hop], x, yh, core),
                    )
                )
                out.append(
                    rcopy(
                        "%s%dx%d" % (k, step, y), r0.at[:, x_flip[block], y, :, hi],
                        buf(slot + "x", k).at[y], place(z, x_flip[hop], yh, core),
                    )
                )
            return out
        if step == 4:
            for i in range(3):
                out.append(
                    rcopy(
                        "%s4x%d" % (k, i), r0.at[z, (x + 1 + i) % 4, :, :, lo], buf("r2x", k).at[i], x_dev[i]
                    )
                )
                out.append(
                    rcopy(
                        "%s4z%d" % (k, i), r0.at[(z + 1 + i) % 4, x, :, :, hi], buf("r2z", k).at[i], z_dev[i]
                    )
                )
            return out
        if step == 5:
            return [rcopy(k + "5", buf("sb3", k), buf("r3", k), y_dev)]
        quarter = rows // 4
        return [rcopy(k + "6", buf("t4", k).at[pl.ds((1 - core) * quarter, quarter)], buf("r4", k), core_dev)]

    def arrived(k, step):
        for cp in copies(k, step):
            cp.wait_recv()

    def send(k, step):
        for cp in copies(k, step):
            cp.start()

    def reduce_step(k, step):
        if k == "s":
            if step > 0:
                arrived(k, step - 1)
            if step == 1:
                s.s0[...] += s.s_acc[:, :, core]
            elif step == 2:
                s.s0[z] += (s.s1[0] + s.s1[1]) + s.s1[2]
            elif step == 3:
                here = pl.ds(2 * x, 2)
                s.s0[z, here] += (s.s2[0] + s.s2[1]) + s.s2[2]
            elif step == 4:
                small_ref[...] = s.s0[z, 2 * x + yh] + s.s3[...]
                return
            send(k, step)
            return
        rows, w = CHUNKS[k]
        h = w // 2
        half = rows // 2
        r0 = buf("r0", k)
        lo, hi = pl.ds(0, h), pl.ds(h, h)
        if step == 0:
            sb0 = buf("sb0", k)

            def body(i, carry):
                sb0[i // 4, i % 4] = load_half(k, i, 1 - core).astype(BF)
                return carry

            lax.fori_loop(0, 16, body, 0)
            send(k, 0)
        elif step == 1:
            arrived(k, 0)

            def body(i, carry):
                r0[i // 4, i % 4] = (load_half(k, i, core) + r0[i // 4, i % 4].astype(F32)).astype(BF)
                return carry

            lax.fori_loop(0, 16, body, 0)
            send(k, 1)
            send(k, 2)
        elif step == 2:
            arrived(k, 1)
            for y in range(2):
                second = (3, 1)[y]
                zb, xb = z_flip[second], x_flip[second]
                r0[zb, :, y, :, lo] = (
                    r0[zb, :, y, :, lo].astype(F32) + buf("q1z", k)[y].astype(F32)
                ).astype(BF)
                r0[:, xb, y, :, hi] = (
                    r0[:, xb, y, :, hi].astype(F32) + buf("q1x", k)[y].astype(F32)
                ).astype(BF)
            send(k, 3)
        elif step == 3:
            arrived(k, 2)
            arrived(k, 3)
            for y in range(2):
                r0[z, :, y, :, lo] = (
                    r0[z, :, y, :, lo].astype(F32) + buf("q0z", k)[y].astype(F32)
                    + buf("q2z", k)[y].astype(F32)
                ).astype(BF)
                r0[:, x, y, :, hi] = (
                    r0[:, x, y, :, hi].astype(F32) + buf("q0x", k)[y].astype(F32)
                    + buf("q2x", k)[y].astype(F32)
                ).astype(BF)
            send(k, 4)
        elif step == 4:
            arrived(k, 4)
            ra = buf("r2x", k)
            rb = buf("r2z", k)
            t3 = buf("t3", k)
            t3[:, :, lo] = (r0[z, x, :, :, lo].astype(F32) + ra[0].astype(F32)) + (
                ra[1].astype(F32) + ra[2].astype(F32)
            )
            t3[:, :, hi] = (r0[z, x, :, :, hi].astype(F32) + rb[0].astype(F32)) + (
                rb[1].astype(F32) + rb[2].astype(F32)
            )
            buf("sb3", k)[...] = t3[1 - yh].astype(BF)
            send(k, 5)
        elif step == 5:
            arrived(k, 5)
            buf("t4", k)[...] = buf("t3", k)[yh] + buf("r3", k)[...].astype(F32)
            send(k, 6)
        else:
            arrived(k, 6)
            quarter = rows // 4
            mine = buf("t4", k)[pl.ds(core * quarter, quarter), :]
            other = buf("r4", k)[...]

            def put(ref, start, width, part):
                for c, v in ((core, mine), (1 - core, other)):
                    ref[0, :, pl.ds(pl.multiple_of(start + c * width, 128), width)] = v[:, part : part + width]

            if k == "a":
                put(gdn_ref, 0, 256, 0)
                piece = s.wdn[pl.ds(dp * 32, 32), :].astype(F32)
                adn_ref[0] = AVG_DECAY * avgdn_ref[0] + (1.0 - AVG_DECAY) * (
                    piece - LEARN_RATE * gdn_ref[0]
                )
            elif k == "b":
                put(gin_ref, 2048, 1024, 0)
                put(gin_ref, 1536, 256, 1024)
            else:
                put(gin_ref, 0, 768, 0)

    def code_copy(c):
        return pltpu.make_async_remote_copy(
            src_ref=s.cxs.at[c], dst_ref=s.cxr.at[c], send_sem=send_sems.at[N_SEM - 2 + c],
            recv_sem=recv_sems.at[N_SEM - 2 + c], device_id=sec_dev, device_id_type=MESH,
        )

    ag_start(0)

    @pl.when(is_e)
    def _():
        for c in range(2):
            grid_now = grids_ref[c]
            width = jnp.where(grid_now == 0, 16, jnp.where(grid_now == 1, 32, 8)).astype(I32)
            log_across = jnp.where(grid_now == 0, 1, jnp.where(grid_now == 1, 2, 0)).astype(I32)
            across_mask = jnp.where(grid_now == 0, 1, jnp.where(grid_now == 1, 3, 0)).astype(I32)
            window_no = rows_i >> 6
            inner = rows_i & 63
            source = (
                ((window_no >> log_across) * 8 + (inner >> 3)) * width
                + (window_no & across_mask) * 8
                + (inner & 7)
            )
            s.perm[c] = (source == cols_i).astype(F32).astype(BF)
        loads[0].wait()
        loads[1].wait()

        def forward(c, carry):
            @pl.when(c == 1)
            def _():
                loads[4].wait()

            for f in range(2):
                rows = slice(GRID * f, GRID * f + GRID)
                norm_qkv(c, rows, nn(s.perm[c], s.xs[c, rows]))

            @pl.when(c == 0)
            def _():
                ag_wait(0)
                ag_start(1)

            window_forward(c, 0)

            @pl.when(c == 0)
            def _():
                ag_wait(1)
                ag_start(2)

            window_forward(c, 1)

            @pl.when(c == 0)
            def _():
                ag_wait(2)
                ag_start(3)
                loads[2].wait()
                loads[3].wait()

            def put(rows, acc):
                s.eb[c, rows] = acc.astype(BF)

            feed_forward(c, put)

            @pl.when(c == 0)
            def _():
                ag_wait(3)

            entries(c)
            entry = s.ent[c]
            vec = nt(proj_t, s.eb[c])
            for f in range(2):
                cols = slice(GRID * f, GRID * f + GRID)
                entry_enc = nt(pad16(entry[:, cols]), s.perm[c])[0:8]
                sent = pad16(vec[:, cols] + entry_enc)
                s.cxs[c, :, cols] = nn(sent, s.perm[c]).astype(BF)
            code_copy(c).start()
            return carry

        lax.fori_loop(0, 2, forward, 0)

    @pl.when(is_d)
    def _():
        for step in range(4):
            ag_wait(step)
            if step < 3:
                ag_start(step + 1)
        for c in range(2):
            entries(c)
        for load in loads:
            load.wait()

        def both(c, carry):
            code_copy(c).wait_recv()
            quant = s.cxr[c][0:8].astype(F32) + s.ent[c]
            s.cvec[c] = pad16(quant)
            for f in range(2):
                rows = slice(GRID * f, GRID * f + GRID)
                h = tn(s.cvec[c][0:8, rows], proj_t)
                norm_qkv(c, rows, h)
            frames_forward(c)

            def put(rows, acc):
                s.bo[pl.ds(c * CLIP + rows.start, rows.size), :] = acc.astype(BF)

            feed_forward(c, put)
            bout_copy(c).start()
            back_ff(c, lambda rows: s.xs[c, rows].astype(F32))
            frames_backward(c)

            def put_back(rows, acc):
                s.eb[c, rows] = acc.astype(BF)

            back_in(c, put_back)
            s.cxs[c] = pad16(nt(proj_t, s.eb[c]))
            code_copy(c).start()
            return carry

        lax.fori_loop(0, 2, both, 0)

        def downs(c, carry):
            grad_down(c)
            return carry

        lax.fori_loop(0, 2, downs, 0)
        reduce_step("a", 0)

        def ups(c, carry):
            grad_up(c)

            @pl.when(c == 0)
            def _():
                reduce_step("a", 1)

            return carry

        lax.fori_loop(0, 2, ups, 0)
        reduce_step("b", 0)
        reduce_step("a", 2)

        def attns(c, carry):
            grad_attn(c)

            @pl.when(c == 0)
            def _():
                reduce_step("b", 1)

            return carry

        lax.fori_loop(0, 2, attns, 0)
        reduce_step("c", 0)
        reduce_step("a", 3)
        reduce_step("b", 2)
        for c in range(2):
            book_proj_terms(c, s.cxs[c][0:8].astype(F32), s.eb[c], s.cvec[c][0:8].astype(F32))

    @pl.when(is_e)
    def _():
        def backward(c, carry):
            code_copy(c).wait_recv()
            for f in range(2):
                cols = slice(GRID * f, GRID * f + GRID)
                s.cvec[c, :, cols] = nt(s.cxr[c, :, cols], s.perm[c]).astype(BF)
            g = tn(s.cvec[c][0:8], proj_t)
            s.hb[...] = g
            s.xs[c] = g.astype(BF)
            grad_down(c)

            @pl.when(c == 1)
            def _():
                reduce_step("a", 0)

            back_ff(c, lambda rows: s.hb[rows])

            @pl.when(c == 1)
            def _():
                reduce_step("a", 1)

            grad_up(c)

            @pl.when(c == 1)
            def _():
                reduce_step("b", 0)
                reduce_step("a", 2)

            window_backward(c, 0)

            @pl.when(c == 1)
            def _():
                reduce_step("b", 1)

            window_backward(c, 1)

            @pl.when(c == 1)
            def _():
                reduce_step("a", 3)

            def put_back(rows, acc):
                s.gob[rows] = acc.astype(BF)

            back_in(c, put_back)
            for f in range(2):
                back = tn(s.perm[c], s.gob[GRID * f : GRID * f + GRID])
                s.bo[pl.ds(c * CLIP + GRID * f, GRID), :] = back.astype(BF)
            bout_copy(c).start()
            grad_attn(c)

            @pl.when(c == 1)
            def _():
                reduce_step("c", 0)
                reduce_step("b", 2)

            book_proj_terms(c, s.cxr[c][0:8].astype(F32), s.eb[c], s.cvec[c][0:8].astype(F32))
            return carry

        lax.fori_loop(0, 2, backward, 0)

    reduce_step("c", 1)
    sums = jnp.concatenate(
        [
            jnp.sum(s.gacc[0], axis=0, keepdims=True),
            jnp.sum(s.gacc[1], axis=0, keepdims=True),
            jnp.zeros((6, D), F32),
        ],
        axis=0,
    )
    wide_sums = jnp.concatenate([jnp.zeros((72, D), F32), sums, jnp.zeros((48, D), F32)], axis=0)
    s.s_acc[...] += jnp.transpose(wide_sums).reshape(4, 8, 2, 8, 128)
    order = [
        "s0", "a4", "b3", "s1", "c2", "a5", "s2", "c3", "b4", "s3", "a6", "b5", "c4", "s4", "b6", "c5", "c6",
    ]
    for item in order:
        reduce_step(item[0], int(item[1]))

    half_rows = s.win[pl.ds(16 * (dp // 2), 16), :].astype(F32)
    piece = jnp.where(core == 0, half_rows[0:8], half_rows[8:16])
    ain_ref[0] = AVG_DECAY * avgin_ref[0] + (1.0 - AVG_DECAY) * (piece - LEARN_RATE * gin_ref[0])

    for c in range(2):
        code_copy(c).wait_send()
        bout_copy(c).wait()
    for k in ("a", "b", "c", "s"):
        for step in range(4 if k == "s" else 7):
            for cp in copies(k, step):
                cp.wait_send()


def body(
    boundary, in_weights, down_weight, gains, proj, codebook, codes, grids, orders, avg_in, avg_down
):
    vmem = pl.BlockSpec(memory_space=pltpu.VMEM)
    smem = pl.BlockSpec(memory_space=pltpu.SMEM)
    hbm = pl.BlockSpec(memory_space=pl.ANY)
    outs = (
        jax.ShapeDtypeStruct(boundary.shape, BF),
        jax.ShapeDtypeStruct(avg_in.shape, F32),
        jax.ShapeDtypeStruct(avg_down.shape, F32),
        jax.ShapeDtypeStruct((8, 128), F32),
        jax.ShapeDtypeStruct(avg_in.shape, F32),
        jax.ShapeDtypeStruct(avg_down.shape, F32),
    )
    scratch = [pltpu.VMEM(shape, dtype) for shape, dtype in SHAPES.values()]
    scratch += [pltpu.SemaphoreType.DMA((N_SEM,)), pltpu.SemaphoreType.DMA((N_SEM,)), pltpu.SemaphoreType.DMA((8,))]
    made = pl.pallas_call(
        mega,
        out_shape=outs,
        in_specs=[hbm, hbm, hbm, vmem, vmem, vmem, vmem, smem, smem, vmem, vmem],
        out_specs=[hbm] + [vmem] * 5,
        scratch_shapes=scratch,
        compiler_params=pltpu.CompilerParams(
            collective_id=0, has_side_effects=True, vmem_limit_bytes=63 << 20
        ),
        name="both_sections",
    )(
        boundary, in_weights, down_weight, gains, proj[0].T, codebook, codes.reshape(8, 128), grids, orders,
        avg_in, avg_down,
    )
    return pl.pallas_call(
        split_outputs,
        out_shape=(
            outs[0], outs[1], outs[2],
            jax.ShapeDtypeStruct((1, 2, 8), F32),
            jax.ShapeDtypeStruct((1, 8, 8), F32),
            jax.ShapeDtypeStruct(codebook.shape, F32),
            outs[4], outs[5],
        ),
        in_specs=[vmem] * 6,
        out_specs=[vmem] * 8,
        name="split_outputs",
    )(*made)


def split_outputs(
    bout_in, gin_in, gdn_in, small_in, ain_in, adn_in,
    bout, gin, gdn, ggain, gproj, gbook, ain, adn,
):
    bout[...] = bout_in[...]
    gin[...] = gin_in[...]
    gdn[...] = gdn_in[...]
    ain[...] = ain_in[...]
    adn[...] = adn_in[...]
    small = small_in[...]
    gbook[...] = small[:, 0:64]
    gproj[0] = small[:, 64:72]
    ggain[0] = jnp.transpose(jnp.concatenate([small] * 16, axis=0))[72:74, 0:8]


def solution(mesh):
    placed = (
        P("section", "dp", None),
        P("section", None, None),
        P("section", None, None),
        P("section", None, None),
        P("section", None, None),
        P(None, ("section", "dp")),
        P("dp"),
        P("dp"),
        P("dp", None),
        P("section", "dp", None),
        P("section", "dp", None),
    )
    return jax.shard_map(
        body,
        mesh=mesh,
        in_specs=placed,
        out_specs=(
            P("section", "dp", None),
            P("section", "dp", None),
            P("section", "dp", None),
            P("section", None, "dp"),
            P("section", "dp", None),
            P(None, ("section", "dp")),
            P("section", "dp", None),
            P("section", "dp", None),
        ),
        check_vma=False,
    )
```

```python
import functools

import jax
import jax.numpy as jnp
from jax import lax
from jax.experimental import pallas as pl
from jax.experimental.pallas import tpu as pltpu
from jax.sharding import PartitionSpec as P

BF = jnp.bfloat16
F32 = jnp.float32
I32 = jnp.int32
MESH = pl.DeviceIdType.MESH

D = 512
FF = 2048
CLIP = 512
GRID = 256
WINDOW = 64
HALF = 4096
NORM_EPS = 1e-05
AVG_DECAY = 0.9
LEARN_RATE = 0.0005
SCALE = 0.125
WB = 4

CHUNKS = {"a": (32, 512), "b": (16, 1024), "c": (16, 1024)}


def nn(left, right):
    return lax.dot_general(left, right, (((1,), (0,)), ((), ())), preferred_element_type=F32)


def nt(left, right):
    return lax.dot_general(left, right, (((1,), (1,)), ((), ())), preferred_element_type=F32)


def tn(left, right):
    return lax.dot_general(left, right, (((0,), (0,)), ((), ())), preferred_element_type=F32)


def tt(left, right):
    return lax.dot_general(left, right, (((0,), (1,)), ((), ())), preferred_element_type=F32)


def iota(shape, axis):
    return lax.broadcasted_iota(I32, shape, axis)


def normed(h):
    mean = jnp.mean(h, axis=-1, keepdims=True)
    c = h - mean
    var = jnp.mean(c * c, axis=-1, keepdims=True)
    r = lax.rsqrt(var + NORM_EPS)
    return c * r, r


def normed_back(grad, xhat, r, gain):
    t = grad * gain
    m1 = jnp.mean(t, axis=-1, keepdims=True)
    m2 = jnp.mean(t * xhat, axis=-1, keepdims=True)
    return r * (t - m1 - xhat * m2)


def gelu_pair(u):
    c0 = 0.7978845608028654
    c1 = 0.7978845608028654 * 0.044715
    m = c1 * (u * u)
    half = 0.5 + 0.5 * jnp.tanh(u * (c0 + m))
    value = u * half
    slope = half + (value - value * half) * (2.0 * c0 + 6.0 * m)
    return value, slope


def ten_shapes():
    shapes = {
        "xs": ((2, CLIP, D), BF),
        "win": ((D, 4 * D + FF), BF),
        "wdn": ((FF, D), BF),
        "perm": ((2, GRID, GRID), BF),
        "bd1": ((256, 256), BF),
        "bds": ((256, 256), BF),
        "bdf": ((256, 256), F32),
        "tbl": ((32, 2, 16, 128), BF),
        "pre": ((2, 2, 8, 128), F32),
        "cds": ((2, 8, CLIP), I32),
        "cxs": ((2, 16, CLIP), BF),
        "cxr": ((2, 16, CLIP), BF),
        "fcs": ((2, 8, CLIP), F32),
        "fcr": ((2, 8, CLIP), F32),
        "ent": ((2, 2, 8, CLIP), F32),
        "cvec": ((2, 16, CLIP), BF),
        "hb": ((CLIP, D), F32),
        "bo": ((2 * CLIP, D), BF),
        "gob": ((CLIP, D), BF),
        "xh1": ((2, CLIP, D), F32),
        "xh2": ((2, CLIP, D), F32),
        "r1": ((2, CLIP, 1), F32),
        "r2": ((2, CLIP, 1), F32),
        "a1": ((2, CLIP, D), BF),
        "a2": ((2, CLIP, D), BF),
        "qkv": ((2, CLIP, 3 * D), BF),
        "prob": ((2, CLIP, D), F32),
        "att": ((2, CLIP, D), BF),
        "act": ((2, CLIP, FF), BF),
        "gel": ((2, CLIP, FF), BF),
        "gy": ((2, CLIP, D), BF),
        "eb": ((2, CLIP, D), BF),
        "acc_dn": ((FF, D), F32),
        "acc_up": ((D, FF), F32),
        "acc_qkv": ((D, 3 * D), F32),
        "acc_out": ((D, D), F32),
        "s_acc": ((4, 8, 2, 8, 128), F32),
        "gacc": ((2, 8, D), F32),
        "s0": ((4, 8, 8, 128), F32),
        "s1": ((3, 8, 8, 128), F32),
        "s2": ((7, 8, 128), F32),
    }
    for k, (rows, w) in CHUNKS.items():
        h = w // 2
        shapes["sb0" + k] = ((4, 4, 2, rows, w), BF)
        shapes["r0" + k] = ((4, 4, 2, rows, w), BF)
        for ax in "zx":
            if k == "c":
                shapes["q" + ax + k] = ((3, 4, 2, rows, h), BF)
            else:
                for slot in "012":
                    shapes["q" + slot + ax + k] = ((2, 4, rows, h), BF)
            shapes["p" + ax + k] = ((7, rows, h), BF)
    return shapes


SHAPES = ten_shapes()
N_SEM = 130


class Refs:
    pass


def mega(
    x_hbm, win_hbm, wdn_hbm, gains_ref, proj_ref, book_ref, codes_ref, grids_ref, orders_ref,
    avgin_ref, avgdn_ref,
    bout_hbm, gin_ref, gdn_ref, small_ref, ain_ref, adn_ref,
    *scratch,
):
    s = Refs()
    for name, ref in zip(SHAPES, scratch):
        setattr(s, name, ref)
    send_sems, recv_sems, load_sems = scratch[len(SHAPES):]

    sec = lax.axis_index("section")
    dp = lax.axis_index("dp")
    core = dp % 2
    yh = (dp // 2) % 2
    x = (dp // 4) % 4
    z = dp // 16
    is_e = sec == 0
    is_d = sec == 1

    def place(zz, xx, yy, cc):
        return (sec, ((zz * 4 + xx) * 2 + yy) * 2 + cc)

    core_dev = place(z, x, yh, 1 - core)
    y_dev = place(z, x, 1 - yh, core)
    def flips(v):
        return {1: v + 1 - 2 * (v % 2), 2: (v + 2) % 4, 3: 3 - v}

    z_flip, x_flip = flips(z), flips(x)
    z_dev = [place((z + d) % 4, x, yh, core) for d in (1, 2, 3)]
    x_dev = [place(z, (x + d) % 4, yh, core) for d in (1, 2, 3)]
    sec_dev = (1 - sec, dp)
    sec_core_dev = (1 - sec, dp + 1 - 2 * core)
    around = [(d, y) for d in range(4) for y in range(2) if d + y > 0]
    zy_dev = [place((z + d) % 4, x, (yh + y) % 2, core) for d, y in around]
    xy_dev = [place(z, (x + d) % 4, (yh + y) % 2, core) for d, y in around]

    counter = [0]
    slots = {}

    def rcopy(key, src, dst, dev):
        if key not in slots:
            slots[key] = counter[0]
            counter[0] += 1
        i = slots[key]
        return pltpu.make_async_remote_copy(
            src_ref=src, dst_ref=dst, send_sem=send_sems.at[i], recv_sem=recv_sems.at[i],
            device_id=dev, device_id_type=MESH,
        )

    loads = [
        pltpu.make_async_copy(x_hbm.at[0, pl.ds(0, CLIP)], s.xs.at[0], load_sems.at[0]),
        pltpu.make_async_copy(win_hbm.at[0, :, pl.ds(0, 3 * D)], s.win.at[:, pl.ds(0, 3 * D)], load_sems.at[1]),
        pltpu.make_async_copy(
            win_hbm.at[0, :, pl.ds(3 * D, D + FF)], s.win.at[:, pl.ds(3 * D, D + FF)], load_sems.at[2]
        ),
        pltpu.make_async_copy(wdn_hbm.at[0], s.wdn, load_sems.at[3]),
        pltpu.make_async_copy(x_hbm.at[0, pl.ds(CLIP, CLIP)], s.xs.at[1], load_sems.at[4]),
    ]
    for load in loads:
        load.start()

    def bout_copy(c):
        rows = pl.ds(c * CLIP, CLIP)
        return pltpu.make_async_copy(s.bo.at[rows], bout_hbm.at[0, rows], load_sems.at[5 + c])

    barrier = pltpu.get_barrier_semaphore()
    peers = [core_dev, sec_dev, sec_core_dev] + zy_dev + xy_dev[1:]
    for dev in peers:
        pl.semaphore_signal(barrier, inc=1, device_id=dev, device_id_type=MESH)

    rows_i = iota((256, 256), 0)
    cols_i = iota((256, 256), 1)
    same = ((rows_i >> 6) == (cols_i >> 6)).astype(F32)
    s.bdf[...] = same * SCALE
    s.bd1[...] = same.astype(BF)
    s.bds[...] = (same * SCALE).astype(BF)
    for c in range(2):
        code_row = jnp.concatenate([codes_ref[4 * c + k : 4 * c + k + 1, :] for k in range(4)], axis=1)
        s.cds[c] = jnp.broadcast_to(code_row, (8, CLIP))

    proj_t = proj_ref[...]
    gain_one = gains_ref[0, 0:1, :].astype(F32)
    gain_two = gains_ref[0, 1:2, :].astype(F32)
    book = book_ref[...].astype(F32)
    s.pre[sec, core] = jnp.concatenate([book, jnp.zeros((8, 64), F32)], axis=1)
    s.gacc[...] = jnp.zeros((2, 8, D), F32)
    s.s_acc[...] = jnp.zeros((4, 8, 2, 8, 128), F32)

    pl.semaphore_wait(barrier, len(peers))

    def book_start():
        mine = s.pre.at[sec, core]

        @pl.when(is_e)
        def _():
            rcopy("ag0", mine, mine, sec_dev).start()
            rcopy("ag1", mine, mine, sec_core_dev).start()

        @pl.when(is_d)
        def _():
            rcopy("ag2", mine, mine, core_dev).start()

    def gather_book():
        chip = dp // 2
        rcopy("ag0", s.pre.at[0, core], s.pre.at[0, core], sec_dev).wait_recv()
        rcopy("ag1", s.pre.at[0, 1 - core], s.pre.at[0, 1 - core], sec_core_dev).wait_recv()
        rcopy("ag2", s.pre.at[1, 1 - core], s.pre.at[1, 1 - core], core_dev).wait_recv()
        for half in range(2):
            s.tbl[chip, half] = jnp.concatenate([s.pre[half, 0], s.pre[half, 1]], axis=0).astype(BF)
        part = s.tbl.at[chip]
        for i in range(7):
            rcopy("ag3%d" % i, part, part, xy_dev[i]).start()
        for i, (d, y) in enumerate(around):
            part = s.tbl.at[(z * 4 + (x + 4 - d) % 4) * 2 + (yh + 2 - y) % 2]
            rcopy("ag3%d" % i, part, part, xy_dev[i]).wait_recv()
        part = s.tbl.at[pl.ds(z * 8, 8)]
        for i in range(3):
            rcopy("ag4%d" % i, part, part, z_dev[i]).start()
        for i in range(3):
            part = s.tbl.at[pl.ds(((z + 3 - i) % 4) * 8, 8)]
            rcopy("ag4%d" % i, part, part, z_dev[i]).wait_recv()

    def book_finish():
        mine = s.pre.at[sec, core]

        @pl.when(is_e)
        def _():
            rcopy("ag0", mine, mine, sec_dev).wait_send()
            rcopy("ag1", mine, mine, sec_core_dev).wait_send()

        @pl.when(is_d)
        def _():
            rcopy("ag2", mine, mine, core_dev).wait_send()
            part = s.tbl.at[dp // 2]
            for i in range(7):
                rcopy("ag3%d" % i, part, part, xy_dev[i]).wait_send()
            part = s.tbl.at[pl.ds(z * 8, 8)]
            for i in range(3):
                rcopy("ag4%d" % i, part, part, z_dev[i]).wait_send()

    def onehots(c, half):
        code_row = s.cds[c][0:1, :] - half * HALF
        hi = code_row >> 6
        lo = code_row & 63
        lo_one = (iota((128, CLIP), 0) == lo).astype(F32).astype(BF)
        hi_mask = (iota((CLIP, CLIP), 0) >> 3) == hi
        return lo_one, hi_mask

    def entries(c):
        for half in range(2):
            lo_one, hi_mask = onehots(c, half)
            table = s.tbl[:, half].reshape(CLIP, 128)
            picked = jnp.where(hi_mask, nn(table, lo_one), 0.0)
            s.ent[c, half] = jnp.sum(picked.reshape(64, 8, CLIP), axis=0)

    def pad16(v):
        return jnp.concatenate([v, jnp.zeros((8, v.shape[1]), F32)], axis=0).astype(BF)

    def book_proj_terms(c, code_grad, wide_rows, narrow):
        lo_one, hi_mask = onehots(c, sec)
        spread = jnp.broadcast_to(code_grad[None], (64, 8, CLIP)).reshape(CLIP, CLIP)
        left = jnp.where(hi_mask, spread, 0.0).astype(BF)
        total = nt(left, lo_one)
        narrow_wide = jnp.concatenate(
            [jnp.zeros((64, CLIP), F32), narrow, jnp.zeros((56, CLIP), F32)], axis=0
        ).astype(BF)
        total = total + tt(wide_rows, narrow_wide)
        s.s_acc[...] += total.reshape(4, 8, 2, 8, 128)

    def norm_qkv(c, h):
        s.hb[...] = h
        xh, r = normed(h)
        s.xh1[c] = xh
        s.r1[c] = r
        a = (xh * gain_one).astype(BF)
        s.a1[c] = a
        for j in range(3):
            s.qkv[c, :, 512 * j : 512 * j + 512] = nn(a, s.win[:, 512 * j : 512 * j + 512]).astype(BF)

    def feed_forward(c, put):
        m = s.hb[...] + nn(s.att[c], s.win[:, 1536:2048])
        xh, r = normed(m)
        s.xh2[c] = xh
        s.r2[c] = r
        a = (xh * gain_two).astype(BF)
        s.a2[c] = a
        acc = m
        nxt = nn(a, s.win[:, 2048:2304])
        for j in range(8):
            cols = slice(256 * j, 256 * j + 256)
            u = nxt
            if j < 7:
                nxt = nn(a, s.win[:, 2304 + 256 * j : 2560 + 256 * j])
            value, slope = gelu_pair(u.astype(BF))
            s.act[c, :, cols] = value
            s.gel[c, :, cols] = slope
            acc = acc + nn(value, s.wdn[cols, :])
        put(acc)

    def units(c, w, count):
        out = []
        for n in range(count):
            rows = pl.ds((w * count + n) * WINDOW, WINDOW)
            for quad in range(2):
                out.append((rows, 256 * quad))
        return out

    def widened(v, mask):
        return jnp.concatenate([v] * 4, axis=0) * mask

    def heads_of(wide):
        return (wide[0:64] + wide[64:128]) + (wide[128:192] + wide[192:256])

    def window_forward(c, w):
        if True:
            us = units(c, w, WB)
            bds = s.bds[...]
            bdf = s.bdf[...]
            q = [s.qkv[c, r, o : o + 256] for r, o in us]
            k = [s.qkv[c, r, 512 + o : 768 + o] for r, o in us]
            v = [s.qkv[c, r, 1024 + o : 1280 + o] for r, o in us]
            scores = [nt(kk, widened(qq, bds)) for kk, qq in zip(k, q)]
            e = [jnp.exp(x - jnp.max(x, axis=0, keepdims=True)) for x in scores]
            p = [x * (1.0 / jnp.sum(x, axis=0, keepdims=True)) for x in e]
            wide = [tn(x.astype(BF), vv) for x, vv in zip(p, v)]
            att = [(heads_of(x * bdf) * (1.0 / SCALE)).astype(BF) for x in wide]
            for (r, o), pp, aa in zip(us, p, att):
                s.prob[c, r, o : o + 256] = pp
                s.att[c, r, o : o + 256] = aa

    def window_backward(c, w):
        if True:
            us = units(c, w, WB)
            bds = s.bds[...]
            bd1 = s.bd1[...]
            bdf = s.bdf[...]
            q = [s.qkv[c, r, o : o + 256] for r, o in us]
            k = [s.qkv[c, r, 512 + o : 768 + o] for r, o in us]
            v = [s.qkv[c, r, 1024 + o : 1280 + o] for r, o in us]
            go = [widened(s.gob[r, o : o + 256], bd1) for r, o in us]
            p = [s.prob[c, r, o : o + 256] for r, o in us]
            gp = [nt(vv, gg) for vv, gg in zip(v, go)]
            gv = [nn(pp.astype(BF), gg).astype(BF) for pp, gg in zip(p, go)]
            gs = [
                (pp * (x - jnp.sum(x * pp, axis=0, keepdims=True))).astype(BF)
                for pp, x in zip(p, gp)
            ]
            gk = [nn(x, widened(qq, bds)).astype(BF) for x, qq in zip(gs, q)]
            gq = [heads_of(tn(x, kk) * bdf).astype(BF) for x, kk in zip(gs, k)]
            for (r, o), a, b, d in zip(us, gq, gk, gv):
                s.qkv[c, r, o : o + 256] = a
                s.qkv[c, r, 512 + o : 768 + o] = b
                s.qkv[c, r, 1024 + o : 1280 + o] = d

    def head_sums(v):
        hi = v.astype(BF)
        lo = (v - hi.astype(F32)).astype(BF)
        return nn(hi, s.bd1[...]) + nn(lo, s.bd1[...])

    CR = 128

    def frames_forward(c):
        late0 = orders_ref[c, 0] > orders_ref[c, 1]
        sign = jnp.where(late0, 1.0, -1.0).astype(F32)

        def step(i, carry):
            r0 = pl.ds(i * CR, CR)
            r1 = pl.ds(GRID + i * CR, CR)
            for quad in range(2):
                qc = slice(256 * quad, 256 * quad + 256)
                kc = slice(512 + 256 * quad, 768 + 256 * quad)
                vc = slice(1024 + 256 * quad, 1280 + 256 * quad)
                q_late = jnp.where(late0, s.qkv[c, r0, qc].astype(F32), s.qkv[c, r1, qc].astype(F32))
                k_diff = sign * (s.qkv[c, r1, kc].astype(F32) - s.qkv[c, r0, kc].astype(F32))
                v0 = s.qkv[c, r0, vc].astype(F32)
                v1 = s.qkv[c, r1, vc].astype(F32)
                d = head_sums(q_late * k_diff) * SCALE
                e = jnp.exp(-jnp.abs(d))
                big = 1.0 / (1.0 + e)
                small = e * big
                p_other = jnp.where(d > 0.0, big, small)
                p_self = jnp.where(d > 0.0, small, big)
                s.prob[c, r0, qc] = p_other
                s.prob[c, r1, qc] = p_self
                po = p_other.astype(BF).astype(F32)
                ps = p_self.astype(BF).astype(F32)
                v_late = jnp.where(late0, v0, v1)
                v_early = jnp.where(late0, v1, v0)
                mix = ps * v_late + po * v_early
                s.att[c, r0, qc] = jnp.where(late0, mix, v0).astype(BF)
                s.att[c, r1, qc] = jnp.where(late0, v1, mix).astype(BF)
            return carry

        lax.fori_loop(0, GRID // CR, step, 0)

    def frames_backward(c):
        late0 = orders_ref[c, 0] > orders_ref[c, 1]
        sign = jnp.where(late0, 1.0, -1.0).astype(F32)

        def step(i, carry):
            r0 = pl.ds(i * CR, CR)
            r1 = pl.ds(GRID + i * CR, CR)
            for quad in range(2):
                qc = slice(256 * quad, 256 * quad + 256)
                kc = slice(512 + 256 * quad, 768 + 256 * quad)
                vc = slice(1024 + 256 * quad, 1280 + 256 * quad)
                q_late = jnp.where(late0, s.qkv[c, r0, qc].astype(F32), s.qkv[c, r1, qc].astype(F32))
                k_diff = sign * (s.qkv[c, r1, kc].astype(F32) - s.qkv[c, r0, kc].astype(F32))
                v_diff = sign * (s.qkv[c, r1, vc].astype(F32) - s.qkv[c, r0, vc].astype(F32))
                go0 = s.gob[r0, qc].astype(F32)
                go1 = s.gob[r1, qc].astype(F32)
                go_late = jnp.where(late0, go0, go1)
                go_early = jnp.where(late0, go1, go0)
                p_other = s.prob[c, r0, qc]
                p_self = s.prob[c, r1, qc]
                gs = p_other * p_self * head_sums(go_late * v_diff)
                gs = gs.astype(BF).astype(F32) * SCALE
                gq = gs * k_diff
                gk = gs * q_late
                gv_late = p_self.astype(BF).astype(F32) * go_late
                gv_early = go_early + p_other.astype(BF).astype(F32) * go_late
                s.qkv[c, r0, qc] = jnp.where(late0, gq, 0.0).astype(BF)
                s.qkv[c, r1, qc] = jnp.where(late0, 0.0, gq).astype(BF)
                s.qkv[c, r0, kc] = (-sign * gk).astype(BF)
                s.qkv[c, r1, kc] = (sign * gk).astype(BF)
                s.qkv[c, r0, vc] = jnp.where(late0, gv_late, gv_early).astype(BF)
                s.qkv[c, r1, vc] = jnp.where(late0, gv_early, gv_late).astype(BF)
            return carry

        lax.fori_loop(0, GRID // CR, step, 0)

    def gain_terms(which, grad, xhat):
        part = jnp.sum((grad * xhat).reshape(-1, 8, D), axis=0)
        s.gacc[which] += part

    def back_down(c):
        gz = s.xs[c]
        for j in range(4):
            cols = slice(512 * j, 512 * j + 512)
            s.gel[c, :, cols] = (nt(gz, s.wdn[cols, :]) * s.gel[c, :, cols].astype(F32)).astype(BF)

    def back_up(c, grad_of):
        acc = None
        for j in range(4):
            term = nt(s.gel[c, :, 512 * j : 512 * j + 512], s.win[:, 2048 + 512 * j : 2560 + 512 * j])
            acc = term if acc is None else acc + term
        xh = s.xh2[c]
        gain_terms(1, acc, xh)
        gm = grad_of() + normed_back(acc, xh, s.r2[c], gain_two)
        s.hb[...] = gm
        gy = gm.astype(BF)
        s.gy[c] = gy
        s.gob[...] = nt(gy, s.win[:, 1536:2048]).astype(BF)

    def back_in(c):
        acc = None
        for j in range(3):
            cols = slice(512 * j, 512 * j + 512)
            term = nt(s.qkv[c, :, cols], s.win[:, cols])
            acc = term if acc is None else acc + term
        xh = s.xh1[c]
        gain_terms(0, acc, xh)
        return s.hb[...] + normed_back(acc, xh, s.r1[c], gain_one)

    def add_into(ref, rows, cols, c, value):
        ref[rows, cols] = jnp.where(c == 0, value, ref[rows, cols] + value)

    def grad_down(c):
        for j in range(4):
            cols = slice(512 * j, 512 * j + 512)
            add_into(s.acc_dn, cols, slice(None), c, tn(s.act[c, :, cols], s.xs[c]))

    def grad_up(c):
        for j in range(4):
            cols = slice(512 * j, 512 * j + 512)
            add_into(s.acc_up, slice(None), cols, c, tn(s.a2[c], s.gel[c, :, cols]))

    def grad_attn(c):
        for j in range(3):
            cols = slice(512 * j, 512 * j + 512)
            add_into(s.acc_qkv, slice(None), cols, c, tn(s.a1[c], s.qkv[c, :, cols]))
        add_into(s.acc_out, slice(None), slice(None), c, tn(s.att[c], s.gy[c]))

    def share(k, i, to_core):
        n = 2 * i + to_core
        if k == "a":
            return s.acc_dn[pl.ds(pl.multiple_of(n * 32, 32), 32), :]
        rows = pl.ds(pl.multiple_of(n * 8, 8), 8)
        if k == "b":
            return jnp.concatenate([s.acc_up[rows, 0:1024], s.acc_up[rows, 1024:2048]], axis=0)
        return jnp.concatenate(
            [
                jnp.concatenate([s.acc_qkv[rows, 0:768], s.acc_out[rows, 0:256]], axis=1),
                jnp.concatenate([s.acc_qkv[rows, 768:1536], s.acc_out[rows, 256:512]], axis=1),
            ],
            axis=0,
        )

    def buf(name, k):
        return getattr(s, name + k)

    def copies(k, step):
        if k == "s":
            if step == 0:
                return [rcopy("s0", s.s_acc.at[:, :, 1 - core], s.s0, core_dev)]
            if step == 1:
                return [rcopy("s1%d" % i, s.s0.at[(z + 1 + i) % 4], s.s1.at[i], z_dev[i]) for i in range(3)]
            return [
                rcopy(
                    "s2%d" % i, s.s0.at[z, 2 * ((x + d) % 4) + (yh + y) % 2], s.s2.at[i], xy_dev[i]
                )
                for i, (d, y) in enumerate(around)
            ]
        rows, w = CHUNKS[k]
        h = w // 2
        r0 = buf("r0", k)
        if step == 0:
            return [rcopy(k + "0", buf("sb0", k), r0, core_dev)]
        lo, hi = pl.ds(0, h), pl.ds(h, h)
        out = []
        if step == 4:
            for i, (d, y) in enumerate(around):
                out.append(
                    rcopy(
                        "%s4x%d" % (k, i), r0.at[z, (x + d) % 4, (yh + y) % 2, :, lo],
                        buf("px", k).at[i], xy_dev[i],
                    )
                )
                out.append(
                    rcopy(
                        "%s4z%d" % (k, i), r0.at[(z + d) % 4, x, (yh + y) % 2, :, hi],
                        buf("pz", k).at[i], zy_dev[i],
                    )
                )
            return out
        if k == "c":
            for i in range(3):
                out.append(
                    rcopy("%s1z%d" % (k, i), r0.at[(z + 1 + i) % 4, :, :, :, lo], buf("qz", k).at[i], z_dev[i])
                )
                out.append(
                    rcopy("%s1x%d" % (k, i), r0.at[:, (x + 1 + i) % 4, :, :, hi], buf("qx", k).at[i], x_dev[i])
                )
            return out
        for y in range(2):
            first, second = ((1, 3), (3, 1))[y]
            hop = second if step == 3 else first
            block = {1: 2, 2: first, 3: second}[step]
            slot = {1: "q1", 2: "q0", 3: "q2"}[step]
            out.append(
                rcopy(
                    "%s%dz%d" % (k, step, y), r0.at[z_flip[block], :, y, :, lo],
                    buf(slot + "z", k).at[y], place(z_flip[hop], x, yh, core),
                )
            )
            out.append(
                rcopy(
                    "%s%dx%d" % (k, step, y), r0.at[:, x_flip[block], y, :, hi],
                    buf(slot + "x", k).at[y], place(z, x_flip[hop], yh, core),
                )
            )
        return out

    def arrived(k, step):
        for cp in copies(k, step):
            cp.wait_recv()

    def send(k, step):
        for cp in copies(k, step):
            cp.start()

    def total(parts):
        parts = [v.astype(F32) for v in parts]
        while len(parts) > 1:
            parts = [a + b for a, b in zip(parts[::2], parts[1::2])] + parts[len(parts) // 2 * 2 :]
        return parts[0]

    def reduce_step(k, step):
        if k == "s":
            if step > 0:
                arrived(k, step - 1)
            if step == 1:
                s.s0[...] += s.s_acc[:, :, core]
            elif step == 2:
                s.s0[z] += (s.s1[0] + s.s1[1]) + s.s1[2]
            elif step == 3:
                small_ref[...] = total([s.s0[z, 2 * x + yh]] + [s.s2[i] for i in range(7)])
                return
            send(k, step)
            return
        rows, w = CHUNKS[k]
        h = w // 2
        r0 = buf("r0", k)
        lo, hi = pl.ds(0, h), pl.ds(h, h)
        if step == 0:
            sb0 = buf("sb0", k)

            def body(i, carry):
                for y in range(2):
                    sb0[i // 4, i % 4, y] = share(k, 2 * i + y, 1 - core).astype(BF)
                return carry

            lax.fori_loop(0, 16, body, 0)
            send(k, 0)
        elif step == 1:
            arrived(k, 0)

            def body(i, carry):
                for y in range(2):
                    r0[i // 4, i % 4, y] = total([share(k, 2 * i + y, core), r0[i // 4, i % 4, y]]).astype(BF)
                return carry

            lax.fori_loop(0, 16, body, 0)
            send(k, 1)
            if k != "c":
                send(k, 2)
        elif step == 2:
            arrived(k, 1)
            for y in range(2):
                second = (3, 1)[y]
                zb, xb = z_flip[second], x_flip[second]
                r0[zb, :, y, :, lo] = total([r0[zb, :, y, :, lo], buf("q1z", k)[y]]).astype(BF)
                r0[:, xb, y, :, hi] = total([r0[:, xb, y, :, hi], buf("q1x", k)[y]]).astype(BF)
            send(k, 3)
        elif step == 3:
            if k == "c":
                arrived(k, 1)
                r0[z, :, :, :, lo] = total([r0[z, :, :, :, lo]] + [buf("qz", k)[i] for i in range(3)]).astype(BF)
                r0[:, x, :, :, hi] = total([r0[:, x, :, :, hi]] + [buf("qx", k)[i] for i in range(3)]).astype(BF)
            else:
                arrived(k, 2)
                arrived(k, 3)
                for y in range(2):
                    r0[z, :, y, :, lo] = total(
                        [r0[z, :, y, :, lo], buf("q0z", k)[y], buf("q2z", k)[y]]
                    ).astype(BF)
                    r0[:, x, y, :, hi] = total(
                        [r0[:, x, y, :, hi], buf("q0x", k)[y], buf("q2x", k)[y]]
                    ).astype(BF)
            send(k, 4)
        else:
            arrived(k, 4)
            left = total([r0[z, x, yh, :, lo]] + [buf("px", k)[i] for i in range(7)])
            right = total([r0[z, x, yh, :, hi]] + [buf("pz", k)[i] for i in range(7)])
            mine = jnp.concatenate([left, right], axis=1)
            if k == "a":
                gdn_ref[0] = mine
                piece = s.wdn[pl.ds(dp * 32, 32), :].astype(F32)
                adn_ref[0] = AVG_DECAY * avgdn_ref[0] + (1.0 - AVG_DECAY) * (piece - LEARN_RATE * mine)
            elif k == "b":
                gin_ref[0, :, 2048:3072] = mine[0:8]
                gin_ref[0, :, 3072:4096] = mine[8:16]
            else:
                gin_ref[0, :, 0:768] = mine[0:8, :768]
                gin_ref[0, :, 768:1536] = mine[8:16, :768]
                gin_ref[0, :, 1536:1792] = mine[0:8, 768:]
                gin_ref[0, :, 1792:2048] = mine[8:16, 768:]

    def code_copy(c):
        return pltpu.make_async_remote_copy(
            src_ref=s.fcs.at[c], dst_ref=s.fcr.at[c], send_sem=send_sems.at[N_SEM - 2 + c],
            recv_sem=recv_sems.at[N_SEM - 2 + c], device_id=sec_dev, device_id_type=MESH,
        )

    def grad_copy(c):
        return pltpu.make_async_remote_copy(
            src_ref=s.cxs.at[c], dst_ref=s.cxr.at[c], send_sem=send_sems.at[N_SEM - 4 + c],
            recv_sem=recv_sems.at[N_SEM - 4 + c], device_id=sec_dev, device_id_type=MESH,
        )

    book_start()

    @pl.when(is_e)
    def _():
        for c in range(2):
            grid_now = grids_ref[c]
            width = jnp.where(grid_now == 0, 16, jnp.where(grid_now == 1, 32, 8)).astype(I32)
            log_across = jnp.where(grid_now == 0, 1, jnp.where(grid_now == 1, 2, 0)).astype(I32)
            across_mask = jnp.where(grid_now == 0, 1, jnp.where(grid_now == 1, 3, 0)).astype(I32)
            window_no = rows_i >> 6
            inner = rows_i & 63
            source = (
                ((window_no >> log_across) * 8 + (inner >> 3)) * width
                + (window_no & across_mask) * 8
                + (inner & 7)
            )
            s.perm[c] = (source == cols_i).astype(F32).astype(BF)
        loads[0].wait()
        loads[1].wait()

        def forward(c, carry):
            @pl.when(c == 1)
            def _():
                loads[4].wait()

            raster = [s.xs[c, 0:GRID], s.xs[c, GRID:CLIP]]
            norm_qkv(c, jnp.concatenate([nn(s.perm[c], v) for v in raster], axis=0))
            window_forward(c, 0)
            window_forward(c, 1)

            @pl.when(c == 0)
            def _():
                loads[2].wait()
                loads[3].wait()

            def put(acc):
                s.eb[c] = acc.astype(BF)

            feed_forward(c, put)
            vec = nt(proj_t, s.eb[c])
            hi = vec.astype(BF).astype(F32)
            mid = (vec - hi).astype(BF).astype(F32)
            parts = jnp.concatenate([hi, mid, vec - hi - mid, jnp.zeros((8, CLIP), F32)], axis=0).astype(BF)
            for f in range(2):
                cols = slice(GRID * f, GRID * f + GRID)
                moved = nn(parts[:, cols], s.perm[c])
                s.fcs[c, :, cols] = (moved[0:8] + moved[8:16]) + moved[16:24]
            code_copy(c).start()
            return carry

        lax.fori_loop(0, 2, forward, 0)

    @pl.when(is_d)
    def _():
        gather_book()
        for c in range(2):
            entries(c)
        for load in loads:
            load.wait()

        def both(c, carry):
            code_copy(c).wait_recv()
            sent = (s.fcr[c] + s.ent[c, 0]).astype(BF).astype(F32)
            s.cvec[c] = pad16(sent + s.ent[c, 1])
            norm_qkv(c, tn(s.cvec[c][0:8], proj_t))
            frames_forward(c)

            def put(acc):
                s.bo[pl.ds(c * CLIP, CLIP), :] = acc.astype(BF)

            feed_forward(c, put)
            bout_copy(c).start()
            back_down(c)
            back_up(c, lambda: s.xs[c].astype(F32))
            frames_backward(c)
            s.eb[c] = back_in(c).astype(BF)
            s.cxs[c] = pad16(nt(proj_t, s.eb[c]))
            grad_copy(c).start()
            return carry

        lax.fori_loop(0, 2, both, 0)

        def downs(c, carry):
            grad_down(c)
            return carry

        lax.fori_loop(0, 2, downs, 0)
        reduce_step("a", 0)

        def ups(c, carry):
            grad_up(c)

            @pl.when(c == 0)
            def _():
                reduce_step("a", 1)

            return carry

        lax.fori_loop(0, 2, ups, 0)
        reduce_step("b", 0)

        def attns(c, carry):
            grad_attn(c)

            @pl.when(c == 0)
            def _():
                reduce_step("a", 2)
                reduce_step("b", 1)

            return carry

        lax.fori_loop(0, 2, attns, 0)
        reduce_step("c", 0)
        reduce_step("b", 2)
        for c in range(2):
            book_proj_terms(c, s.cxs[c][0:8].astype(F32), s.eb[c], s.cvec[c][0:8].astype(F32))
        reduce_step("c", 1)
        reduce_step("a", 3)

    @pl.when(is_e)
    def _():
        def backward(c, carry):
            grad_copy(c).wait_recv()
            for f in range(2):
                cols = slice(GRID * f, GRID * f + GRID)
                s.cvec[c, :, cols] = nt(s.cxr[c, :, cols], s.perm[c]).astype(BF)
            g = tn(s.cvec[c][0:8], proj_t)
            s.hb[...] = g
            s.xs[c] = g.astype(BF)
            grad_down(c)

            @pl.when(c == 1)
            def _():
                reduce_step("a", 0)

            back_down(c)
            grad_up(c)

            @pl.when(c == 1)
            def _():
                reduce_step("a", 1)
                reduce_step("b", 0)

            back_up(c, lambda: s.hb[...])

            @pl.when(c == 1)
            def _():
                reduce_step("b", 1)

            window_backward(c, 0)

            @pl.when(c == 1)
            def _():
                reduce_step("a", 2)

            window_backward(c, 1)
            grad_attn(c)

            @pl.when(c == 1)
            def _():
                reduce_step("c", 0)
                reduce_step("b", 2)

            s.gob[...] = back_in(c).astype(BF)
            for f in range(2):
                back = tn(s.perm[c], s.gob[GRID * f : GRID * f + GRID])
                s.bo[pl.ds(c * CLIP + GRID * f, GRID), :] = back.astype(BF)
            bout_copy(c).start()

            @pl.when(c == 1)
            def _():
                reduce_step("c", 1)
                reduce_step("a", 3)

            book_proj_terms(c, s.cxr[c][0:8].astype(F32), s.eb[c], s.cvec[c][0:8].astype(F32))
            return carry

        lax.fori_loop(0, 2, backward, 0)

    sums = jnp.concatenate(
        [
            jnp.sum(s.gacc[0], axis=0, keepdims=True),
            jnp.sum(s.gacc[1], axis=0, keepdims=True),
            jnp.zeros((6, D), F32),
        ],
        axis=0,
    )
    wide_sums = jnp.concatenate([jnp.zeros((72, D), F32), sums, jnp.zeros((48, D), F32)], axis=0)
    s.s_acc[...] += jnp.transpose(wide_sums).reshape(4, 8, 2, 8, 128)
    order = ["s0", "b3", "s1", "c3", "a4", "s2", "b4", "c4", "s3"]
    for item in order:
        reduce_step(item[0], int(item[1]))

    half_rows = s.win[pl.ds(16 * (dp // 2), 16), :].astype(F32)
    piece = jnp.where(core == 0, half_rows[0:8], half_rows[8:16])
    ain_ref[0] = AVG_DECAY * avgin_ref[0] + (1.0 - AVG_DECAY) * (piece - LEARN_RATE * gin_ref[0])

    for c in range(2):
        bout_copy(c).wait()

        @pl.when(is_e)
        def _():
            code_copy(c).wait_send()

        @pl.when(is_d)
        def _():
            grad_copy(c).wait_send()

    book_finish()
    for k in ("a", "b", "c", "s"):
        for step in {"s": (0, 1, 2), "c": (0, 1, 4)}.get(k, (0, 1, 2, 3, 4)):
            for cp in copies(k, step):
                cp.wait_send()


def body(
    boundary, in_weights, down_weight, gains, proj, codebook, codes, grids, orders, avg_in, avg_down
):
    vmem = pl.BlockSpec(memory_space=pltpu.VMEM)
    smem = pl.BlockSpec(memory_space=pltpu.SMEM)
    hbm = pl.BlockSpec(memory_space=pl.ANY)
    outs = (
        jax.ShapeDtypeStruct(boundary.shape, BF),
        jax.ShapeDtypeStruct(avg_in.shape, F32),
        jax.ShapeDtypeStruct(avg_down.shape, F32),
        jax.ShapeDtypeStruct((8, 128), F32),
        jax.ShapeDtypeStruct(avg_in.shape, F32),
        jax.ShapeDtypeStruct(avg_down.shape, F32),
    )
    scratch = [pltpu.VMEM(shape, dtype) for shape, dtype in SHAPES.values()]
    scratch += [pltpu.SemaphoreType.DMA((N_SEM,)), pltpu.SemaphoreType.DMA((N_SEM,)), pltpu.SemaphoreType.DMA((8,))]
    made = pl.pallas_call(
        mega,
        out_shape=outs,
        in_specs=[hbm, hbm, hbm, vmem, vmem, vmem, vmem, smem, smem, vmem, vmem],
        out_specs=[hbm] + [vmem] * 5,
        scratch_shapes=scratch,
        compiler_params=pltpu.CompilerParams(
            collective_id=0, has_side_effects=True, vmem_limit_bytes=63 << 20
        ),
        name="both_sections",
    )(
        boundary, in_weights, down_weight, gains, proj[0].T, codebook, codes.reshape(8, 128), grids, orders,
        avg_in, avg_down,
    )
    return pl.pallas_call(
        split_outputs,
        out_shape=(
            outs[0], outs[1], outs[2],
            jax.ShapeDtypeStruct((1, 2, 8), F32),
            jax.ShapeDtypeStruct((1, 8, 8), F32),
            jax.ShapeDtypeStruct(codebook.shape, F32),
            outs[4], outs[5],
        ),
        in_specs=[vmem] * 6,
        out_specs=[vmem] * 8,
        name="split_outputs",
    )(*made)


def split_outputs(
    bout_in, gin_in, gdn_in, small_in, ain_in, adn_in,
    bout, gin, gdn, ggain, gproj, gbook, ain, adn,
):
    bout[...] = bout_in[...]
    gin[...] = gin_in[...]
    gdn[...] = gdn_in[...]
    ain[...] = ain_in[...]
    adn[...] = adn_in[...]
    small = small_in[...]
    gbook[...] = small[:, 0:64]
    gproj[0] = small[:, 64:72]
    ggain[0] = jnp.transpose(jnp.concatenate([small] * 16, axis=0))[72:74, 0:8]


def solution(mesh):
    placed = (
        P("section", "dp", None),
        P("section", None, None),
        P("section", None, None),
        P("section", None, None),
        P("section", None, None),
        P(None, ("section", "dp")),
        P("dp"),
        P("dp"),
        P("dp", None),
        P("section", "dp", None),
        P("section", "dp", None),
    )
    return jax.shard_map(
        body,
        mesh=mesh,
        in_specs=placed,
        out_specs=(
            P("section", "dp", None),
            P("section", "dp", None),
            P("section", "dp", None),
            P("section", None, "dp"),
            P("section", "dp", None),
            P(None, ("section", "dp")),
            P("section", "dp", None),
            P("section", "dp", None),
        ),
        check_vma=False,
    )
```

```python
import functools

import jax
import jax.numpy as jnp
from jax import lax
from jax.experimental import pallas as pl
from jax.experimental.pallas import tpu as pltpu
from jax.sharding import PartitionSpec as P

BF = jnp.bfloat16
F32 = jnp.float32
I32 = jnp.int32
MESH = pl.DeviceIdType.MESH

D = 512
FF = 2048
CLIP = 512
GRID = 256
WINDOW = 64
HALF = 4096
NORM_EPS = 1e-05
AVG_DECAY = 0.9
LEARN_RATE = 0.0005
SCALE = 0.125
WB = 4

CHUNKS = {"a": (32, 512), "b": (16, 1024), "c": (16, 768), "o": (16, 256)}


def nn(left, right):
    return lax.dot_general(left, right, (((1,), (0,)), ((), ())), preferred_element_type=F32)


def nt(left, right):
    return lax.dot_general(left, right, (((1,), (1,)), ((), ())), preferred_element_type=F32)


def tn(left, right):
    return lax.dot_general(left, right, (((0,), (0,)), ((), ())), preferred_element_type=F32)


def tt(left, right):
    return lax.dot_general(left, right, (((0,), (1,)), ((), ())), preferred_element_type=F32)


def iota(shape, axis):
    return lax.broadcasted_iota(I32, shape, axis)


def normed(h):
    mean = jnp.mean(h, axis=-1, keepdims=True)
    c = h - mean
    var = jnp.mean(c * c, axis=-1, keepdims=True)
    r = lax.rsqrt(var + NORM_EPS)
    return c * r, r


def normed_back(grad, xhat, r, gain):
    t = grad * gain
    m1 = jnp.mean(t, axis=-1, keepdims=True)
    m2 = jnp.mean(t * xhat, axis=-1, keepdims=True)
    return r * (t - m1 - xhat * m2)


def gelu_pair(u):
    c0 = 0.7978845608028654
    c1 = 0.7978845608028654 * 0.044715
    m = c1 * (u * u)
    half = 0.5 + 0.5 * jnp.tanh(u * (c0 + m))
    value = u * half
    slope = half + (value - value * half) * (2.0 * c0 + 6.0 * m)
    return value, slope


def ten_shapes():
    shapes = {
        "xs": ((2, CLIP, D), BF),
        "win": ((D, 4 * D + FF), BF),
        "wdn": ((FF, D), BF),
        "perm": ((2, GRID, GRID), BF),
        "bd1": ((256, 256), BF),
        "bds": ((256, 256), BF),
        "bdf": ((256, 256), F32),
        "tbl": ((32, 16, 128), BF),
        "pre": ((2, 2, 8, 128), F32),
        "cds": ((2, 8, CLIP), I32),
        "cxs": ((2, 16, CLIP), BF),
        "cxr": ((2, 16, CLIP), BF),
        "fcs": ((2, 8, CLIP), F32),
        "fcr": ((2, 8, CLIP), F32),
        "ent": ((2, 2, 8, CLIP), F32),
        "cvec": ((2, 16, CLIP), BF),
        "hb": ((CLIP, D), F32),
        "bo": ((2 * CLIP, D), BF),
        "avi": ((8, 4 * D + FF), F32),
        "avd": ((32, D), F32),
        "gob": ((CLIP, D), BF),
        "xh1": ((2, CLIP, D), F32),
        "xh2": ((2, CLIP, D), F32),
        "r1": ((2, CLIP, 1), F32),
        "r2": ((2, CLIP, 1), F32),
        "a1": ((2, CLIP, D), BF),
        "a2": ((2, CLIP, D), BF),
        "qkv": ((2, CLIP, 3 * D), BF),
        "prob": ((2, CLIP, D), F32),
        "att": ((2, CLIP, D), BF),
        "act": ((2, CLIP, FF), BF),
        "gel": ((2, CLIP, FF), BF),
        "gy": ((2, CLIP, D), BF),
        "eb": ((2, CLIP, D), BF),
        "acc_dn": ((FF, D), F32),
        "acc_up": ((D, FF), F32),
        "acc_qkv": ((D, 3 * D), F32),
        "acc_out": ((D, D), F32),
        "s_acc": ((4, 8, 2, 8, 128), F32),
        "gacc": ((2, 8, D), F32),
        "s0": ((4, 8, 8, 128), F32),
        "s1": ((3, 8, 8, 128), F32),
        "s2": ((7, 8, 128), F32),
    }
    for k, (rows, w) in CHUNKS.items():
        h = w // 2
        shapes["sb0" + k] = ((4, 4, 2, rows, w), BF)
        shapes["r0" + k] = ((4, 4, 2, rows, w), BF)
        for ax in "zx":
            if k in "co":
                shapes["q" + ax + k] = ((3, 4, 2, rows, h), BF)
            else:
                for slot in "012":
                    shapes["q" + slot + ax + k] = ((2, 4, rows, h), BF)
            shapes["p" + ax + k] = ((7, rows, h), BF)
    return shapes


SHAPES = ten_shapes()
N_SEM = 160


class Refs:
    pass


def mega(
    x_hbm, win_hbm, wdn_hbm, gains_ref, proj_ref, book_ref, codes_ref, grids_ref, orders_ref,
    avgin_hbm, avgdn_hbm,
    bout_hbm, gin_ref, gdn_ref, small_ref, ain_ref, adn_ref,
    *scratch,
):
    s = Refs()
    for name, ref in zip(SHAPES, scratch):
        setattr(s, name, ref)
    send_sems, recv_sems, load_sems = scratch[len(SHAPES):]

    sec = lax.axis_index("section")
    dp = lax.axis_index("dp")
    core = dp % 2
    yh = (dp // 2) % 2
    x = (dp // 4) % 4
    z = dp // 16
    is_e = sec == 0
    is_d = sec == 1

    def place(zz, xx, yy, cc):
        return (sec, ((zz * 4 + xx) * 2 + yy) * 2 + cc)

    core_dev = place(z, x, yh, 1 - core)
    y_dev = place(z, x, 1 - yh, core)
    def flips(v):
        return {1: v + 1 - 2 * (v % 2), 2: (v + 2) % 4, 3: 3 - v}

    z_flip, x_flip = flips(z), flips(x)
    z_dev = [place((z + d) % 4, x, yh, core) for d in (1, 2, 3)]
    x_dev = [place(z, (x + d) % 4, yh, core) for d in (1, 2, 3)]
    sec_dev = (1 - sec, dp)
    sec_core_dev = (1 - sec, dp + 1 - 2 * core)
    around = [(d, y) for d in range(4) for y in range(2) if d + y > 0]
    zy_dev = [place((z + d) % 4, x, (yh + y) % 2, core) for d, y in around]
    xy_dev = [place(z, (x + d) % 4, (yh + y) % 2, core) for d, y in around]

    counter = [0]
    slots = {}

    def rcopy(key, src, dst, dev):
        if key not in slots:
            slots[key] = counter[0]
            counter[0] += 1
        i = slots[key]
        return pltpu.make_async_remote_copy(
            src_ref=src, dst_ref=dst, send_sem=send_sems.at[i], recv_sem=recv_sems.at[i],
            device_id=dev, device_id_type=MESH,
        )

    loads = [
        pltpu.make_async_copy(x_hbm.at[0, pl.ds(0, CLIP)], s.xs.at[0], load_sems.at[0]),
        pltpu.make_async_copy(win_hbm.at[0, :, pl.ds(0, 3 * D)], s.win.at[:, pl.ds(0, 3 * D)], load_sems.at[1]),
        pltpu.make_async_copy(
            win_hbm.at[0, :, pl.ds(3 * D, D + FF)], s.win.at[:, pl.ds(3 * D, D + FF)], load_sems.at[2]
        ),
        pltpu.make_async_copy(wdn_hbm.at[0], s.wdn, load_sems.at[3]),
        pltpu.make_async_copy(x_hbm.at[0, pl.ds(CLIP, CLIP)], s.xs.at[1], load_sems.at[4]),
    ]
    averages = [
        pltpu.make_async_copy(avgin_hbm.at[0], s.avi, load_sems.at[7]),
        pltpu.make_async_copy(avgdn_hbm.at[0], s.avd, load_sems.at[8]),
    ]
    for load in loads + averages:
        load.start()

    def bout_copy(c):
        rows = pl.ds(c * CLIP, CLIP)
        return pltpu.make_async_copy(s.bo.at[rows], bout_hbm.at[0, rows], load_sems.at[5 + c])

    barrier = pltpu.get_barrier_semaphore()
    far = [(i, j, y) for i in range(4) for j in range(4) for y in range(2) if i + j + y > 0]
    far_dev = [place((z + i) % 4, (x + j) % 4, (yh + y) % 2, core) for i, j, y in far]
    peers = [core_dev, sec_dev, sec_core_dev] + far_dev
    for dev in peers:
        pl.semaphore_signal(barrier, inc=1, device_id=dev, device_id_type=MESH)

    rows_i = iota((256, 256), 0)
    cols_i = iota((256, 256), 1)
    same = ((rows_i >> 6) == (cols_i >> 6)).astype(F32)
    s.bdf[...] = same * SCALE
    s.bd1[...] = same.astype(BF)
    s.bds[...] = (same * SCALE).astype(BF)
    for c in range(2):
        code_row = jnp.concatenate([codes_ref[4 * c + k : 4 * c + k + 1, :] for k in range(4)], axis=1)
        s.cds[c] = jnp.broadcast_to(code_row, (8, CLIP))

    proj_t = proj_ref[...]
    gain_one = gains_ref[0, 0:1, :].astype(F32)
    gain_two = gains_ref[0, 1:2, :].astype(F32)
    book = book_ref[...].astype(F32)
    empty = jnp.zeros((8, 64), F32)
    s.pre[sec, core] = jnp.where(
        is_e, jnp.concatenate([book, empty], axis=1), jnp.concatenate([empty, book], axis=1)
    )
    s.gacc[...] = jnp.zeros((2, 8, D), F32)
    s.s_acc[...] = jnp.zeros((4, 8, 2, 8, 128), F32)

    def book_start():
        pl.semaphore_wait(barrier, len(peers))
        mine = s.pre.at[sec, core]

        @pl.when(is_e)
        def _():
            rcopy("ag0", mine, mine, sec_dev).start()
            rcopy("ag1", mine, mine, sec_core_dev).start()

        @pl.when(is_d)
        def _():
            rcopy("ag2", mine, mine, core_dev).start()

    def gather_book():
        chip = dp // 2
        rcopy("ag0", s.pre.at[0, core], s.pre.at[0, core], sec_dev).wait_recv()
        rcopy("ag1", s.pre.at[0, 1 - core], s.pre.at[0, 1 - core], sec_core_dev).wait_recv()
        rcopy("ag2", s.pre.at[1, 1 - core], s.pre.at[1, 1 - core], core_dev).wait_recv()
        s.tbl[chip] = jnp.concatenate([s.pre[0, 0] + s.pre[1, 0], s.pre[0, 1] + s.pre[1, 1]], axis=0).astype(BF)
        part = s.tbl.at[chip]
        for n in range(31):
            rcopy("ag3%d" % n, part, part, far_dev[n]).start()
        for n, (i, j, y) in enumerate(far):
            part = s.tbl.at[(((z + 4 - i) % 4) * 4 + (x + 4 - j) % 4) * 2 + (yh + 2 - y) % 2]
            rcopy("ag3%d" % n, part, part, far_dev[n]).wait_recv()

    def book_finish():
        mine = s.pre.at[sec, core]

        @pl.when(is_e)
        def _():
            rcopy("ag0", mine, mine, sec_dev).wait_send()
            rcopy("ag1", mine, mine, sec_core_dev).wait_send()

        @pl.when(is_d)
        def _():
            rcopy("ag2", mine, mine, core_dev).wait_send()
            part = s.tbl.at[dp // 2]
            for n in range(31):
                rcopy("ag3%d" % n, part, part, far_dev[n]).wait_send()

    def onehots(c, half, shift):
        code_row = s.cds[c][0:1, :] - half * HALF
        hi = code_row >> 6
        lo = code_row & 63
        lo_one = (iota((128, CLIP), 0) == lo + shift).astype(F32).astype(BF)
        hi_mask = (iota((CLIP, CLIP), 0) >> 3) == hi
        return lo_one, hi_mask

    def entries(c):
        for half in range(2):
            lo_one, hi_mask = onehots(c, half, 64 * half)
            table = s.tbl[...].reshape(CLIP, 128)
            picked = jnp.where(hi_mask, nn(table, lo_one), 0.0)
            s.ent[c, half] = jnp.sum(picked.reshape(64, 8, CLIP), axis=0)

    def pad16(v):
        return jnp.concatenate([v, jnp.zeros((8, v.shape[1]), F32)], axis=0).astype(BF)

    def book_proj_terms(c, code_grad, wide_rows, narrow):
        lo_one, hi_mask = onehots(c, sec, 0)
        spread = jnp.broadcast_to(code_grad[None], (64, 8, CLIP)).reshape(CLIP, CLIP)
        left = jnp.where(hi_mask, spread, 0.0).astype(BF)
        total = nt(left, lo_one)
        narrow_wide = jnp.concatenate(
            [jnp.zeros((64, CLIP), F32), narrow, jnp.zeros((56, CLIP), F32)], axis=0
        ).astype(BF)
        total = total + tt(wide_rows, narrow_wide)
        s.s_acc[...] += total.reshape(4, 8, 2, 8, 128)

    def norm_qkv(c, parts):
        halves = [slice(0, 256), slice(256, 512)]
        a = []
        for rows, h in zip(halves, parts):
            s.hb[rows] = h
            xh, r = normed(h)
            s.xh1[c, rows] = xh
            s.r1[c, rows] = r
            a.append((xh * gain_one).astype(BF))
            s.a1[c, rows] = a[-1]
        for j in range(3):
            for rows, v in zip(halves, a):
                s.qkv[c, rows, 512 * j : 512 * j + 512] = nn(v, s.win[:, 512 * j : 512 * j + 512]).astype(BF)

    def feed_forward(c, put):
        m = s.hb[...] + nn(s.att[c], s.win[:, 1536:2048])
        xh, r = normed(m)
        s.xh2[c] = xh
        s.r2[c] = r
        a = (xh * gain_two).astype(BF)
        s.a2[c] = a
        acc = m
        nxt = nn(a, s.win[:, 2048:2304])
        for j in range(8):
            cols = slice(256 * j, 256 * j + 256)
            u = nxt
            if j < 7:
                nxt = nn(a, s.win[:, 2304 + 256 * j : 2560 + 256 * j])
            value, slope = gelu_pair(u.astype(BF))
            s.act[c, :, cols] = value
            s.gel[c, :, cols] = slope
            acc = acc + nn(value, s.wdn[cols, :])
        put(acc)

    def units(c, w, count):
        out = []
        for n in range(count):
            rows = pl.ds((w * count + n) * WINDOW, WINDOW)
            for quad in range(2):
                out.append((rows, 256 * quad))
        return out

    def widened(v, mask):
        return jnp.concatenate([v] * 4, axis=0) * mask

    def heads_of(wide):
        return (wide[0:64] + wide[64:128]) + (wide[128:192] + wide[192:256])

    def window_forward(c, w):
        if True:
            us = units(c, w, WB)
            bds = s.bds[...]
            bdf = s.bdf[...]
            q = [s.qkv[c, r, o : o + 256] for r, o in us]
            k = [s.qkv[c, r, 512 + o : 768 + o] for r, o in us]
            v = [s.qkv[c, r, 1024 + o : 1280 + o] for r, o in us]
            scores = [nt(kk, widened(qq, bds)) for kk, qq in zip(k, q)]
            e = [jnp.exp(x - jnp.max(x, axis=0, keepdims=True)) for x in scores]
            p = [x * (1.0 / jnp.sum(x, axis=0, keepdims=True)) for x in e]
            wide = [tn(x.astype(BF), vv) for x, vv in zip(p, v)]
            att = [(heads_of(x * bdf) * (1.0 / SCALE)).astype(BF) for x in wide]
            for (r, o), pp, aa in zip(us, p, att):
                s.prob[c, r, o : o + 256] = pp
                s.att[c, r, o : o + 256] = aa

    def window_backward(c, w):
        if True:
            us = units(c, w, WB)
            bds = s.bds[...]
            bd1 = s.bd1[...]
            bdf = s.bdf[...]
            q = [s.qkv[c, r, o : o + 256] for r, o in us]
            k = [s.qkv[c, r, 512 + o : 768 + o] for r, o in us]
            v = [s.qkv[c, r, 1024 + o : 1280 + o] for r, o in us]
            go = [widened(s.gob[r, o : o + 256], bd1) for r, o in us]
            p = [s.prob[c, r, o : o + 256] for r, o in us]
            gp = [nt(vv, gg) for vv, gg in zip(v, go)]
            gv = [nn(pp.astype(BF), gg).astype(BF) for pp, gg in zip(p, go)]
            gs = [
                (pp * (x - jnp.sum(x * pp, axis=0, keepdims=True))).astype(BF)
                for pp, x in zip(p, gp)
            ]
            gk = [nn(x, widened(qq, bds)).astype(BF) for x, qq in zip(gs, q)]
            gq = [heads_of(tn(x, kk) * bdf).astype(BF) for x, kk in zip(gs, k)]
            for (r, o), a, b, d in zip(us, gq, gk, gv):
                s.qkv[c, r, o : o + 256] = a
                s.qkv[c, r, 512 + o : 768 + o] = b
                s.qkv[c, r, 1024 + o : 1280 + o] = d

    def head_sums(v):
        return nn(v, s.bd1[...])

    CR = 256

    def frames_forward(c):
        late0 = orders_ref[c, 0] > orders_ref[c, 1]
        sign = jnp.where(late0, 1.0, -1.0).astype(F32)
        r0 = slice(0, GRID)
        r1 = slice(GRID, CLIP)
        for quad in range(2):
            qc = slice(256 * quad, 256 * quad + 256)
            kc = slice(512 + 256 * quad, 768 + 256 * quad)
            vc = slice(1024 + 256 * quad, 1280 + 256 * quad)
            q_late = jnp.where(late0, s.qkv[c, r0, qc], s.qkv[c, r1, qc])
            k_diff = s.qkv[c, r1, kc] - s.qkv[c, r0, kc]
            v0 = s.qkv[c, r0, vc]
            v1 = s.qkv[c, r1, vc]
            d = head_sums(q_late * k_diff) * (sign * SCALE)
            e = jnp.exp(-jnp.abs(d))
            big = 1.0 / (1.0 + e)
            small = e * big
            p_other = jnp.where(d > 0.0, big, small)
            p_self = jnp.where(d > 0.0, small, big)
            s.prob[c, r0, qc] = p_other
            s.prob[c, r1, qc] = p_self
            p0 = jnp.where(late0, p_self, p_other).astype(BF)
            p1 = jnp.where(late0, p_other, p_self).astype(BF)
            mix = (p0.astype(F32) * v0.astype(F32) + p1.astype(F32) * v1.astype(F32)).astype(BF)
            s.att[c, r0, qc] = jnp.where(late0, mix, v0)
            s.att[c, r1, qc] = jnp.where(late0, v1, mix)

    def frames_backward(c):
        late0 = orders_ref[c, 0] > orders_ref[c, 1]
        r0 = slice(0, GRID)
        r1 = slice(GRID, CLIP)
        for quad in range(2):
            qc = slice(256 * quad, 256 * quad + 256)
            kc = slice(512 + 256 * quad, 768 + 256 * quad)
            vc = slice(1024 + 256 * quad, 1280 + 256 * quad)
            q_late = jnp.where(late0, s.qkv[c, r0, qc], s.qkv[c, r1, qc])
            k_diff = s.qkv[c, r1, kc] - s.qkv[c, r0, kc]
            v_diff = s.qkv[c, r1, vc] - s.qkv[c, r0, vc]
            go0 = s.gob[r0, qc]
            go1 = s.gob[r1, qc]
            go_late = jnp.where(late0, go0, go1)
            go_early = jnp.where(late0, go1, go0)
            p_other = s.prob[c, r0, qc]
            p_self = s.prob[c, r1, qc]
            gs = (p_other * p_self * head_sums(go_late * v_diff)).astype(BF).astype(F32) * SCALE
            gq = (gs * k_diff.astype(F32)).astype(BF)
            gk = gs * q_late.astype(F32)
            late32 = go_late.astype(F32)
            gv_late = (p_self.astype(BF).astype(F32) * late32).astype(BF)
            gv_early = (go_early.astype(F32) + p_other.astype(BF).astype(F32) * late32).astype(BF)
            none = jnp.zeros_like(gq)
            s.qkv[c, r0, qc] = jnp.where(late0, gq, none)
            s.qkv[c, r1, qc] = jnp.where(late0, none, gq)
            s.qkv[c, r0, kc] = (-gk).astype(BF)
            s.qkv[c, r1, kc] = gk.astype(BF)
            s.qkv[c, r0, vc] = jnp.where(late0, gv_late, gv_early)
            s.qkv[c, r1, vc] = jnp.where(late0, gv_early, gv_late)

    def gain_terms(which, grad, xhat):
        part = jnp.sum((grad * xhat).reshape(-1, 8, D), axis=0)
        s.gacc[which] += part

    def back_down(c):
        gz = s.xs[c]
        for j in range(4):
            cols = slice(512 * j, 512 * j + 512)
            s.gel[c, :, cols] = (nt(gz, s.wdn[cols, :]) * s.gel[c, :, cols].astype(F32)).astype(BF)

    def back_up(c, grad_of):
        acc = None
        for j in range(4):
            term = nt(s.gel[c, :, 512 * j : 512 * j + 512], s.win[:, 2048 + 512 * j : 2560 + 512 * j])
            acc = term if acc is None else acc + term
        xh = s.xh2[c]
        gain_terms(1, acc, xh)
        gm = grad_of() + normed_back(acc, xh, s.r2[c], gain_two)
        s.hb[...] = gm
        gy = gm.astype(BF)
        s.gy[c] = gy
        s.gob[...] = nt(gy, s.win[:, 1536:2048]).astype(BF)

    def back_in(c):
        acc = None
        for j in range(3):
            cols = slice(512 * j, 512 * j + 512)
            term = nt(s.qkv[c, :, cols], s.win[:, cols])
            acc = term if acc is None else acc + term
        xh = s.xh1[c]
        gain_terms(0, acc, xh)
        return s.hb[...] + normed_back(acc, xh, s.r1[c], gain_one)

    def add_into(ref, rows, cols, c, value):
        ref[rows, cols] = jnp.where(c == 0, value, ref[rows, cols] + value)

    def grad_down(c):
        for j in range(4):
            cols = slice(512 * j, 512 * j + 512)
            add_into(s.acc_dn, cols, slice(None), c, tn(s.act[c, :, cols], s.xs[c]))

    def grad_up(c):
        for j in range(4):
            cols = slice(512 * j, 512 * j + 512)
            add_into(s.acc_up, slice(None), cols, c, tn(s.a2[c], s.gel[c, :, cols]))

    def grad_out(c):
        add_into(s.acc_out, slice(None), slice(None), c, tn(s.att[c], s.gy[c]))

    def grad_attn(c):
        for j in range(3):
            cols = slice(512 * j, 512 * j + 512)
            add_into(s.acc_qkv, slice(None), cols, c, tn(s.a1[c], s.qkv[c, :, cols]))

    def share(k, i, to_core):
        n = 2 * i + to_core
        if k == "a":
            return s.acc_dn[pl.ds(pl.multiple_of(n * 32, 32), 32), :]
        rows = pl.ds(pl.multiple_of(n * 8, 8), 8)
        ref, w = {"b": (s.acc_up, 1024), "c": (s.acc_qkv, 768), "o": (s.acc_out, 256)}[k]
        return jnp.concatenate([ref[rows, 0:w], ref[rows, w : 2 * w]], axis=0)

    def buf(name, k):
        return getattr(s, name + k)

    def copies(k, step):
        if k == "s":
            if step == 0:
                return [rcopy("s0", s.s_acc.at[:, :, 1 - core], s.s0, core_dev)]
            if step == 1:
                return [rcopy("s1%d" % i, s.s0.at[(z + 1 + i) % 4], s.s1.at[i], z_dev[i]) for i in range(3)]
            return [
                rcopy(
                    "s2%d" % i, s.s0.at[z, 2 * ((x + d) % 4) + (yh + y) % 2], s.s2.at[i], xy_dev[i]
                )
                for i, (d, y) in enumerate(around)
            ]
        rows, w = CHUNKS[k]
        h = w // 2
        r0 = buf("r0", k)
        if step == 0:
            return [rcopy(k + "0", buf("sb0", k), r0, core_dev)]
        lo, hi = pl.ds(0, h), pl.ds(h, h)
        out = []
        if step == 4:
            for i, (d, y) in enumerate(around):
                out.append(
                    rcopy(
                        "%s4x%d" % (k, i), r0.at[z, (x + d) % 4, (yh + y) % 2, :, lo],
                        buf("px", k).at[i], xy_dev[i],
                    )
                )
                out.append(
                    rcopy(
                        "%s4z%d" % (k, i), r0.at[(z + d) % 4, x, (yh + y) % 2, :, hi],
                        buf("pz", k).at[i], zy_dev[i],
                    )
                )
            return out
        if k in "co":
            for i in range(3):
                out.append(
                    rcopy("%s1z%d" % (k, i), r0.at[(z + 1 + i) % 4, :, :, :, lo], buf("qz", k).at[i], z_dev[i])
                )
                out.append(
                    rcopy("%s1x%d" % (k, i), r0.at[:, (x + 1 + i) % 4, :, :, hi], buf("qx", k).at[i], x_dev[i])
                )
            return out
        for y in range(2):
            first, second = ((1, 3), (3, 1))[y]
            hop = second if step == 3 else first
            block = {1: 2, 2: first, 3: second}[step]
            slot = {1: "q1", 2: "q0", 3: "q2"}[step]
            out.append(
                rcopy(
                    "%s%dz%d" % (k, step, y), r0.at[z_flip[block], :, y, :, lo],
                    buf(slot + "z", k).at[y], place(z_flip[hop], x, yh, core),
                )
            )
            out.append(
                rcopy(
                    "%s%dx%d" % (k, step, y), r0.at[:, x_flip[block], y, :, hi],
                    buf(slot + "x", k).at[y], place(z, x_flip[hop], yh, core),
                )
            )
        return out

    def arrived(k, step):
        for cp in copies(k, step):
            cp.wait_recv()

    def send(k, step):
        for cp in copies(k, step):
            cp.start()

    def total(parts):
        parts = [v.astype(F32) for v in parts]
        while len(parts) > 1:
            parts = [a + b for a, b in zip(parts[::2], parts[1::2])] + parts[len(parts) // 2 * 2 :]
        return parts[0]

    def reduce_step(k, step):
        if k == "s":
            if step > 0:
                arrived(k, step - 1)
            if step == 1:
                s.s0[...] += s.s_acc[:, :, core]
            elif step == 2:
                s.s0[z] += (s.s1[0] + s.s1[1]) + s.s1[2]
            elif step == 3:
                small_ref[...] = total([s.s0[z, 2 * x + yh]] + [s.s2[i] for i in range(7)])
                return
            send(k, step)
            return
        rows, w = CHUNKS[k]
        h = w // 2
        r0 = buf("r0", k)
        lo, hi = pl.ds(0, h), pl.ds(h, h)
        if step == 0:
            sb0 = buf("sb0", k)

            def body(i, carry):
                for y in range(2):
                    sb0[i // 4, i % 4, y] = share(k, 2 * i + y, 1 - core).astype(BF)
                return carry

            lax.fori_loop(0, 16, body, 0)
            send(k, 0)
        elif step == 1:
            arrived(k, 0)

            def body(i, carry):
                for y in range(2):
                    r0[i // 4, i % 4, y] = total([share(k, 2 * i + y, core), r0[i // 4, i % 4, y]]).astype(BF)
                return carry

            lax.fori_loop(0, 16, body, 0)
            send(k, 1)
            if k not in "co":
                send(k, 2)
        elif step == 2:
            arrived(k, 1)
            for y in range(2):
                second = (3, 1)[y]
                zb, xb = z_flip[second], x_flip[second]
                r0[zb, :, y, :, lo] = total([r0[zb, :, y, :, lo], buf("q1z", k)[y]]).astype(BF)
                r0[:, xb, y, :, hi] = total([r0[:, xb, y, :, hi], buf("q1x", k)[y]]).astype(BF)
            send(k, 3)
        elif step == 3:
            if k in "co":
                arrived(k, 1)
                r0[z, :, :, :, lo] = total([r0[z, :, :, :, lo]] + [buf("qz", k)[i] for i in range(3)]).astype(BF)
                r0[:, x, :, :, hi] = total([r0[:, x, :, :, hi]] + [buf("qx", k)[i] for i in range(3)]).astype(BF)
            else:
                arrived(k, 2)
                arrived(k, 3)
                for y in range(2):
                    r0[z, :, y, :, lo] = total(
                        [r0[z, :, y, :, lo], buf("q0z", k)[y], buf("q2z", k)[y]]
                    ).astype(BF)
                    r0[:, x, y, :, hi] = total(
                        [r0[:, x, y, :, hi], buf("q0x", k)[y], buf("q2x", k)[y]]
                    ).astype(BF)
            send(k, 4)
        else:
            arrived(k, 4)
            left = total([r0[z, x, yh, :, lo]] + [buf("px", k)[i] for i in range(7)])
            right = total([r0[z, x, yh, :, hi]] + [buf("pz", k)[i] for i in range(7)])
            mine = jnp.concatenate([left, right], axis=1)
            if k == "a":
                gdn_ref[0] = mine
                piece = s.wdn[pl.ds(dp * 32, 32), :].astype(F32)
                adn_ref[0] = AVG_DECAY * s.avd[...] + (1.0 - AVG_DECAY) * (piece - LEARN_RATE * mine)
            else:
                first = {"b": 2048, "c": 0, "o": 1536}[k]
                gin_ref[0, :, first : first + w] = mine[0:8]
                gin_ref[0, :, first + w : first + 2 * w] = mine[8:16]

    def code_copy(c):
        return pltpu.make_async_remote_copy(
            src_ref=s.fcs.at[c], dst_ref=s.fcr.at[c], send_sem=send_sems.at[N_SEM - 2 + c],
            recv_sem=recv_sems.at[N_SEM - 2 + c], device_id=sec_dev, device_id_type=MESH,
        )

    def grad_copy(c):
        return pltpu.make_async_remote_copy(
            src_ref=s.cxs.at[c], dst_ref=s.cxr.at[c], send_sem=send_sems.at[N_SEM - 4 + c],
            recv_sem=recv_sems.at[N_SEM - 4 + c], device_id=sec_dev, device_id_type=MESH,
        )

    @pl.when(is_e)
    def _():
        for c in range(2):
            grid_now = grids_ref[c]
            width = jnp.where(grid_now == 0, 16, jnp.where(grid_now == 1, 32, 8)).astype(I32)
            log_across = jnp.where(grid_now == 0, 1, jnp.where(grid_now == 1, 2, 0)).astype(I32)
            across_mask = jnp.where(grid_now == 0, 1, jnp.where(grid_now == 1, 3, 0)).astype(I32)
            window_no = rows_i >> 6
            inner = rows_i & 63
            source = (
                ((window_no >> log_across) * 8 + (inner >> 3)) * width
                + (window_no & across_mask) * 8
                + (inner & 7)
            )
            s.perm[c] = (source == cols_i).astype(F32).astype(BF)
        loads[0].wait()
        loads[1].wait()

        def forward(c, carry):
            @pl.when(c == 1)
            def _():
                loads[4].wait()

            raster = [s.xs[c, 0:GRID], s.xs[c, GRID:CLIP]]
            norm_qkv(c, [nn(s.perm[c], v) for v in raster])

            @pl.when(c == 0)
            def _():
                book_start()

            window_forward(c, 0)
            window_forward(c, 1)

            @pl.when(c == 0)
            def _():
                loads[2].wait()
                loads[3].wait()

            def put(acc):
                s.eb[c] = acc.astype(BF)

            feed_forward(c, put)
            vec = nt(proj_t, s.eb[c])
            hi = vec.astype(BF).astype(F32)
            mid = (vec - hi).astype(BF).astype(F32)
            parts = jnp.concatenate([hi, mid, vec - hi - mid, jnp.zeros((8, CLIP), F32)], axis=0).astype(BF)
            for f in range(2):
                cols = slice(GRID * f, GRID * f + GRID)
                moved = nn(parts[:, cols], s.perm[c])
                s.fcs[c, :, cols] = (moved[0:8] + moved[8:16]) + moved[16:24]
            code_copy(c).start()
            return carry

        lax.fori_loop(0, 2, forward, 0)

    @pl.when(is_d)
    def _():
        book_start()
        gather_book()
        for load in loads:
            load.wait()

        def both(c, carry):
            entries(c)
            code_copy(c).wait_recv()
            sent = (s.fcr[c] + s.ent[c, 0]).astype(BF).astype(F32)
            s.cvec[c] = pad16(sent + s.ent[c, 1])
            norm_qkv(c, [tn(s.cvec[c][0:8, 0:256], proj_t), tn(s.cvec[c][0:8, 256:512], proj_t)])
            frames_forward(c)

            def put(acc):
                s.bo[pl.ds(c * CLIP, CLIP), :] = acc.astype(BF)

            feed_forward(c, put)
            bout_copy(c).start()
            back_down(c)
            back_up(c, lambda: s.xs[c].astype(F32))
            frames_backward(c)
            s.eb[c] = back_in(c).astype(BF)
            s.cxs[c] = pad16(nt(proj_t, s.eb[c]))
            grad_copy(c).start()
            return carry

        lax.fori_loop(0, 2, both, 0)

        def downs(c, carry):
            grad_down(c)
            return carry

        lax.fori_loop(0, 2, downs, 0)
        reduce_step("a", 0)

        def ups(c, carry):
            grad_up(c)

            @pl.when(c == 0)
            def _():
                reduce_step("a", 1)

            return carry

        lax.fori_loop(0, 2, ups, 0)
        reduce_step("b", 0)

        def attns(c, carry):
            grad_out(c)
            grad_attn(c)

            @pl.when(c == 0)
            def _():
                reduce_step("a", 2)
                reduce_step("b", 1)

            return carry

        lax.fori_loop(0, 2, attns, 0)
        reduce_step("c", 0)
        reduce_step("o", 0)
        reduce_step("a", 3)
        book_proj_terms(0, s.cxs[0][0:8].astype(F32), s.eb[0], s.cvec[0][0:8].astype(F32))
        reduce_step("b", 2)
        reduce_step("c", 1)
        reduce_step("o", 1)
        book_proj_terms(1, s.cxs[1][0:8].astype(F32), s.eb[1], s.cvec[1][0:8].astype(F32))

    @pl.when(is_e)
    def _():
        def backward(c, carry):
            grad_copy(c).wait_recv()
            for f in range(2):
                cols = slice(GRID * f, GRID * f + GRID)
                s.cvec[c, :, cols] = nt(s.cxr[c, :, cols], s.perm[c]).astype(BF)
            g = tn(s.cvec[c][0:8], proj_t)
            s.hb[...] = g
            s.xs[c] = g.astype(BF)
            grad_down(c)

            @pl.when(c == 1)
            def _():
                reduce_step("a", 0)

            back_down(c)
            grad_up(c)

            @pl.when(c == 1)
            def _():
                reduce_step("b", 0)
                reduce_step("a", 1)

            back_up(c, lambda: s.hb[...])
            grad_out(c)

            @pl.when(c == 1)
            def _():
                reduce_step("o", 0)
                reduce_step("b", 1)
                reduce_step("a", 2)

            window_backward(c, 0)

            @pl.when(c == 1)
            def _():
                reduce_step("o", 1)

            window_backward(c, 1)

            @pl.when(c == 1)
            def _():
                reduce_step("b", 2)

            grad_attn(c)

            @pl.when(c == 1)
            def _():
                reduce_step("c", 0)
                reduce_step("a", 3)

            s.act[c, :, 0:D] = back_in(c).astype(BF)
            return carry

        lax.fori_loop(0, 2, backward, 0)
        reduce_step("c", 1)

        def leave(c, carry):
            for f in range(2):
                back = tn(s.perm[c], s.act[c, GRID * f : GRID * f + GRID, 0:D])
                s.bo[pl.ds(c * CLIP + GRID * f, GRID), :] = back.astype(BF)
            bout_copy(c).start()
            book_proj_terms(c, s.cxr[c][0:8].astype(F32), s.eb[c], s.cvec[c][0:8].astype(F32))
            return carry

        lax.fori_loop(0, 2, leave, 0)

    sums = jnp.concatenate(
        [
            jnp.sum(s.gacc[0], axis=0, keepdims=True),
            jnp.sum(s.gacc[1], axis=0, keepdims=True),
            jnp.zeros((6, D), F32),
        ],
        axis=0,
    )
    wide_sums = jnp.concatenate([jnp.zeros((72, D), F32), sums, jnp.zeros((48, D), F32)], axis=0)
    s.s_acc[...] += jnp.transpose(wide_sums).reshape(4, 8, 2, 8, 128)
    order = ["s0", "b3", "o3", "s1", "a4", "s2", "c3", "b4", "o4", "s3", "c4"]
    for load in averages:
        load.wait()
    for item in order:
        reduce_step(item[0], int(item[1]))

    half_rows = s.win[pl.ds(16 * (dp // 2), 16), :].astype(F32)
    piece = jnp.where(core == 0, half_rows[0:8], half_rows[8:16])
    ain_ref[0] = AVG_DECAY * s.avi[...] + (1.0 - AVG_DECAY) * (piece - LEARN_RATE * gin_ref[0])

    for c in range(2):
        bout_copy(c).wait()

        @pl.when(is_e)
        def _():
            code_copy(c).wait_send()

        @pl.when(is_d)
        def _():
            grad_copy(c).wait_send()

    book_finish()
    for k in ("a", "b", "c", "o", "s"):
        for step in {"s": (0, 1, 2), "c": (0, 1, 4), "o": (0, 1, 4)}.get(k, (0, 1, 2, 3, 4)):
            for cp in copies(k, step):
                cp.wait_send()


def body(
    boundary, in_weights, down_weight, gains, proj, codebook, codes, grids, orders, avg_in, avg_down
):
    vmem = pl.BlockSpec(memory_space=pltpu.VMEM)
    smem = pl.BlockSpec(memory_space=pltpu.SMEM)
    hbm = pl.BlockSpec(memory_space=pl.ANY)
    outs = (
        jax.ShapeDtypeStruct(boundary.shape, BF),
        jax.ShapeDtypeStruct(avg_in.shape, F32),
        jax.ShapeDtypeStruct(avg_down.shape, F32),
        jax.ShapeDtypeStruct((8, 128), F32),
        jax.ShapeDtypeStruct(avg_in.shape, F32),
        jax.ShapeDtypeStruct(avg_down.shape, F32),
    )
    scratch = [pltpu.VMEM(shape, dtype) for shape, dtype in SHAPES.values()]
    scratch += [pltpu.SemaphoreType.DMA((N_SEM,)), pltpu.SemaphoreType.DMA((N_SEM,)), pltpu.SemaphoreType.DMA((9,))]
    made = pl.pallas_call(
        mega,
        out_shape=outs,
        in_specs=[hbm, hbm, hbm, vmem, vmem, vmem, vmem, smem, smem, hbm, hbm],
        out_specs=[hbm] + [vmem] * 5,
        scratch_shapes=scratch,
        compiler_params=pltpu.CompilerParams(
            collective_id=0, has_side_effects=True, vmem_limit_bytes=63 << 20
        ),
        name="both_sections",
    )(
        boundary, in_weights, down_weight, gains, proj[0].T, codebook, codes.reshape(8, 128), grids, orders,
        avg_in, avg_down,
    )
    return pl.pallas_call(
        split_outputs,
        out_shape=(
            outs[0], outs[1], outs[2],
            jax.ShapeDtypeStruct((1, 2, 8), F32),
            jax.ShapeDtypeStruct((1, 8, 8), F32),
            jax.ShapeDtypeStruct(codebook.shape, F32),
            outs[4], outs[5],
        ),
        in_specs=[vmem] * 6,
        out_specs=[vmem] * 8,
        name="split_outputs",
    )(*made)


def split_outputs(
    bout_in, gin_in, gdn_in, small_in, ain_in, adn_in,
    bout, gin, gdn, ggain, gproj, gbook, ain, adn,
):
    bout[...] = bout_in[...]
    gin[...] = gin_in[...]
    gdn[...] = gdn_in[...]
    ain[...] = ain_in[...]
    adn[...] = adn_in[...]
    small = small_in[...]
    gbook[...] = small[:, 0:64]
    gproj[0] = small[:, 64:72]
    ggain[0] = jnp.transpose(jnp.concatenate([small] * 16, axis=0))[72:74, 0:8]


def solution(mesh):
    placed = (
        P("section", "dp", None),
        P("section", None, None),
        P("section", None, None),
        P("section", None, None),
        P("section", None, None),
        P(None, ("section", "dp")),
        P("dp"),
        P("dp"),
        P("dp", None),
        P("section", "dp", None),
        P("section", "dp", None),
    )
    return jax.shard_map(
        body,
        mesh=mesh,
        in_specs=placed,
        out_specs=(
            P("section", "dp", None),
            P("section", "dp", None),
            P("section", "dp", None),
            P("section", None, "dp"),
            P("section", "dp", None),
            P(None, ("section", "dp")),
            P("section", "dp", None),
            P("section", "dp", None),
        ),
        check_vma=False,
    )
```

```python
import functools

import jax
import jax.numpy as jnp
from jax import lax
from jax.experimental import pallas as pl
from jax.experimental.pallas import tpu as pltpu
from jax.sharding import PartitionSpec as P

BF = jnp.bfloat16
F32 = jnp.float32
I32 = jnp.int32
MESH = pl.DeviceIdType.MESH

D = 512
FF = 2048
CLIP = 512
GRID = 256
WINDOW = 64
HALF = 4096
NORM_EPS = 1e-05
AVG_DECAY = 0.9
LEARN_RATE = 0.0005
SCALE = 0.125
WB = 4

CHUNKS = {"a": (32, 512), "b": (16, 1024), "c": (16, 768), "o": (16, 256)}


def nn(left, right):
    return lax.dot_general(left, right, (((1,), (0,)), ((), ())), preferred_element_type=F32)


def nt(left, right):
    return lax.dot_general(left, right, (((1,), (1,)), ((), ())), preferred_element_type=F32)


def tn(left, right):
    return lax.dot_general(left, right, (((0,), (0,)), ((), ())), preferred_element_type=F32)


def tt(left, right):
    return lax.dot_general(left, right, (((0,), (1,)), ((), ())), preferred_element_type=F32)


def iota(shape, axis):
    return lax.broadcasted_iota(I32, shape, axis)


def normed(h):
    mean = jnp.mean(h, axis=-1, keepdims=True)
    c = h - mean
    var = jnp.mean(c * c, axis=-1, keepdims=True)
    r = lax.rsqrt(var + NORM_EPS)
    return c * r, r


def normed_back(grad, xhat, r, gain):
    t = grad * gain
    m1 = jnp.mean(t, axis=-1, keepdims=True)
    m2 = jnp.mean(t * xhat, axis=-1, keepdims=True)
    return r * (t - m1 - xhat * m2)


def gelu_pair(u):
    c0 = 0.7978845608028654
    c1 = 0.7978845608028654 * 0.044715
    m = c1 * (u * u)
    half = 0.5 + 0.5 * jnp.tanh(u * (c0 + m))
    value = u * half
    slope = half + (value - value * half) * (2.0 * c0 + 6.0 * m)
    return value, slope


def ten_shapes():
    shapes = {
        "xs": ((2, CLIP, D), BF),
        "win": ((D, 4 * D + FF), BF),
        "wdn": ((FF, D), BF),
        "perm": ((2, GRID, GRID), BF),
        "bd1": ((256, 256), BF),
        "bds": ((256, 256), BF),
        "bdf": ((256, 256), F32),
        "tbl": ((32, 16, 128), BF),
        "pre": ((2, 2, 8, 128), F32),
        "cds": ((2, 8, CLIP), I32),
        "cxs": ((2, 16, CLIP), BF),
        "cxr": ((2, 16, CLIP), BF),
        "fcs": ((2, 8, CLIP), F32),
        "fcr": ((2, 8, CLIP), F32),
        "ent": ((2, 2, 8, CLIP), F32),
        "cvec": ((2, 16, CLIP), BF),
        "hb": ((CLIP, D), F32),
        "bo": ((2 * CLIP, D), BF),
        "m8": ((16, FF), BF),
        "pgt": ((D, 128), F32),
        "q8": ((2, 8, 768), F32),
        "q0": ((8, 768), F32),
        "qs1": ((8, 768), F32),
        "qz": ((3, 8, 768), F32),
        "qs2": ((8, 768), F32),
        "qx": ((3, 8, 768), F32),
        "qs3": ((8, 768), F32),
        "qy": ((8, 768), F32),
        "qs4": ((8, 768), F32),
        "qg": ((8, 768), F32),
        "avi": ((8, 4 * D + FF), F32),
        "avd": ((32, D), F32),
        "gob": ((CLIP, D), BF),
        "xh1": ((2, CLIP, D), F32),
        "xh2": ((2, CLIP, D), F32),
        "r1": ((2, CLIP, 1), F32),
        "r2": ((2, CLIP, 1), F32),
        "a1": ((2, CLIP, D), BF),
        "a2": ((2, CLIP, D), BF),
        "qkv": ((2, CLIP, 3 * D), BF),
        "prob": ((2, CLIP, D), F32),
        "att": ((2, CLIP, D), BF),
        "act": ((2, CLIP, FF), BF),
        "gel": ((2, CLIP, FF), BF),
        "gy": ((2, CLIP, D), BF),
        "eb": ((2, CLIP, D), BF),
        "acc_dn": ((FF, D), F32),
        "acc_up": ((D, FF), F32),
        "acc_qkv": ((D, 3 * D), F32),
        "acc_out": ((D, D), F32),
        "s_acc": ((4, 8, 2, 8, 128), F32),
        "gacc": ((2, 8, D), F32),
        "s0": ((4, 8, 8, 128), F32),
        "s1": ((3, 8, 8, 128), F32),
        "s2": ((7, 8, 128), F32),
    }
    for k, (rows, w) in CHUNKS.items():
        h = w // 2
        shapes["sb0" + k] = ((4, 4, 2, rows, w), BF)
        shapes["r0" + k] = ((4, 4, 2, rows, w), BF)
        for ax in "zx":
            for slot in "012":
                shapes["q" + slot + ax + k] = ((2, 4, rows, h), BF)
            shapes["p" + ax + k] = ((7, rows, h), BF)
    return shapes


SHAPES = ten_shapes()
N_SEM = 200


class Refs:
    pass


def mega(
    x_hbm, win_hbm, wdn_hbm, gains_ref, proj_ref, book_ref, codes_ref, grids_ref, orders_ref,
    avgin_hbm, avgdn_hbm,
    bout_hbm, gin_ref, gdn_ref, small_ref, ain_ref, adn_ref,
    *scratch,
):
    s = Refs()
    for name, ref in zip(SHAPES, scratch):
        setattr(s, name, ref)
    send_sems, recv_sems, load_sems = scratch[len(SHAPES):]

    sec = lax.axis_index("section")
    dp = lax.axis_index("dp")
    core = dp % 2
    yh = (dp // 2) % 2
    x = (dp // 4) % 4
    z = dp // 16
    is_e = sec == 0
    is_d = sec == 1

    def place(zz, xx, yy, cc):
        return (sec, ((zz * 4 + xx) * 2 + yy) * 2 + cc)

    core_dev = place(z, x, yh, 1 - core)
    y_dev = place(z, x, 1 - yh, core)
    def flips(v):
        return {1: v + 1 - 2 * (v % 2), 2: (v + 2) % 4, 3: 3 - v}

    z_flip, x_flip = flips(z), flips(x)
    z_dev = [place((z + d) % 4, x, yh, core) for d in (1, 2, 3)]
    x_dev = [place(z, (x + d) % 4, yh, core) for d in (1, 2, 3)]
    sec_dev = (1 - sec, dp)
    sec_core_dev = (1 - sec, dp + 1 - 2 * core)
    around = [(d, y) for d in range(4) for y in range(2) if d + y > 0]
    zy_dev = [place((z + d) % 4, x, (yh + y) % 2, core) for d, y in around]
    xy_dev = [place(z, (x + d) % 4, (yh + y) % 2, core) for d, y in around]

    counter = [0]
    slots = {}

    def rcopy(key, src, dst, dev):
        if key not in slots:
            slots[key] = counter[0]
            counter[0] += 1
        i = slots[key]
        return pltpu.make_async_remote_copy(
            src_ref=src, dst_ref=dst, send_sem=send_sems.at[i], recv_sem=recv_sems.at[i],
            device_id=dev, device_id_type=MESH,
        )

    loads = [
        pltpu.make_async_copy(x_hbm.at[0, pl.ds(0, CLIP)], s.xs.at[0], load_sems.at[0]),
        pltpu.make_async_copy(win_hbm.at[0, :, pl.ds(0, 3 * D)], s.win.at[:, pl.ds(0, 3 * D)], load_sems.at[1]),
        pltpu.make_async_copy(
            win_hbm.at[0, :, pl.ds(3 * D, D + FF)], s.win.at[:, pl.ds(3 * D, D + FF)], load_sems.at[2]
        ),
        pltpu.make_async_copy(wdn_hbm.at[0], s.wdn, load_sems.at[3]),
        pltpu.make_async_copy(x_hbm.at[0, pl.ds(CLIP, CLIP)], s.xs.at[1], load_sems.at[4]),
    ]
    averages = [
        pltpu.make_async_copy(avgin_hbm.at[0], s.avi, load_sems.at[7]),
        pltpu.make_async_copy(avgdn_hbm.at[0], s.avd, load_sems.at[8]),
    ]
    for load in loads + averages:
        load.start()

    def bout_copy(c):
        rows = pl.ds(c * CLIP, CLIP)
        return pltpu.make_async_copy(s.bo.at[rows], bout_hbm.at[0, rows], load_sems.at[5 + c])

    barrier = pltpu.get_barrier_semaphore()
    far = [(i, j, y) for i in range(4) for j in range(4) for y in range(2) if i + j + y > 0]
    far_dev = [place((z + i) % 4, (x + j) % 4, (yh + y) % 2, core) for i, j, y in far]
    peers = [core_dev, sec_dev, sec_core_dev] + far_dev
    for dev in peers:
        pl.semaphore_signal(barrier, inc=1, device_id=dev, device_id_type=MESH)

    rows_i = iota((256, 256), 0)
    cols_i = iota((256, 256), 1)
    same = ((rows_i >> 6) == (cols_i >> 6)).astype(F32)
    s.bdf[...] = same * SCALE
    s.bd1[...] = same.astype(BF)
    s.bds[...] = (same * SCALE).astype(BF)
    for c in range(2):
        code_row = jnp.concatenate([codes_ref[4 * c + k : 4 * c + k + 1, :] for k in range(4)], axis=1)
        s.cds[c] = jnp.broadcast_to(code_row, (8, CLIP))

    proj_t = proj_ref[...]
    gain_one = gains_ref[0, 0:1, :].astype(F32)
    gain_two = gains_ref[0, 1:2, :].astype(F32)
    book = book_ref[...].astype(F32)
    empty = jnp.zeros((8, 64), F32)
    s.pre[sec, core] = jnp.where(
        is_e, jnp.concatenate([book, empty], axis=1), jnp.concatenate([empty, book], axis=1)
    )
    s.gacc[...] = jnp.zeros((2, 8, D), F32)
    s.s_acc[...] = jnp.zeros((4, 8, 2, 8, 128), F32)

    def book_start():
        pl.semaphore_wait(barrier, len(peers))
        mine = s.pre.at[sec, core]

        @pl.when(is_e)
        def _():
            rcopy("ag0", mine, mine, sec_dev).start()
            rcopy("ag1", mine, mine, sec_core_dev).start()

        @pl.when(is_d)
        def _():
            rcopy("ag2", mine, mine, core_dev).start()

    def gather_book_start():
        chip = dp // 2
        rcopy("ag0", s.pre.at[0, core], s.pre.at[0, core], sec_dev).wait_recv()
        rcopy("ag1", s.pre.at[0, 1 - core], s.pre.at[0, 1 - core], sec_core_dev).wait_recv()
        rcopy("ag2", s.pre.at[1, 1 - core], s.pre.at[1, 1 - core], core_dev).wait_recv()
        s.tbl[chip] = jnp.concatenate([s.pre[0, 0] + s.pre[1, 0], s.pre[0, 1] + s.pre[1, 1]], axis=0).astype(BF)
        part = s.tbl.at[chip]
        for n in range(31):
            rcopy("ag3%d" % n, part, part, far_dev[n]).start()

    def gather_book_wait():
        for n, (i, j, y) in enumerate(far):
            part = s.tbl.at[(((z + 4 - i) % 4) * 4 + (x + 4 - j) % 4) * 2 + (yh + 2 - y) % 2]
            rcopy("ag3%d" % n, part, part, far_dev[n]).wait_recv()

    def book_finish():
        mine = s.pre.at[sec, core]

        @pl.when(is_e)
        def _():
            rcopy("ag0", mine, mine, sec_dev).wait_send()
            rcopy("ag1", mine, mine, sec_core_dev).wait_send()

        @pl.when(is_d)
        def _():
            rcopy("ag2", mine, mine, core_dev).wait_send()
            part = s.tbl.at[dp // 2]
            for n in range(31):
                rcopy("ag3%d" % n, part, part, far_dev[n]).wait_send()

    def onehots(c, half, shift):
        code_row = s.cds[c][0:1, :] - half * HALF
        hi = code_row >> 6
        lo = code_row & 63
        lo_one = (iota((128, CLIP), 0) == lo + shift).astype(F32).astype(BF)
        hi_mask = (iota((CLIP, CLIP), 0) >> 3) == hi
        return lo_one, hi_mask

    def entries(c):
        for half in range(2):
            lo_one, hi_mask = onehots(c, half, 64 * half)
            table = s.tbl[...].reshape(CLIP, 128)
            picked = jnp.where(hi_mask, nn(table, lo_one), 0.0)
            s.ent[c, half] = jnp.sum(picked.reshape(64, 8, CLIP), axis=0)

    def total(parts):
        parts = [v.astype(F32) for v in parts]
        while len(parts) > 1:
            parts = [a + b for a, b in zip(parts[::2], parts[1::2])] + parts[len(parts) // 2 * 2 :]
        return parts[0]

    def pad16(v):
        return jnp.concatenate([v, jnp.zeros((8, v.shape[1]), F32)], axis=0).astype(BF)

    def book_proj_terms(c, code_grad, wide_rows, narrow):
        lo_one, hi_mask = onehots(c, sec, 0)
        spread = jnp.broadcast_to(code_grad[None], (64, 8, CLIP)).reshape(CLIP, CLIP)
        left = jnp.where(hi_mask, spread, 0.0).astype(BF)
        total = nt(left, lo_one)
        narrow_wide = jnp.concatenate(
            [jnp.zeros((64, CLIP), F32), narrow, jnp.zeros((56, CLIP), F32)], axis=0
        ).astype(BF)
        total = total + tt(wide_rows, narrow_wide)
        s.s_acc[...] += total.reshape(4, 8, 2, 8, 128)

    def norm_qkv(c, parts):
        halves = [slice(0, 256), slice(256, 512)]
        a = []
        for rows, h in zip(halves, parts):
            s.hb[rows] = h
            xh, r = normed(h)
            s.xh1[c, rows] = xh
            s.r1[c, rows] = r
            a.append((xh * gain_one).astype(BF))
            s.a1[c, rows] = a[-1]
        for j in range(3):
            for rows, v in zip(halves, a):
                s.qkv[c, rows, 512 * j : 512 * j + 512] = nn(v, s.win[:, 512 * j : 512 * j + 512]).astype(BF)

    def feed_forward(c, put, ahead=False):
        m = s.hb[...] + nn(s.att[c], s.win[:, 1536:2048])
        xh, r = normed(m)
        s.xh2[c] = xh
        s.r2[c] = r
        a = (xh * gain_two).astype(BF)
        s.a2[c] = a
        acc = m
        nxt = nn(a, s.win[:, 2048:2304])
        for j in range(8):
            cols = slice(256 * j, 256 * j + 256)
            u = nxt
            if j < 7:
                nxt = nn(a, s.win[:, 2304 + 256 * j : 2560 + 256 * j])
            value, slope = gelu_pair(u.astype(BF))
            s.act[c, :, cols] = value
            s.gel[c, :, cols] = s.gel[c, :, cols] * slope if ahead else slope
            acc = acc + nn(value, s.wdn[cols, :])
        put(acc)

    def units(c, w, count):
        out = []
        for n in range(count):
            rows = pl.ds((w * count + n) * WINDOW, WINDOW)
            for quad in range(2):
                out.append((rows, 256 * quad))
        return out

    def widened(v, mask):
        return jnp.concatenate([v] * 4, axis=0) * mask

    def heads_of(wide):
        return (wide[0:64] + wide[64:128]) + (wide[128:192] + wide[192:256])

    def window_forward(c, w):
        if True:
            us = units(c, w, WB)
            bds = s.bds[...]
            bdf = s.bdf[...]
            q = [s.qkv[c, r, o : o + 256] for r, o in us]
            k = [s.qkv[c, r, 512 + o : 768 + o] for r, o in us]
            v = [s.qkv[c, r, 1024 + o : 1280 + o] for r, o in us]
            scores = [nt(kk, widened(qq, bds)) for kk, qq in zip(k, q)]
            e = [jnp.exp(x - jnp.max(x, axis=0, keepdims=True)) for x in scores]
            p = [x * (1.0 / jnp.sum(x, axis=0, keepdims=True)) for x in e]
            wide = [tn(x.astype(BF), vv) for x, vv in zip(p, v)]
            att = [(heads_of(x * bdf) * (1.0 / SCALE)).astype(BF) for x in wide]
            for (r, o), pp, aa in zip(us, p, att):
                s.prob[c, r, o : o + 256] = pp
                s.att[c, r, o : o + 256] = aa

    def window_backward(c, w):
        if True:
            us = units(c, w, WB)
            bds = s.bds[...]
            bd1 = s.bd1[...]
            bdf = s.bdf[...]
            q = [s.qkv[c, r, o : o + 256] for r, o in us]
            k = [s.qkv[c, r, 512 + o : 768 + o] for r, o in us]
            v = [s.qkv[c, r, 1024 + o : 1280 + o] for r, o in us]
            go = [widened(s.gob[r, o : o + 256], bd1) for r, o in us]
            p = [s.prob[c, r, o : o + 256] for r, o in us]
            gp = [nt(vv, gg) for vv, gg in zip(v, go)]
            gv = [nn(pp.astype(BF), gg).astype(BF) for pp, gg in zip(p, go)]
            gs = [
                (pp * (x - jnp.sum(x * pp, axis=0, keepdims=True))).astype(BF)
                for pp, x in zip(p, gp)
            ]
            gk = [nn(x, widened(qq, bds)).astype(BF) for x, qq in zip(gs, q)]
            gq = [heads_of(tn(x, kk) * bdf).astype(BF) for x, kk in zip(gs, k)]
            for (r, o), a, b, d in zip(us, gq, gk, gv):
                s.qkv[c, r, o : o + 256] = a
                s.qkv[c, r, 512 + o : 768 + o] = b
                s.qkv[c, r, 1024 + o : 1280 + o] = d

    def head_sums(v):
        return nn(v, s.bd1[...])

    CR = 256

    def frames_forward(c):
        late0 = orders_ref[c, 0] > orders_ref[c, 1]
        sign = jnp.where(late0, 1.0, -1.0).astype(F32)
        r0 = slice(0, GRID)
        r1 = slice(GRID, CLIP)
        for quad in range(2):
            qc = slice(256 * quad, 256 * quad + 256)
            kc = slice(512 + 256 * quad, 768 + 256 * quad)
            vc = slice(1024 + 256 * quad, 1280 + 256 * quad)
            q_late = jnp.where(late0, s.qkv[c, r0, qc], s.qkv[c, r1, qc])
            k_diff = s.qkv[c, r1, kc] - s.qkv[c, r0, kc]
            v0 = s.qkv[c, r0, vc]
            v1 = s.qkv[c, r1, vc]
            d = head_sums(q_late * k_diff) * (sign * SCALE)
            e = jnp.exp(-jnp.abs(d))
            big = 1.0 / (1.0 + e)
            small = e * big
            p_other = jnp.where(d > 0.0, big, small)
            p_self = jnp.where(d > 0.0, small, big)
            s.prob[c, r0, qc] = p_other
            s.prob[c, r1, qc] = p_self
            p0 = jnp.where(late0, p_self, p_other).astype(BF)
            p1 = jnp.where(late0, p_other, p_self).astype(BF)
            mix = (p0.astype(F32) * v0.astype(F32) + p1.astype(F32) * v1.astype(F32)).astype(BF)
            s.att[c, r0, qc] = jnp.where(late0, mix, v0)
            s.att[c, r1, qc] = jnp.where(late0, v1, mix)

    def frames_backward(c):
        late0 = orders_ref[c, 0] > orders_ref[c, 1]
        r0 = slice(0, GRID)
        r1 = slice(GRID, CLIP)
        for quad in range(2):
            qc = slice(256 * quad, 256 * quad + 256)
            kc = slice(512 + 256 * quad, 768 + 256 * quad)
            vc = slice(1024 + 256 * quad, 1280 + 256 * quad)
            q_late = jnp.where(late0, s.qkv[c, r0, qc], s.qkv[c, r1, qc])
            k_diff = s.qkv[c, r1, kc] - s.qkv[c, r0, kc]
            v_diff = s.qkv[c, r1, vc] - s.qkv[c, r0, vc]
            go0 = s.gob[r0, qc]
            go1 = s.gob[r1, qc]
            go_late = jnp.where(late0, go0, go1)
            go_early = jnp.where(late0, go1, go0)
            p_other = s.prob[c, r0, qc]
            p_self = s.prob[c, r1, qc]
            gs = (p_other * p_self * head_sums(go_late * v_diff)).astype(BF).astype(F32) * SCALE
            gq = (gs * k_diff.astype(F32)).astype(BF)
            gk = gs * q_late.astype(F32)
            late32 = go_late.astype(F32)
            gv_late = (p_self.astype(BF).astype(F32) * late32).astype(BF)
            gv_early = (go_early.astype(F32) + p_other.astype(BF).astype(F32) * late32).astype(BF)
            none = jnp.zeros_like(gq)
            s.qkv[c, r0, qc] = jnp.where(late0, gq, none)
            s.qkv[c, r1, qc] = jnp.where(late0, none, gq)
            s.qkv[c, r0, kc] = (-gk).astype(BF)
            s.qkv[c, r1, kc] = gk.astype(BF)
            s.qkv[c, r0, vc] = jnp.where(late0, gv_late, gv_early)
            s.qkv[c, r1, vc] = jnp.where(late0, gv_early, gv_late)

    def gain_terms(which, grad, xhat):
        part = jnp.sum((grad * xhat).reshape(-1, 8, D), axis=0)
        s.gacc[which] += part

    def back_down_codes(c):
        twice = jnp.concatenate([s.cvec[c][0:8].astype(F32)] * 2, axis=0).astype(BF)
        for j in range(4):
            cols = slice(512 * j, 512 * j + 512)
            s.gel[c, :, cols] = (tn(twice, s.m8[:, cols]) * s.gel[c, :, cols].astype(F32)).astype(BF)

    def back_up(c, grad_of):
        acc = None
        for j in range(4):
            term = nt(s.gel[c, :, 512 * j : 512 * j + 512], s.win[:, 2048 + 512 * j : 2560 + 512 * j])
            acc = term if acc is None else acc + term
        xh = s.xh2[c]
        gain_terms(1, acc, xh)
        gm = grad_of() + normed_back(acc, xh, s.r2[c], gain_two)
        s.hb[...] = gm
        gy = gm.astype(BF)
        s.gy[c] = gy
        s.gob[...] = nt(gy, s.win[:, 1536:2048]).astype(BF)

    def back_in(c):
        acc = None
        for j in range(3):
            cols = slice(512 * j, 512 * j + 512)
            term = nt(s.qkv[c, :, cols], s.win[:, cols])
            acc = term if acc is None else acc + term
        xh = s.xh1[c]
        gain_terms(0, acc, xh)
        return s.hb[...] + normed_back(acc, xh, s.r1[c], gain_one)

    def add_into(ref, rows, cols, c, value):
        ref[rows, cols] = jnp.where(c == 0, value, ref[rows, cols] + value)

    def grad_down(c):
        for j in range(4):
            cols = slice(512 * j, 512 * j + 512)
            add_into(s.acc_dn, cols, slice(None), c, tn(s.act[c, :, cols], s.xs[c]))

    def grad_down_codes(c):
        code = s.cvec[c][0:8].astype(F32)
        wide = jnp.concatenate([jnp.zeros((80, CLIP), F32)] + [code] * 4 + [jnp.zeros((16, CLIP), F32)], axis=0)
        wide = wide.astype(BF)
        lanes = (iota((8, 128), 1) >> 3) - 10
        for j in range(4):
            v = tt(s.act[c, :, 512 * j : 512 * j + 512], wide).reshape(16, 4, 8, 128)
            picked = [jnp.where(lanes == m, v[:, m], 0.0) for m in range(4)]
            s.s_acc[j] += total(picked).reshape(8, 2, 8, 128)

    def grad_qkv_codes(c):
        norm_row = jnp.transpose(jnp.broadcast_to(s.r1[c], (CLIP, 128)))[0:1, :]
        part = nn(pad16(s.cvec[c][0:8].astype(F32) * norm_row), s.qkv[c])[0:8]
        for half in range(2):
            v = part[:, 768 * half : 768 * half + 768]
            s.q8[half] = jnp.where(c == 0, v, s.q8[half] + v)

    def grad_up(c):
        for j in range(4):
            cols = slice(512 * j, 512 * j + 512)
            add_into(s.acc_up, slice(None), cols, c, tn(s.a2[c], s.gel[c, :, cols]))

    def grad_out(c):
        add_into(s.acc_out, slice(None), slice(None), c, tn(s.att[c], s.gy[c]))

    def grad_attn(c):
        for j in range(3):
            cols = slice(512 * j, 512 * j + 512)
            add_into(s.acc_qkv, slice(None), cols, c, tn(s.a1[c], s.qkv[c, :, cols]))

    def share(k, i, to_core):
        n = 2 * i + to_core
        if k == "a":
            return s.acc_dn[pl.ds(pl.multiple_of(n * 32, 32), 32), :]
        rows = pl.ds(pl.multiple_of(n * 8, 8), 8)
        ref, w = {"b": (s.acc_up, 1024), "c": (s.acc_qkv, 768), "o": (s.acc_out, 256)}[k]
        return jnp.concatenate([ref[rows, 0:w], ref[rows, w : 2 * w]], axis=0)

    def buf(name, k):
        return getattr(s, name + k)

    def copies(k, step):
        if k == "s":
            if step == 0:
                return [rcopy("s0", s.s_acc.at[:, :, 1 - core], s.s0, core_dev)]
            if step == 1:
                return [rcopy("s1%d" % i, s.s0.at[(z + 1 + i) % 4], s.s1.at[i], z_dev[i]) for i in range(3)]
            return [
                rcopy(
                    "s2%d" % i, s.s0.at[z, 2 * ((x + d) % 4) + (yh + y) % 2], s.s2.at[i], xy_dev[i]
                )
                for i, (d, y) in enumerate(around)
            ]
        if k == "q":
            if step == 0:
                return [rcopy("q0", s.q8.at[1 - core], s.q0, core_dev)]
            if step == 1:
                return [rcopy("q1%d" % i, s.qs1, s.qz.at[i], z_dev[i]) for i in range(3)]
            if step == 2:
                return [rcopy("q2%d" % i, s.qs2, s.qx.at[i], x_dev[i]) for i in range(3)]
            if step == 3:
                return [rcopy("q3", s.qs3, s.qy, y_dev)]
            return [rcopy("q4", s.qs4, s.qg, core_dev)]
        rows, w = CHUNKS[k]
        h = w // 2
        r0 = buf("r0", k)
        if step == 0:
            return [rcopy(k + "0", buf("sb0", k), r0, core_dev)]
        lo, hi = pl.ds(0, h), pl.ds(h, h)
        out = []
        if step == 4:
            for i, (d, y) in enumerate(around):
                out.append(
                    rcopy(
                        "%s4x%d" % (k, i), r0.at[z, (x + d) % 4, (yh + y) % 2, :, lo],
                        buf("px", k).at[i], xy_dev[i],
                    )
                )
                out.append(
                    rcopy(
                        "%s4z%d" % (k, i), r0.at[(z + d) % 4, x, (yh + y) % 2, :, hi],
                        buf("pz", k).at[i], zy_dev[i],
                    )
                )
            return out
        for y in range(2):
            first, second = ((1, 3), (3, 1))[y]
            hop = second if step == 3 else first
            block = {1: 2, 2: first, 3: second}[step]
            slot = {1: "q1", 2: "q0", 3: "q2"}[step]
            out.append(
                rcopy(
                    "%s%dz%d" % (k, step, y), r0.at[z_flip[block], :, y, :, lo],
                    buf(slot + "z", k).at[y], place(z_flip[hop], x, yh, core),
                )
            )
            out.append(
                rcopy(
                    "%s%dx%d" % (k, step, y), r0.at[:, x_flip[block], y, :, hi],
                    buf(slot + "x", k).at[y], place(z, x_flip[hop], yh, core),
                )
            )
        return out

    def arrived(k, step):
        for cp in copies(k, step):
            cp.wait_recv()

    def send(k, step):
        for cp in copies(k, step):
            cp.start()

    def put_down(mine):
        gdn_ref[0] = mine
        piece = s.wdn[pl.ds(dp * 32, 32), :].astype(F32)
        adn_ref[0] = AVG_DECAY * s.avd[...] + (1.0 - AVG_DECAY) * (piece - LEARN_RATE * mine)

    def reduce_step(k, step):
        if k == "s":
            if step > 0:
                arrived(k, step - 1)
            if step == 1:
                s.s0[...] += s.s_acc[:, :, core]
            elif step == 2:
                s.s0[z] += (s.s1[0] + s.s1[1]) + s.s1[2]
            elif step == 3:
                small = total([s.s0[z, 2 * x + yh]] + [s.s2[i] for i in range(7)])
                small_ref[...] = small

                @pl.when(is_e)
                def _():
                    narrow = proj_t.astype(F32)
                    shares = [
                        total([small[:, n : n + 1] * narrow[n % 8 : n % 8 + 1, :] for n in range(80 + 8 * m, 88 + 8 * m)])
                        for m in range(4)
                    ]
                    put_down(jnp.concatenate(shares, axis=0))

                return
            send(k, step)
            return
        if k == "q":
            if step > 0:
                arrived(k, step - 1)
            if step == 1:
                s.qs1[...] = s.q8[core] + s.q0[...]
            elif step == 2:
                s.qs2[...] = total([s.qs1[...]] + [s.qz[i] for i in range(3)])
            elif step == 3:
                s.qs3[...] = total([s.qs2[...]] + [s.qx[i] for i in range(3)])
            elif step == 4:
                s.qs4[...] = s.qs3[...] + s.qy[...]
            elif step == 5:
                mine, other = s.qs4[...], s.qg[...]
                narrow = s.pgt[pl.ds(pl.multiple_of(dp * 8, 8), 8), :]
                for half, v in enumerate((jnp.where(core == 0, mine, other), jnp.where(core == 0, other, mine))):
                    gin_ref[0, :, 768 * half : 768 * half + 768] = total(
                        [narrow[:, n : n + 1] * v[n : n + 1, :] for n in range(8)]
                    )
                return
            send(k, step)
            return
        rows, w = CHUNKS[k]
        h = w // 2
        r0 = buf("r0", k)
        lo, hi = pl.ds(0, h), pl.ds(h, h)
        if step == 0:
            sb0 = buf("sb0", k)

            def body(i, carry):
                for y in range(2):
                    sb0[i // 4, i % 4, y] = share(k, 2 * i + y, 1 - core).astype(BF)
                return carry

            lax.fori_loop(0, 16, body, 0)
            send(k, 0)
        elif step == 1:
            arrived(k, 0)

            def body(i, carry):
                for y in range(2):
                    r0[i // 4, i % 4, y] = total([share(k, 2 * i + y, core), r0[i // 4, i % 4, y]]).astype(BF)
                return carry

            lax.fori_loop(0, 16, body, 0)
            send(k, 1)
            send(k, 2)
        elif step == 2:
            arrived(k, 1)
            for y in range(2):
                second = (3, 1)[y]
                zb, xb = z_flip[second], x_flip[second]
                r0[zb, :, y, :, lo] = total([r0[zb, :, y, :, lo], buf("q1z", k)[y]]).astype(BF)
                r0[:, xb, y, :, hi] = total([r0[:, xb, y, :, hi], buf("q1x", k)[y]]).astype(BF)
            send(k, 3)
        elif step == 3:
            arrived(k, 2)
            arrived(k, 3)
            for y in range(2):
                r0[z, :, y, :, lo] = total(
                    [r0[z, :, y, :, lo], buf("q0z", k)[y], buf("q2z", k)[y]]
                ).astype(BF)
                r0[:, x, y, :, hi] = total(
                    [r0[:, x, y, :, hi], buf("q0x", k)[y], buf("q2x", k)[y]]
                ).astype(BF)
            send(k, 4)
        else:
            arrived(k, 4)
            left = total([r0[z, x, yh, :, lo]] + [buf("px", k)[i] for i in range(7)])
            right = total([r0[z, x, yh, :, hi]] + [buf("pz", k)[i] for i in range(7)])
            mine = jnp.concatenate([left, right], axis=1)
            if k == "a":
                put_down(mine)
            else:
                first = {"b": 2048, "c": 0, "o": 1536}[k]
                gin_ref[0, :, first : first + w] = mine[0:8]
                gin_ref[0, :, first + w : first + 2 * w] = mine[8:16]

    def add_gains():
        sums = jnp.concatenate(
            [
                jnp.sum(s.gacc[0], axis=0, keepdims=True),
                jnp.sum(s.gacc[1], axis=0, keepdims=True),
                jnp.zeros((6, D), F32),
            ],
            axis=0,
        )
        wide_sums = jnp.concatenate([jnp.zeros((72, D), F32), sums, jnp.zeros((48, D), F32)], axis=0)
        s.s_acc[...] += jnp.transpose(wide_sums).reshape(4, 8, 2, 8, 128)

    def code_copy(c):
        return pltpu.make_async_remote_copy(
            src_ref=s.fcs.at[c], dst_ref=s.fcr.at[c], send_sem=send_sems.at[N_SEM - 2 + c],
            recv_sem=recv_sems.at[N_SEM - 2 + c], device_id=sec_dev, device_id_type=MESH,
        )

    def grad_copy(c):
        return pltpu.make_async_remote_copy(
            src_ref=s.cxs.at[c], dst_ref=s.cxr.at[c], send_sem=send_sems.at[N_SEM - 4 + c],
            recv_sem=recv_sems.at[N_SEM - 4 + c], device_id=sec_dev, device_id_type=MESH,
        )

    @pl.when(is_e)
    def _():
        for c in range(2):
            grid_now = grids_ref[c]
            width = jnp.where(grid_now == 0, 16, jnp.where(grid_now == 1, 32, 8)).astype(I32)
            log_across = jnp.where(grid_now == 0, 1, jnp.where(grid_now == 1, 2, 0)).astype(I32)
            across_mask = jnp.where(grid_now == 0, 1, jnp.where(grid_now == 1, 3, 0)).astype(I32)
            window_no = rows_i >> 6
            inner = rows_i & 63
            source = (
                ((window_no >> log_across) * 8 + (inner >> 3)) * width
                + (window_no & across_mask) * 8
                + (inner & 7)
            )
            s.perm[c] = (source == cols_i).astype(F32).astype(BF)
        loads[0].wait()
        loads[1].wait()

        def forward(c, carry):
            @pl.when(c == 1)
            def _():
                loads[4].wait()

            raster = [s.xs[c, 0:GRID], s.xs[c, GRID:CLIP]]
            norm_qkv(c, [nn(s.perm[c], v) for v in raster])

            @pl.when(c == 0)
            def _():
                book_start()

            window_forward(c, 0)
            window_forward(c, 1)

            @pl.when(c == 0)
            def _():
                loads[2].wait()
                loads[3].wait()

            def put(acc):
                s.eb[c] = acc.astype(BF)

            feed_forward(c, put)
            vec = nt(proj_t, s.eb[c])
            hi = vec.astype(BF).astype(F32)
            mid = (vec - hi).astype(BF).astype(F32)
            parts = jnp.concatenate([hi, mid, vec - hi - mid, jnp.zeros((8, CLIP), F32)], axis=0).astype(BF)
            for f in range(2):
                cols = slice(GRID * f, GRID * f + GRID)
                moved = nn(parts[:, cols], s.perm[c])
                s.fcs[c, :, cols] = (moved[0:8] + moved[8:16]) + moved[16:24]
            code_copy(c).start()
            return carry

        lax.fori_loop(0, 2, forward, 0)
        for j in range(4):
            cols = slice(512 * j, 512 * j + 512)
            m = nt(proj_t, s.wdn[cols, :])
            hi = m.astype(BF).astype(F32)
            s.m8[:, cols] = jnp.concatenate([hi, m - hi], axis=0).astype(BF)

    @pl.when(is_d)
    def _():
        book_start()
        gather_book_start()
        for load in loads:
            load.wait()

        def ahead(c, carry):
            for j in range(4):
                cols = slice(512 * j, 512 * j + 512)
                s.gel[c, :, cols] = nt(s.xs[c], s.wdn[cols, :]).astype(BF)
            return carry

        lax.fori_loop(0, 2, ahead, 0)
        narrow = proj_t.astype(F32)
        narrow = (narrow - jnp.mean(narrow, axis=-1, keepdims=True)) * gain_one
        s.pgt[...] = jnp.transpose(jnp.concatenate([narrow, jnp.zeros((120, D), F32)], axis=0))
        gather_book_wait()

        def both(c, carry):
            entries(c)
            code_copy(c).wait_recv()
            sent = (s.fcr[c] + s.ent[c, 0]).astype(BF).astype(F32)
            s.cvec[c] = pad16(sent + s.ent[c, 1])
            norm_qkv(c, [tn(s.cvec[c][0:8, 0:256], proj_t), tn(s.cvec[c][0:8, 256:512], proj_t)])
            frames_forward(c)

            def put(acc):
                s.bo[pl.ds(c * CLIP, CLIP), :] = acc.astype(BF)

            feed_forward(c, put, ahead=True)
            bout_copy(c).start()
            back_up(c, lambda: s.xs[c].astype(F32))
            frames_backward(c)
            s.eb[c] = back_in(c).astype(BF)
            s.cxs[c] = pad16(nt(proj_t, s.eb[c]))
            grad_copy(c).start()
            return carry

        lax.fori_loop(0, 2, both, 0)

        def downs(c, carry):
            grad_down(c)
            return carry

        def ups(c, carry):
            grad_up(c)
            return carry

        def outs(c, carry):
            grad_out(c)
            return carry

        def codes_of(c, carry):
            grad_qkv_codes(c)
            return carry

        def books(c):
            book_proj_terms(c, s.cxs[c][0:8].astype(F32), s.eb[c], s.cvec[c][0:8].astype(F32))

        lax.fori_loop(0, 2, downs, 0)
        reduce_step("a", 0)
        lax.fori_loop(0, 2, ups, 0)
        reduce_step("b", 0)
        reduce_step("a", 1)
        lax.fori_loop(0, 2, outs, 0)
        reduce_step("o", 0)
        books(0)
        reduce_step("o", 1)
        reduce_step("b", 1)
        books(1)
        reduce_step("a", 2)
        add_gains()
        lax.fori_loop(0, 2, codes_of, 0)
        for load in averages:
            load.wait()
        for item in ["q0", "s0", "q1", "b2", "o2", "a3", "s1", "q2", "b3", "o3", "s2", "q3", "a4", "q4", "o4", "s3", "b4", "q5"]:
            reduce_step(item[0], int(item[1]))

    @pl.when(is_e)
    def _():
        def backward(c, carry):
            grad_copy(c).wait_recv()
            for f in range(2):
                cols = slice(GRID * f, GRID * f + GRID)
                s.cvec[c, :, cols] = nt(s.cxr[c, :, cols], s.perm[c]).astype(BF)
            g = tn(s.cvec[c][0:8], proj_t)
            s.hb[...] = g
            back_down_codes(c)
            grad_up(c)

            @pl.when(c == 1)
            def _():
                reduce_step("b", 0)

            back_up(c, lambda: s.hb[...])
            window_backward(c, 0)

            @pl.when(c == 1)
            def _():
                reduce_step("b", 1)

            window_backward(c, 1)
            grad_attn(c)

            @pl.when(c == 1)
            def _():
                reduce_step("c", 0)
                reduce_step("b", 2)

            grad_out(c)

            @pl.when(c == 1)
            def _():
                reduce_step("o", 0)
                reduce_step("c", 1)

            s.a2[c] = back_in(c).astype(BF)
            return carry

        lax.fori_loop(0, 2, backward, 0)
        reduce_step("o", 1)

        def leave(c, carry):
            for f in range(2):
                back = tn(s.perm[c], s.a2[c, GRID * f : GRID * f + GRID])
                s.bo[pl.ds(c * CLIP + GRID * f, GRID), :] = back.astype(BF)
            bout_copy(c).start()
            book_proj_terms(c, s.cxr[c][0:8].astype(F32), s.eb[c], s.cvec[c][0:8].astype(F32))
            return carry

        lax.fori_loop(0, 2, leave, 0)
        reduce_step("c", 2)
        reduce_step("b", 3)

        def downs(c, carry):
            grad_down_codes(c)
            return carry

        lax.fori_loop(0, 2, downs, 0)
        add_gains()
        for load in averages:
            load.wait()
        for item in ["o2", "s0", "s1", "c3", "o3", "s2", "c4", "b4", "o4", "s3"]:
            reduce_step(item[0], int(item[1]))

    half_rows = s.win[pl.ds(16 * (dp // 2), 16), :].astype(F32)
    piece = jnp.where(core == 0, half_rows[0:8], half_rows[8:16])
    ain_ref[0] = AVG_DECAY * s.avi[...] + (1.0 - AVG_DECAY) * (piece - LEARN_RATE * gin_ref[0])

    for c in range(2):
        bout_copy(c).wait()

        @pl.when(is_e)
        def _():
            code_copy(c).wait_send()

        @pl.when(is_d)
        def _():
            grad_copy(c).wait_send()

    book_finish()
    def finish(chunks):
        for k in chunks:
            for step in {"s": (0, 1, 2)}.get(k, (0, 1, 2, 3, 4)):
                for cp in copies(k, step):
                    cp.wait_send()

    @pl.when(is_e)
    def _():
        finish("bcos")

    @pl.when(is_d)
    def _():
        finish("abosq")


def body(
    boundary, in_weights, down_weight, gains, proj, codebook, codes, grids, orders, avg_in, avg_down
):
    vmem = pl.BlockSpec(memory_space=pltpu.VMEM)
    smem = pl.BlockSpec(memory_space=pltpu.SMEM)
    hbm = pl.BlockSpec(memory_space=pl.ANY)
    outs = (
        jax.ShapeDtypeStruct(boundary.shape, BF),
        jax.ShapeDtypeStruct(avg_in.shape, F32),
        jax.ShapeDtypeStruct(avg_down.shape, F32),
        jax.ShapeDtypeStruct((8, 128), F32),
        jax.ShapeDtypeStruct(avg_in.shape, F32),
        jax.ShapeDtypeStruct(avg_down.shape, F32),
    )
    scratch = [pltpu.VMEM(shape, dtype) for shape, dtype in SHAPES.values()]
    scratch += [pltpu.SemaphoreType.DMA((N_SEM,)), pltpu.SemaphoreType.DMA((N_SEM,)), pltpu.SemaphoreType.DMA((9,))]
    made = pl.pallas_call(
        mega,
        out_shape=outs,
        in_specs=[hbm, hbm, hbm, vmem, vmem, vmem, vmem, smem, smem, hbm, hbm],
        out_specs=[hbm] + [vmem] * 5,
        scratch_shapes=scratch,
        compiler_params=pltpu.CompilerParams(
            collective_id=0, has_side_effects=True, vmem_limit_bytes=63 << 20
        ),
        name="both_sections",
    )(
        boundary, in_weights, down_weight, gains, proj[0].T, codebook, codes.reshape(8, 128), grids, orders,
        avg_in, avg_down,
    )
    return pl.pallas_call(
        split_outputs,
        out_shape=(
            outs[0], outs[1], outs[2],
            jax.ShapeDtypeStruct((1, 2, 8), F32),
            jax.ShapeDtypeStruct((1, 8, 8), F32),
            jax.ShapeDtypeStruct(codebook.shape, F32),
            outs[4], outs[5],
        ),
        in_specs=[vmem] * 6,
        out_specs=[vmem] * 8,
        name="split_outputs",
    )(*made)


def split_outputs(
    bout_in, gin_in, gdn_in, small_in, ain_in, adn_in,
    bout, gin, gdn, ggain, gproj, gbook, ain, adn,
):
    bout[...] = bout_in[...]
    gin[...] = gin_in[...]
    gdn[...] = gdn_in[...]
    ain[...] = ain_in[...]
    adn[...] = adn_in[...]
    small = small_in[...]
    gbook[...] = small[:, 0:64]
    gproj[0] = small[:, 64:72]
    ggain[0] = jnp.transpose(jnp.concatenate([small] * 16, axis=0))[72:74, 0:8]


def solution(mesh):
    placed = (
        P("section", "dp", None),
        P("section", None, None),
        P("section", None, None),
        P("section", None, None),
        P("section", None, None),
        P(None, ("section", "dp")),
        P("dp"),
        P("dp"),
        P("dp", None),
        P("section", "dp", None),
        P("section", "dp", None),
    )
    return jax.shard_map(
        body,
        mesh=mesh,
        in_specs=placed,
        out_specs=(
            P("section", "dp", None),
            P("section", "dp", None),
            P("section", "dp", None),
            P("section", None, "dp"),
            P("section", "dp", None),
            P(None, ("section", "dp")),
            P("section", "dp", None),
            P("section", "dp", None),
        ),
        check_vma=False,
    )
```

```python
import functools

import jax
import jax.numpy as jnp
from jax import lax
from jax.experimental import pallas as pl
from jax.experimental.pallas import tpu as pltpu
from jax.sharding import PartitionSpec as P

BF = jnp.bfloat16
F32 = jnp.float32
I32 = jnp.int32
MESH = pl.DeviceIdType.MESH

D = 512
FF = 2048
CLIP = 512
GRID = 256
WINDOW = 64
HALF = 4096
NORM_EPS = 1e-05
AVG_DECAY = 0.9
LEARN_RATE = 0.0005
SCALE = 0.125
WB = 4

CHUNKS = {"a": (32, 512), "b": (16, 1024), "c": (16, 768), "o": (16, 256)}


def nn(left, right):
    return lax.dot_general(left, right, (((1,), (0,)), ((), ())), preferred_element_type=F32)


def nt(left, right):
    return lax.dot_general(left, right, (((1,), (1,)), ((), ())), preferred_element_type=F32)


def tn(left, right):
    return lax.dot_general(left, right, (((0,), (0,)), ((), ())), preferred_element_type=F32)


def tt(left, right):
    return lax.dot_general(left, right, (((0,), (1,)), ((), ())), preferred_element_type=F32)


def iota(shape, axis):
    return lax.broadcasted_iota(I32, shape, axis)


def normed(h):
    mean = jnp.mean(h, axis=-1, keepdims=True)
    c = h - mean
    var = jnp.mean(c * c, axis=-1, keepdims=True)
    r = lax.rsqrt(var + NORM_EPS)
    return c * r, r


def normed_back(grad, xhat, r, gain):
    t = grad * gain
    m1 = jnp.mean(t, axis=-1, keepdims=True)
    m2 = jnp.mean(t * xhat, axis=-1, keepdims=True)
    return r * (t - m1 - xhat * m2)


def gelu_pair(u):
    c0 = 0.7978845608028654
    c1 = 0.7978845608028654 * 0.044715
    m = c1 * (u * u)
    half = 0.5 + 0.5 * jnp.tanh(u * (c0 + m))
    value = u * half
    slope = half + (value - value * half) * (2.0 * c0 + 6.0 * m)
    return value, slope


def ten_shapes():
    shapes = {
        "xs": ((2, CLIP, D), BF),
        "win": ((D, 4 * D + FF), BF),
        "wdn": ((FF, D), BF),
        "perm": ((2, GRID, GRID), BF),
        "bd1": ((256, 256), BF),
        "bds": ((256, 256), BF),
        "bdf": ((256, 256), F32),
        "tbl": ((32, 16, 128), BF),
        "pre": ((2, 2, 8, 128), F32),
        "cds": ((2, 8, CLIP), I32),
        "cxs": ((2, 16, CLIP), BF),
        "cxr": ((2, 16, CLIP), BF),
        "fcs": ((2, 8, CLIP), F32),
        "fcr": ((2, 8, CLIP), F32),
        "ent": ((2, 2, 8, CLIP), F32),
        "cvec": ((2, 16, CLIP), BF),
        "hb": ((CLIP, D), F32),
        "bo": ((2 * CLIP, D), BF),
        "m8": ((16, FF), BF),
        "pgt": ((D, 128), F32),
        "q8": ((2, 8, 768), F32),
        "q0": ((8, 768), F32),
        "qs1": ((8, 768), F32),
        "qz": ((3, 8, 768), F32),
        "qs2": ((8, 768), F32),
        "qx": ((3, 8, 768), F32),
        "qs3": ((8, 768), F32),
        "qy": ((8, 768), F32),
        "qs4": ((8, 768), F32),
        "qg": ((8, 768), F32),
        "avi": ((8, 4 * D + FF), F32),
        "avd": ((32, D), F32),
        "gob": ((CLIP, D), BF),
        "xh1": ((2, CLIP, D), F32),
        "xh2": ((2, CLIP, D), F32),
        "r1": ((2, CLIP, 1), F32),
        "r2": ((2, CLIP, 1), F32),
        "a1": ((2, CLIP, D), BF),
        "a2": ((2, CLIP, D), BF),
        "qkv": ((2, CLIP, 3 * D), BF),
        "prob": ((2, CLIP, D), F32),
        "att": ((2, CLIP, D), BF),
        "act": ((2, CLIP, FF), BF),
        "gel": ((2, CLIP, FF), BF),
        "gy": ((2, CLIP, D), BF),
        "eb": ((2, CLIP, D), BF),
        "acc_dn": ((FF, D), F32),
        "acc_up": ((D, FF), F32),
        "acc_qkv": ((D, 3 * D), F32),
        "acc_out": ((D, D), F32),
        "s_acc": ((4, 8, 2, 8, 128), F32),
        "gacc": ((2, 8, D), F32),
        "s0": ((4, 8, 8, 128), F32),
        "s1": ((3, 8, 8, 128), F32),
        "s2": ((7, 8, 128), F32),
    }
    for k, (rows, w) in CHUNKS.items():
        h = w // 2
        shapes["sb0" + k] = ((4, 4, 2, rows, w), BF)
        shapes["r0" + k] = ((4, 4, 2, rows, w), BF)
        for ax in "zx":
            for slot in "012":
                shapes["q" + slot + ax + k] = ((2, 4, rows, h), BF)
            shapes["p" + ax + k] = ((7, rows, h), BF)
    return shapes


SHAPES = ten_shapes()
N_SEM = 200


class Refs:
    pass


def mega(
    x_hbm, win_hbm, wdn_hbm, gains_ref, proj_ref, book_ref, codes_ref, grids_ref, orders_ref,
    avgin_hbm, avgdn_hbm,
    bout_hbm, gin_ref, gdn_ref, small_ref, ain_ref, adn_ref,
    *scratch,
):
    s = Refs()
    for name, ref in zip(SHAPES, scratch):
        setattr(s, name, ref)
    send_sems, recv_sems, load_sems = scratch[len(SHAPES):]

    sec = lax.axis_index("section")
    dp = lax.axis_index("dp")
    core = dp % 2
    yh = (dp // 2) % 2
    x = (dp // 4) % 4
    z = dp // 16
    is_e = sec == 0
    is_d = sec == 1

    def place(zz, xx, yy, cc):
        return (sec, ((zz * 4 + xx) * 2 + yy) * 2 + cc)

    core_dev = place(z, x, yh, 1 - core)
    y_dev = place(z, x, 1 - yh, core)
    def flips(v):
        return {1: v + 1 - 2 * (v % 2), 2: (v + 2) % 4, 3: 3 - v}

    z_flip, x_flip = flips(z), flips(x)
    z_dev = [place((z + d) % 4, x, yh, core) for d in (1, 2, 3)]
    x_dev = [place(z, (x + d) % 4, yh, core) for d in (1, 2, 3)]
    sec_dev = (1 - sec, dp)
    sec_core_dev = (1 - sec, dp + 1 - 2 * core)
    around = [(2, 1), (1, 1), (3, 1), (0, 1), (2, 0), (1, 0), (3, 0)]
    zy_dev = [place((z + d) % 4, x, (yh + y) % 2, core) for d, y in around]
    xy_dev = [place(z, (x + d) % 4, (yh + y) % 2, core) for d, y in around]

    counter = [0]
    slots = {}

    def rcopy(key, src, dst, dev):
        if key not in slots:
            slots[key] = counter[0]
            counter[0] += 1
        i = slots[key]
        return pltpu.make_async_remote_copy(
            src_ref=src, dst_ref=dst, send_sem=send_sems.at[i], recv_sem=recv_sems.at[i],
            device_id=dev, device_id_type=MESH,
        )

    def bout_copy(c):
        rows = pl.ds(c * CLIP, CLIP)
        return pltpu.make_async_copy(s.bo.at[rows], bout_hbm.at[0, rows], load_sems.at[5 + c])

    barrier = pltpu.get_barrier_semaphore()
    far = [(i, j, y) for i in range(4) for j in range(4) for y in range(2) if i + j + y > 0]
    far.sort(key=lambda p: -(min(p[0], 4 - p[0]) + min(p[1], 4 - p[1]) + 2 * p[2]))
    wide = [n for n, (i, j, y) in enumerate(far) if i > 0 and j > 0]
    far_dev = [place((z + i) % 4, (x + j) % 4, (yh + y) % 2, core) for i, j, y in far]
    plane_dev = [dev for n, dev in enumerate(far_dev) if n not in wide]
    near_dev = [sec_core_dev, sec_dev, core_dev]
    @pl.when(is_d)
    def _():
        for n in wide:
            pl.semaphore_signal(barrier, inc=1, device_id=far_dev[n], device_id_type=MESH)

    for dev in plane_dev + near_dev:
        pl.semaphore_signal(barrier, inc=1, device_id=dev, device_id_type=MESH)

    loads = [
        pltpu.make_async_copy(x_hbm.at[0, pl.ds(0, CLIP)], s.xs.at[0], load_sems.at[0]),
        pltpu.make_async_copy(win_hbm.at[0, :, pl.ds(0, 3 * D)], s.win.at[:, pl.ds(0, 3 * D)], load_sems.at[1]),
        pltpu.make_async_copy(
            win_hbm.at[0, :, pl.ds(3 * D, D + FF)], s.win.at[:, pl.ds(3 * D, D + FF)], load_sems.at[2]
        ),
        pltpu.make_async_copy(wdn_hbm.at[0], s.wdn, load_sems.at[3]),
        pltpu.make_async_copy(x_hbm.at[0, pl.ds(CLIP, CLIP)], s.xs.at[1], load_sems.at[4]),
    ]
    averages = [
        pltpu.make_async_copy(avgin_hbm.at[0], s.avi, load_sems.at[7]),
        pltpu.make_async_copy(avgdn_hbm.at[0], s.avd, load_sems.at[8]),
    ]
    for load in loads + averages:
        load.start()

    rows_i = iota((256, 256), 0)
    cols_i = iota((256, 256), 1)
    same = ((rows_i >> 6) == (cols_i >> 6)).astype(F32)
    s.bdf[...] = same * SCALE
    s.bd1[...] = same.astype(BF)
    s.bds[...] = (same * SCALE).astype(BF)
    for c in range(2):
        code_row = jnp.concatenate([codes_ref[4 * c + k : 4 * c + k + 1, :] for k in range(4)], axis=1)
        s.cds[c] = jnp.broadcast_to(code_row, (8, CLIP))

    proj_t = proj_ref[...]
    gain_one = gains_ref[0, 0:1, :].astype(F32)
    gain_two = gains_ref[0, 1:2, :].astype(F32)
    book = book_ref[...].astype(F32)
    empty = jnp.zeros((8, 64), F32)
    s.pre[sec, core] = jnp.where(
        is_e, jnp.concatenate([book, empty], axis=1), jnp.concatenate([empty, book], axis=1)
    )
    s.gacc[...] = jnp.zeros((2, 8, D), F32)
    s.s_acc[...] = jnp.zeros((4, 8, 2, 8, 128), F32)

    def book_start():
        pl.semaphore_wait(barrier, len(plane_dev + near_dev) + sec * len(wide))
        mine = s.pre.at[sec, core]

        @pl.when(is_e)
        def _():
            rcopy("ag0", mine, mine, sec_dev).start()
            rcopy("ag1", mine, mine, sec_core_dev).start()

        @pl.when(is_d)
        def _():
            rcopy("ag2", mine, mine, core_dev).start()

    def gather_book_start():
        chip = dp // 2
        rcopy("ag0", s.pre.at[0, core], s.pre.at[0, core], sec_dev).wait_recv()
        rcopy("ag1", s.pre.at[0, 1 - core], s.pre.at[0, 1 - core], sec_core_dev).wait_recv()
        rcopy("ag2", s.pre.at[1, 1 - core], s.pre.at[1, 1 - core], core_dev).wait_recv()
        s.tbl[chip] = jnp.concatenate([s.pre[0, 0] + s.pre[1, 0], s.pre[0, 1] + s.pre[1, 1]], axis=0).astype(BF)
        part = s.tbl.at[chip]
        for n in range(31):
            rcopy("ag3%d" % n, part, part, far_dev[n]).start()

    def gather_book_wait():
        for n, (i, j, y) in enumerate(far):
            part = s.tbl.at[(((z + 4 - i) % 4) * 4 + (x + 4 - j) % 4) * 2 + (yh + 2 - y) % 2]
            rcopy("ag3%d" % n, part, part, far_dev[n]).wait_recv()

    def book_finish():
        mine = s.pre.at[sec, core]

        @pl.when(is_e)
        def _():
            rcopy("ag0", mine, mine, sec_dev).wait_send()
            rcopy("ag1", mine, mine, sec_core_dev).wait_send()

        @pl.when(is_d)
        def _():
            rcopy("ag2", mine, mine, core_dev).wait_send()
            part = s.tbl.at[dp // 2]
            for n in range(31):
                rcopy("ag3%d" % n, part, part, far_dev[n]).wait_send()

    def onehots(c, half, shift):
        code_row = s.cds[c][0:1, :] - half * HALF
        hi = code_row >> 6
        lo = code_row & 63
        lo_one = (iota((128, CLIP), 0) == lo + shift).astype(F32).astype(BF)
        hi_mask = (iota((CLIP, CLIP), 0) >> 3) == hi
        return lo_one, hi_mask

    def entries(c):
        for half in range(2):
            lo_one, hi_mask = onehots(c, half, 64 * half)
            table = s.tbl[...].reshape(CLIP, 128)
            picked = jnp.where(hi_mask, nn(table, lo_one), 0.0)
            s.ent[c, half] = jnp.sum(picked.reshape(64, 8, CLIP), axis=0)

    def total(parts):
        parts = [v.astype(F32) for v in parts]
        while len(parts) > 1:
            parts = [a + b for a, b in zip(parts[::2], parts[1::2])] + parts[len(parts) // 2 * 2 :]
        return parts[0]

    def pad16(v):
        return jnp.concatenate([v, jnp.zeros((8, v.shape[1]), F32)], axis=0).astype(BF)

    def book_proj_terms(c, code_grad, wide_rows, narrow):
        lo_one, hi_mask = onehots(c, sec, 0)
        spread = jnp.broadcast_to(code_grad[None], (64, 8, CLIP)).reshape(CLIP, CLIP)
        left = jnp.where(hi_mask, spread, 0.0).astype(BF)
        total = nt(left, lo_one)
        narrow_wide = jnp.concatenate(
            [jnp.zeros((64, CLIP), F32), narrow, jnp.zeros((56, CLIP), F32)], axis=0
        ).astype(BF)
        total = total + tt(wide_rows, narrow_wide)
        s.s_acc[...] += total.reshape(4, 8, 2, 8, 128)

    def norm_qkv(c, parts):
        halves = [slice(0, 256), slice(256, 512)]
        a = []
        for rows, h in zip(halves, parts):
            s.hb[rows] = h
            xh, r = normed(h)
            s.xh1[c, rows] = xh
            s.r1[c, rows] = r
            a.append((xh * gain_one).astype(BF))
            s.a1[c, rows] = a[-1]
        for j in range(3):
            for rows, v in zip(halves, a):
                s.qkv[c, rows, 512 * j : 512 * j + 512] = nn(v, s.win[:, 512 * j : 512 * j + 512]).astype(BF)

    def feed_forward(c, put, ahead=False):
        m = s.hb[...] + nn(s.att[c], s.win[:, 1536:2048])
        xh, r = normed(m)
        s.xh2[c] = xh
        s.r2[c] = r
        a = (xh * gain_two).astype(BF)
        s.a2[c] = a
        acc = m
        nxt = nn(a, s.win[:, 2048:2304])
        for j in range(8):
            cols = slice(256 * j, 256 * j + 256)
            u = nxt
            if j < 7:
                nxt = nn(a, s.win[:, 2304 + 256 * j : 2560 + 256 * j])
            value, slope = gelu_pair(u.astype(BF))
            s.act[c, :, cols] = value
            s.gel[c, :, cols] = s.gel[c, :, cols] * slope if ahead else slope
            acc = acc + nn(value, s.wdn[cols, :])
        put(acc)

    def units(c, w, count):
        out = []
        for n in range(count):
            rows = pl.ds((w * count + n) * WINDOW, WINDOW)
            for quad in range(2):
                out.append((rows, 256 * quad))
        return out

    def widened(v, mask):
        return jnp.concatenate([v] * 4, axis=0) * mask

    def heads_of(wide):
        return (wide[0:64] + wide[64:128]) + (wide[128:192] + wide[192:256])

    def window_forward(c, w):
        if True:
            us = units(c, w, WB)
            bds = s.bds[...]
            bdf = s.bdf[...]
            q = [s.qkv[c, r, o : o + 256] for r, o in us]
            k = [s.qkv[c, r, 512 + o : 768 + o] for r, o in us]
            v = [s.qkv[c, r, 1024 + o : 1280 + o] for r, o in us]
            scores = [nt(kk, widened(qq, bds)) for kk, qq in zip(k, q)]
            e = [jnp.exp(x - jnp.max(x, axis=0, keepdims=True)) for x in scores]
            p = [x * (1.0 / jnp.sum(x, axis=0, keepdims=True)) for x in e]
            wide = [tn(x.astype(BF), vv) for x, vv in zip(p, v)]
            att = [(heads_of(x * bdf) * (1.0 / SCALE)).astype(BF) for x in wide]
            for (r, o), pp, aa in zip(us, p, att):
                s.prob[c, r, o : o + 256] = pp
                s.att[c, r, o : o + 256] = aa

    def window_backward(c, w):
        if True:
            us = units(c, w, WB)
            bds = s.bds[...]
            bd1 = s.bd1[...]
            bdf = s.bdf[...]
            q = [s.qkv[c, r, o : o + 256] for r, o in us]
            k = [s.qkv[c, r, 512 + o : 768 + o] for r, o in us]
            v = [s.qkv[c, r, 1024 + o : 1280 + o] for r, o in us]
            go = [widened(s.gob[r, o : o + 256], bd1) for r, o in us]
            p = [s.prob[c, r, o : o + 256] for r, o in us]
            gp = [nt(vv, gg) for vv, gg in zip(v, go)]
            gv = [nn(pp.astype(BF), gg).astype(BF) for pp, gg in zip(p, go)]
            gs = [
                (pp * (x - jnp.sum(x * pp, axis=0, keepdims=True))).astype(BF)
                for pp, x in zip(p, gp)
            ]
            gk = [nn(x, widened(qq, bds)).astype(BF) for x, qq in zip(gs, q)]
            gq = [heads_of(tn(x, kk) * bdf).astype(BF) for x, kk in zip(gs, k)]
            for (r, o), a, b, d in zip(us, gq, gk, gv):
                s.qkv[c, r, o : o + 256] = a
                s.qkv[c, r, 512 + o : 768 + o] = b
                s.qkv[c, r, 1024 + o : 1280 + o] = d

    def head_sums(v):
        return nn(v, s.bd1[...])

    CR = 256

    def frames_forward(c):
        late0 = orders_ref[c, 0] > orders_ref[c, 1]
        sign = jnp.where(late0, 1.0, -1.0).astype(F32)
        r0 = slice(0, GRID)
        r1 = slice(GRID, CLIP)
        for quad in range(2):
            qc = slice(256 * quad, 256 * quad + 256)
            kc = slice(512 + 256 * quad, 768 + 256 * quad)
            vc = slice(1024 + 256 * quad, 1280 + 256 * quad)
            q_late = jnp.where(late0, s.qkv[c, r0, qc], s.qkv[c, r1, qc])
            k_diff = s.qkv[c, r1, kc] - s.qkv[c, r0, kc]
            v0 = s.qkv[c, r0, vc]
            v1 = s.qkv[c, r1, vc]
            d = head_sums(q_late * k_diff) * (sign * SCALE)
            e = jnp.exp(-jnp.abs(d))
            big = 1.0 / (1.0 + e)
            small = e * big
            p_other = jnp.where(d > 0.0, big, small)
            p_self = jnp.where(d > 0.0, small, big)
            s.prob[c, r0, qc] = p_other
            s.prob[c, r1, qc] = p_self
            p0 = jnp.where(late0, p_self, p_other).astype(BF)
            p1 = jnp.where(late0, p_other, p_self).astype(BF)
            mix = (p0.astype(F32) * v0.astype(F32) + p1.astype(F32) * v1.astype(F32)).astype(BF)
            s.att[c, r0, qc] = jnp.where(late0, mix, v0)
            s.att[c, r1, qc] = jnp.where(late0, v1, mix)

    def frames_backward(c):
        late0 = orders_ref[c, 0] > orders_ref[c, 1]
        r0 = slice(0, GRID)
        r1 = slice(GRID, CLIP)
        for quad in range(2):
            qc = slice(256 * quad, 256 * quad + 256)
            kc = slice(512 + 256 * quad, 768 + 256 * quad)
            vc = slice(1024 + 256 * quad, 1280 + 256 * quad)
            q_late = jnp.where(late0, s.qkv[c, r0, qc], s.qkv[c, r1, qc])
            k_diff = s.qkv[c, r1, kc] - s.qkv[c, r0, kc]
            v_diff = s.qkv[c, r1, vc] - s.qkv[c, r0, vc]
            go0 = s.gob[r0, qc]
            go1 = s.gob[r1, qc]
            go_late = jnp.where(late0, go0, go1)
            go_early = jnp.where(late0, go1, go0)
            p_other = s.prob[c, r0, qc]
            p_self = s.prob[c, r1, qc]
            gs = (p_other * p_self * head_sums(go_late * v_diff)).astype(BF).astype(F32) * SCALE
            gq = (gs * k_diff.astype(F32)).astype(BF)
            gk = gs * q_late.astype(F32)
            late32 = go_late.astype(F32)
            gv_late = (p_self.astype(BF).astype(F32) * late32).astype(BF)
            gv_early = (go_early.astype(F32) + p_other.astype(BF).astype(F32) * late32).astype(BF)
            none = jnp.zeros_like(gq)
            s.qkv[c, r0, qc] = jnp.where(late0, gq, none)
            s.qkv[c, r1, qc] = jnp.where(late0, none, gq)
            s.qkv[c, r0, kc] = (-gk).astype(BF)
            s.qkv[c, r1, kc] = gk.astype(BF)
            s.qkv[c, r0, vc] = jnp.where(late0, gv_late, gv_early)
            s.qkv[c, r1, vc] = jnp.where(late0, gv_early, gv_late)

    def gain_terms(which, grad, xhat):
        part = jnp.sum((grad * xhat).reshape(-1, 8, D), axis=0)
        s.gacc[which] += part

    def back_down_codes(c):
        twice = jnp.concatenate([s.cvec[c][0:8].astype(F32)] * 2, axis=0).astype(BF)
        for j in range(4):
            cols = slice(512 * j, 512 * j + 512)
            s.gel[c, :, cols] = (tn(twice, s.m8[:, cols]) * s.gel[c, :, cols].astype(F32)).astype(BF)

    def back_up(c, grad_of):
        acc = None
        for j in range(4):
            term = nt(s.gel[c, :, 512 * j : 512 * j + 512], s.win[:, 2048 + 512 * j : 2560 + 512 * j])
            acc = term if acc is None else acc + term
        xh = s.xh2[c]
        gain_terms(1, acc, xh)
        gm = grad_of() + normed_back(acc, xh, s.r2[c], gain_two)
        s.hb[...] = gm
        gy = gm.astype(BF)
        s.gy[c] = gy
        s.gob[...] = nt(gy, s.win[:, 1536:2048]).astype(BF)

    def back_in(c):
        acc = None
        for j in range(3):
            cols = slice(512 * j, 512 * j + 512)
            term = nt(s.qkv[c, :, cols], s.win[:, cols])
            acc = term if acc is None else acc + term
        xh = s.xh1[c]
        gain_terms(0, acc, xh)
        return s.hb[...] + normed_back(acc, xh, s.r1[c], gain_one)

    def add_into(ref, rows, cols, c, value):
        ref[rows, cols] = jnp.where(c == 0, value, ref[rows, cols] + value)

    def grad_down(c):
        for j in range(4):
            cols = slice(512 * j, 512 * j + 512)
            add_into(s.acc_dn, cols, slice(None), c, tn(s.act[c, :, cols], s.xs[c]))

    def grad_down_codes(c):
        code = s.cvec[c][0:8].astype(F32)
        wide = jnp.concatenate([jnp.zeros((80, CLIP), F32)] + [code] * 4 + [jnp.zeros((16, CLIP), F32)], axis=0)
        wide = wide.astype(BF)
        lanes = (iota((8, 128), 1) >> 3) - 10
        for j in range(4):
            v = tt(s.act[c, :, 512 * j : 512 * j + 512], wide).reshape(16, 4, 8, 128)
            picked = [jnp.where(lanes == m, v[:, m], 0.0) for m in range(4)]
            s.s_acc[j] += total(picked).reshape(8, 2, 8, 128)

    def grad_qkv_codes(c):
        norm_row = jnp.transpose(jnp.broadcast_to(s.r1[c], (CLIP, 128)))[0:1, :]
        part = nn(pad16(s.cvec[c][0:8].astype(F32) * norm_row), s.qkv[c])[0:8]
        for half in range(2):
            v = part[:, 768 * half : 768 * half + 768]
            s.q8[half] = jnp.where(c == 0, v, s.q8[half] + v)

    def grad_up(c):
        for j in range(4):
            cols = slice(512 * j, 512 * j + 512)
            add_into(s.acc_up, slice(None), cols, c, tn(s.a2[c], s.gel[c, :, cols]))

    def grad_out(c):
        add_into(s.acc_out, slice(None), slice(None), c, tn(s.att[c], s.gy[c]))

    def grad_attn(c):
        for j in range(3):
            cols = slice(512 * j, 512 * j + 512)
            add_into(s.acc_qkv, slice(None), cols, c, tn(s.a1[c], s.qkv[c, :, cols]))

    def share(k, i, to_core):
        n = 2 * i + to_core
        if k == "a":
            return s.acc_dn[pl.ds(pl.multiple_of(n * 32, 32), 32), :]
        rows = pl.ds(pl.multiple_of(n * 8, 8), 8)
        ref, w = {"b": (s.acc_up, 1024), "c": (s.acc_qkv, 768), "o": (s.acc_out, 256)}[k]
        return jnp.concatenate([ref[rows, 0:w], ref[rows, w : 2 * w]], axis=0)

    def buf(name, k):
        return getattr(s, name + k)

    def copies(k, step):
        if k == "s":
            if step == 0:
                return [rcopy("s0", s.s_acc.at[:, :, 1 - core], s.s0, core_dev)]
            if step == 1:
                return [rcopy("s1%d" % i, s.s0.at[(z + 1 + i) % 4], s.s1.at[i], z_dev[i]) for i in range(3)]
            return [
                rcopy(
                    "s2%d" % i, s.s0.at[z, 2 * ((x + d) % 4) + (yh + y) % 2], s.s2.at[i], xy_dev[i]
                )
                for i, (d, y) in enumerate(around)
            ]
        if k == "q":
            if step == 0:
                return [rcopy("q0", s.q8.at[1 - core], s.q0, core_dev)]
            if step == 1:
                return [rcopy("q1%d" % i, s.qs1, s.qz.at[i], z_dev[i]) for i in range(3)]
            if step == 2:
                return [rcopy("q2%d" % i, s.qs2, s.qx.at[i], x_dev[i]) for i in range(3)]
            if step == 3:
                return [rcopy("q3", s.qs3, s.qy, y_dev)]
            return [rcopy("q4", s.qs4, s.qg, core_dev)]
        rows, w = CHUNKS[k]
        h = w // 2
        r0 = buf("r0", k)
        if step == 0:
            return [rcopy(k + "0", buf("sb0", k), r0, core_dev)]
        lo, hi = pl.ds(0, h), pl.ds(h, h)
        out = []
        if step == 4:
            for i, (d, y) in enumerate(around):
                out.append(
                    rcopy(
                        "%s4x%d" % (k, i), r0.at[z, (x + d) % 4, (yh + y) % 2, :, lo],
                        buf("px", k).at[i], xy_dev[i],
                    )
                )
                out.append(
                    rcopy(
                        "%s4z%d" % (k, i), r0.at[(z + d) % 4, x, (yh + y) % 2, :, hi],
                        buf("pz", k).at[i], zy_dev[i],
                    )
                )
            return out
        for y in range(2):
            first, second = ((1, 3), (3, 1))[y]
            hop = second if step == 3 else first
            block = {1: 2, 2: first, 3: second}[step]
            slot = {1: "q1", 2: "q0", 3: "q2"}[step]
            out.append(
                rcopy(
                    "%s%dz%d" % (k, step, y), r0.at[z_flip[block], :, y, :, lo],
                    buf(slot + "z", k).at[y], place(z_flip[hop], x, yh, core),
                )
            )
            out.append(
                rcopy(
                    "%s%dx%d" % (k, step, y), r0.at[:, x_flip[block], y, :, hi],
                    buf(slot + "x", k).at[y], place(z, x_flip[hop], yh, core),
                )
            )
        return out

    def arrived(k, step):
        for cp in copies(k, step):
            cp.wait_recv()

    def send(k, step):
        for cp in copies(k, step):
            cp.start()

    def put_down(mine):
        gdn_ref[0] = mine
        piece = s.wdn[pl.ds(dp * 32, 32), :].astype(F32)
        adn_ref[0] = AVG_DECAY * s.avd[...] + (1.0 - AVG_DECAY) * (piece - LEARN_RATE * mine)

    def reduce_step(k, step):
        if k == "s":
            if step > 0:
                arrived(k, step - 1)
            if step == 1:
                s.s0[...] += s.s_acc[:, :, core]
            elif step == 2:
                s.s0[z] += (s.s1[0] + s.s1[1]) + s.s1[2]
            elif step == 3:
                small = total([s.s0[z, 2 * x + yh]] + [s.s2[i] for i in range(7)])
                small_ref[...] = small

                @pl.when(is_e)
                def _():
                    narrow = proj_t.astype(F32)
                    shares = [
                        total([small[:, n : n + 1] * narrow[n % 8 : n % 8 + 1, :] for n in range(80 + 8 * m, 88 + 8 * m)])
                        for m in range(4)
                    ]
                    put_down(jnp.concatenate(shares, axis=0))

                return
            send(k, step)
            return
        if k == "q":
            if step > 0:
                arrived(k, step - 1)
            if step == 1:
                s.qs1[...] = s.q8[core] + s.q0[...]
            elif step == 2:
                s.qs2[...] = total([s.qs1[...]] + [s.qz[i] for i in range(3)])
            elif step == 3:
                s.qs3[...] = total([s.qs2[...]] + [s.qx[i] for i in range(3)])
            elif step == 4:
                s.qs4[...] = s.qs3[...] + s.qy[...]
            elif step == 5:
                mine, other = s.qs4[...], s.qg[...]
                narrow = s.pgt[pl.ds(pl.multiple_of(dp * 8, 8), 8), :]
                for half, v in enumerate((jnp.where(core == 0, mine, other), jnp.where(core == 0, other, mine))):
                    gin_ref[0, :, 768 * half : 768 * half + 768] = total(
                        [narrow[:, n : n + 1] * v[n : n + 1, :] for n in range(8)]
                    )
                return
            send(k, step)
            return
        rows, w = CHUNKS[k]
        h = w // 2
        r0 = buf("r0", k)
        lo, hi = pl.ds(0, h), pl.ds(h, h)
        if step == 0:
            sb0 = buf("sb0", k)

            def body(i, carry):
                for y in range(2):
                    sb0[i // 4, i % 4, y] = share(k, 2 * i + y, 1 - core).astype(BF)
                return carry

            lax.fori_loop(0, 16, body, 0)
            send(k, 0)
        elif step == 1:
            arrived(k, 0)

            def body(i, carry):
                for y in range(2):
                    r0[i // 4, i % 4, y] = total([share(k, 2 * i + y, core), r0[i // 4, i % 4, y]]).astype(BF)
                return carry

            lax.fori_loop(0, 16, body, 0)
            send(k, 1)
            send(k, 2)
        elif step == 2:
            arrived(k, 1)
            for y in range(2):
                second = (3, 1)[y]
                zb, xb = z_flip[second], x_flip[second]
                r0[zb, :, y, :, lo] = total([r0[zb, :, y, :, lo], buf("q1z", k)[y]]).astype(BF)
                r0[:, xb, y, :, hi] = total([r0[:, xb, y, :, hi], buf("q1x", k)[y]]).astype(BF)
            send(k, 3)
        elif step == 3:
            arrived(k, 2)
            arrived(k, 3)
            for y in range(2):
                r0[z, :, y, :, lo] = total(
                    [r0[z, :, y, :, lo], buf("q0z", k)[y], buf("q2z", k)[y]]
                ).astype(BF)
                r0[:, x, y, :, hi] = total(
                    [r0[:, x, y, :, hi], buf("q0x", k)[y], buf("q2x", k)[y]]
                ).astype(BF)
            send(k, 4)
        else:
            arrived(k, 4)
            left = total([r0[z, x, yh, :, lo]] + [buf("px", k)[i] for i in range(7)])
            right = total([r0[z, x, yh, :, hi]] + [buf("pz", k)[i] for i in range(7)])
            mine = jnp.concatenate([left, right], axis=1)
            if k == "a":
                put_down(mine)
            else:
                first = {"b": 2048, "c": 0, "o": 1536}[k]
                gin_ref[0, :, first : first + w] = mine[0:8]
                gin_ref[0, :, first + w : first + 2 * w] = mine[8:16]

    def add_gains():
        sums = jnp.concatenate(
            [
                jnp.sum(s.gacc[0], axis=0, keepdims=True),
                jnp.sum(s.gacc[1], axis=0, keepdims=True),
                jnp.zeros((6, D), F32),
            ],
            axis=0,
        )
        wide_sums = jnp.concatenate([jnp.zeros((72, D), F32), sums, jnp.zeros((48, D), F32)], axis=0)
        s.s_acc[...] += jnp.transpose(wide_sums).reshape(4, 8, 2, 8, 128)

    def code_copy(c):
        return pltpu.make_async_remote_copy(
            src_ref=s.fcs.at[c], dst_ref=s.fcr.at[c], send_sem=send_sems.at[N_SEM - 2 + c],
            recv_sem=recv_sems.at[N_SEM - 2 + c], device_id=sec_dev, device_id_type=MESH,
        )

    def grad_copy(c):
        return pltpu.make_async_remote_copy(
            src_ref=s.cxs.at[c], dst_ref=s.cxr.at[c], send_sem=send_sems.at[N_SEM - 4 + c],
            recv_sem=recv_sems.at[N_SEM - 4 + c], device_id=sec_dev, device_id_type=MESH,
        )

    @pl.when(is_e)
    def _():
        for c in range(2):
            grid_now = grids_ref[c]
            width = jnp.where(grid_now == 0, 16, jnp.where(grid_now == 1, 32, 8)).astype(I32)
            log_across = jnp.where(grid_now == 0, 1, jnp.where(grid_now == 1, 2, 0)).astype(I32)
            across_mask = jnp.where(grid_now == 0, 1, jnp.where(grid_now == 1, 3, 0)).astype(I32)
            window_no = rows_i >> 6
            inner = rows_i & 63
            source = (
                ((window_no >> log_across) * 8 + (inner >> 3)) * width
                + (window_no & across_mask) * 8
                + (inner & 7)
            )
            s.perm[c] = (source == cols_i).astype(F32).astype(BF)
        loads[0].wait()
        loads[1].wait()

        def forward(c, carry):
            @pl.when(c == 1)
            def _():
                loads[4].wait()

            raster = [s.xs[c, 0:GRID], s.xs[c, GRID:CLIP]]
            norm_qkv(c, [nn(s.perm[c], v) for v in raster])

            @pl.when(c == 0)
            def _():
                book_start()

            window_forward(c, 0)
            window_forward(c, 1)

            @pl.when(c == 0)
            def _():
                loads[2].wait()
                loads[3].wait()

            def put(acc):
                s.eb[c] = acc.astype(BF)

            feed_forward(c, put)
            vec = nt(proj_t, s.eb[c])
            hi = vec.astype(BF).astype(F32)
            mid = (vec - hi).astype(BF).astype(F32)
            parts = jnp.concatenate([hi, mid, vec - hi - mid, jnp.zeros((8, CLIP), F32)], axis=0).astype(BF)
            for f in range(2):
                cols = slice(GRID * f, GRID * f + GRID)
                moved = nn(parts[:, cols], s.perm[c])
                s.fcs[c, :, cols] = (moved[0:8] + moved[8:16]) + moved[16:24]
            code_copy(c).start()
            return carry

        lax.fori_loop(0, 2, forward, 0)
        for j in range(4):
            cols = slice(512 * j, 512 * j + 512)
            m = nt(proj_t, s.wdn[cols, :])
            hi = m.astype(BF).astype(F32)
            s.m8[:, cols] = jnp.concatenate([hi, m - hi], axis=0).astype(BF)

    @pl.when(is_d)
    def _():
        book_start()
        for load in loads:
            load.wait()

        def ahead(c, carry):
            for j in range(4):
                cols = slice(512 * j, 512 * j + 512)
                s.gel[c, :, cols] = nt(s.xs[c], s.wdn[cols, :]).astype(BF)
            return carry

        lax.fori_loop(0, 2, ahead, 0)
        gather_book_start()
        narrow = proj_t.astype(F32)
        narrow = (narrow - jnp.mean(narrow, axis=-1, keepdims=True)) * gain_one
        s.pgt[...] = jnp.transpose(jnp.concatenate([narrow, jnp.zeros((120, D), F32)], axis=0))
        gather_book_wait()

        def both(c, carry):
            entries(c)
            code_copy(c).wait_recv()
            sent = (s.fcr[c] + s.ent[c, 0]).astype(BF).astype(F32)
            s.cvec[c] = pad16(sent + s.ent[c, 1])
            norm_qkv(c, [tn(s.cvec[c][0:8, 0:256], proj_t), tn(s.cvec[c][0:8, 256:512], proj_t)])
            frames_forward(c)

            def put(acc):
                s.bo[pl.ds(c * CLIP, CLIP), :] = acc.astype(BF)

            feed_forward(c, put, ahead=True)
            bout_copy(c).start()
            back_up(c, lambda: s.xs[c].astype(F32))
            frames_backward(c)
            s.eb[c] = back_in(c).astype(BF)
            s.cxs[c] = pad16(nt(proj_t, s.eb[c]))
            grad_copy(c).start()
            return carry

        lax.fori_loop(0, 2, both, 0)

        def downs(c, carry):
            grad_down(c)
            return carry

        def ups(c, carry):
            grad_up(c)
            return carry

        def outs(c, carry):
            grad_out(c)
            return carry

        def codes_of(c, carry):
            grad_qkv_codes(c)
            return carry

        def books(c):
            book_proj_terms(c, s.cxs[c][0:8].astype(F32), s.eb[c], s.cvec[c][0:8].astype(F32))

        lax.fori_loop(0, 2, downs, 0)
        reduce_step("a", 0)
        lax.fori_loop(0, 2, ups, 0)
        reduce_step("b", 0)
        reduce_step("a", 1)
        lax.fori_loop(0, 2, outs, 0)
        reduce_step("o", 0)
        books(0)
        reduce_step("o", 1)
        reduce_step("b", 1)
        books(1)
        reduce_step("a", 2)
        add_gains()
        lax.fori_loop(0, 2, codes_of, 0)
        for load in averages:
            load.wait()
        for item in ["q0", "s0", "q1", "b2", "o2", "a3", "s1", "q2", "b3", "o3", "s2", "q3", "a4", "q4", "o4", "s3", "b4", "q5"]:
            reduce_step(item[0], int(item[1]))

    @pl.when(is_e)
    def _():
        def backward(c, carry):
            grad_copy(c).wait_recv()
            for f in range(2):
                cols = slice(GRID * f, GRID * f + GRID)
                s.cvec[c, :, cols] = nt(s.cxr[c, :, cols], s.perm[c]).astype(BF)
            g = tn(s.cvec[c][0:8], proj_t)
            s.hb[...] = g
            back_down_codes(c)
            grad_up(c)

            @pl.when(c == 1)
            def _():
                reduce_step("b", 0)

            back_up(c, lambda: s.hb[...])
            window_backward(c, 0)

            @pl.when(c == 1)
            def _():
                reduce_step("b", 1)

            window_backward(c, 1)
            grad_attn(c)

            @pl.when(c == 1)
            def _():
                reduce_step("c", 0)
                reduce_step("b", 2)

            grad_out(c)

            @pl.when(c == 1)
            def _():
                reduce_step("o", 0)
                reduce_step("c", 1)

            s.a2[c] = back_in(c).astype(BF)
            return carry

        lax.fori_loop(0, 2, backward, 0)
        reduce_step("o", 1)

        def leave(c, carry):
            for f in range(2):
                back = tn(s.perm[c], s.a2[c, GRID * f : GRID * f + GRID])
                s.bo[pl.ds(c * CLIP + GRID * f, GRID), :] = back.astype(BF)
            bout_copy(c).start()
            book_proj_terms(c, s.cxr[c][0:8].astype(F32), s.eb[c], s.cvec[c][0:8].astype(F32))
            return carry

        lax.fori_loop(0, 2, leave, 0)
        reduce_step("c", 2)
        reduce_step("b", 3)

        def downs(c, carry):
            grad_down_codes(c)
            return carry

        lax.fori_loop(0, 2, downs, 0)
        add_gains()
        for load in averages:
            load.wait()
        for item in ["o2", "s0", "s1", "c3", "o3", "s2", "c4", "b4", "o4", "s3"]:
            reduce_step(item[0], int(item[1]))

    half_rows = s.win[pl.ds(16 * (dp // 2), 16), :].astype(F32)
    piece = jnp.where(core == 0, half_rows[0:8], half_rows[8:16])
    ain_ref[0] = AVG_DECAY * s.avi[...] + (1.0 - AVG_DECAY) * (piece - LEARN_RATE * gin_ref[0])

    for c in range(2):
        bout_copy(c).wait()

        @pl.when(is_e)
        def _():
            code_copy(c).wait_send()

        @pl.when(is_d)
        def _():
            grad_copy(c).wait_send()

    book_finish()
    def finish(chunks):
        for k in chunks:
            for step in {"s": (0, 1, 2)}.get(k, (0, 1, 2, 3, 4)):
                for cp in copies(k, step):
                    cp.wait_send()

    @pl.when(is_e)
    def _():
        finish("bcos")

    @pl.when(is_d)
    def _():
        finish("abosq")


def body(
    boundary, in_weights, down_weight, gains, proj, codebook, codes, grids, orders, avg_in, avg_down
):
    vmem = pl.BlockSpec(memory_space=pltpu.VMEM)
    smem = pl.BlockSpec(memory_space=pltpu.SMEM)
    hbm = pl.BlockSpec(memory_space=pl.ANY)
    outs = (
        jax.ShapeDtypeStruct(boundary.shape, BF),
        jax.ShapeDtypeStruct(avg_in.shape, F32),
        jax.ShapeDtypeStruct(avg_down.shape, F32),
        jax.ShapeDtypeStruct((8, 128), F32),
        jax.ShapeDtypeStruct(avg_in.shape, F32),
        jax.ShapeDtypeStruct(avg_down.shape, F32),
    )
    scratch = [pltpu.VMEM(shape, dtype) for shape, dtype in SHAPES.values()]
    scratch += [pltpu.SemaphoreType.DMA((N_SEM,)), pltpu.SemaphoreType.DMA((N_SEM,)), pltpu.SemaphoreType.DMA((9,))]
    made = pl.pallas_call(
        mega,
        out_shape=outs,
        in_specs=[hbm, hbm, hbm, vmem, vmem, vmem, vmem, smem, smem, hbm, hbm],
        out_specs=[hbm] + [vmem] * 5,
        scratch_shapes=scratch,
        compiler_params=pltpu.CompilerParams(
            collective_id=0, has_side_effects=True, vmem_limit_bytes=63 << 20
        ),
        name="both_sections",
    )(
        boundary, in_weights, down_weight, gains, proj[0].T, codebook, codes.reshape(8, 128), grids, orders,
        avg_in, avg_down,
    )
    return pl.pallas_call(
        split_outputs,
        out_shape=(
            outs[0], outs[1], outs[2],
            jax.ShapeDtypeStruct((1, 2, 8), F32),
            jax.ShapeDtypeStruct((1, 8, 8), F32),
            jax.ShapeDtypeStruct(codebook.shape, F32),
            outs[4], outs[5],
        ),
        in_specs=[vmem] * 6,
        out_specs=[vmem] * 8,
        name="split_outputs",
    )(*made)


def split_outputs(
    bout_in, gin_in, gdn_in, small_in, ain_in, adn_in,
    bout, gin, gdn, ggain, gproj, gbook, ain, adn,
):
    bout[...] = bout_in[...]
    gin[...] = gin_in[...]
    gdn[...] = gdn_in[...]
    ain[...] = ain_in[...]
    adn[...] = adn_in[...]
    small = small_in[...]
    gbook[...] = small[:, 0:64]
    gproj[0] = small[:, 64:72]
    ggain[0] = jnp.transpose(jnp.concatenate([small] * 16, axis=0))[72:74, 0:8]


def solution(mesh):
    placed = (
        P("section", "dp", None),
        P("section", None, None),
        P("section", None, None),
        P("section", None, None),
        P("section", None, None),
        P(None, ("section", "dp")),
        P("dp"),
        P("dp"),
        P("dp", None),
        P("section", "dp", None),
        P("section", "dp", None),
    )
    return jax.shard_map(
        body,
        mesh=mesh,
        in_specs=placed,
        out_specs=(
            P("section", "dp", None),
            P("section", "dp", None),
            P("section", "dp", None),
            P("section", None, "dp"),
            P("section", "dp", None),
            P(None, ("section", "dp")),
            P("section", "dp", None),
            P("section", "dp", None),
        ),
        check_vma=False,
    )
```

```python
import functools

import jax
import jax.numpy as jnp
from jax import lax
from jax.experimental import pallas as pl
from jax.experimental.pallas import tpu as pltpu
from jax.sharding import PartitionSpec as P

BF = jnp.bfloat16
F32 = jnp.float32
I32 = jnp.int32
MESH = pl.DeviceIdType.MESH

D = 512
FF = 2048
CLIP = 512
GRID = 256
WINDOW = 64
HALF = 4096
NORM_EPS = 1e-05
AVG_DECAY = 0.9
LEARN_RATE = 0.0005
SCALE = 0.125
WB = 4

CHUNKS = {"a": (32, 512), "b": (16, 1024), "c": (16, 768), "o": (16, 256)}


def nn(left, right):
    return lax.dot_general(left, right, (((1,), (0,)), ((), ())), preferred_element_type=F32)


def nt(left, right):
    return lax.dot_general(left, right, (((1,), (1,)), ((), ())), preferred_element_type=F32)


def tn(left, right):
    return lax.dot_general(left, right, (((0,), (0,)), ((), ())), preferred_element_type=F32)


def tt(left, right):
    return lax.dot_general(left, right, (((0,), (1,)), ((), ())), preferred_element_type=F32)


def iota(shape, axis):
    return lax.broadcasted_iota(I32, shape, axis)


def normed(h):
    mean = jnp.mean(h, axis=-1, keepdims=True)
    c = h - mean
    var = jnp.mean(c * c, axis=-1, keepdims=True)
    r = lax.rsqrt(var + NORM_EPS)
    return c * r, r


def normed_back(grad, xhat, r, gain):
    t = grad * gain
    m1 = jnp.mean(t, axis=-1, keepdims=True)
    m2 = jnp.mean(t * xhat, axis=-1, keepdims=True)
    return r * (t - m1 - xhat * m2)


def gelu_pair(u):
    c0 = 0.7978845608028654
    c1 = 0.7978845608028654 * 0.044715
    m = c1 * (u * u)
    half = 0.5 + 0.5 * jnp.tanh(u * (c0 + m))
    value = u * half
    slope = half + (value - value * half) * (2.0 * c0 + 6.0 * m)
    return value, slope


def ten_shapes():
    shapes = {
        "xs": ((2, CLIP, D), BF),
        "win": ((D, 4 * D + FF), BF),
        "wdn": ((FF, D), BF),
        "perm": ((2, GRID, GRID), BF),
        "bd1": ((256, 256), BF),
        "bds": ((256, 256), BF),
        "bdf": ((256, 256), F32),
        "tbl": ((32, 16, 128), BF),
        "pre": ((2, 2, 8, 128), F32),
        "cds": ((2, 8, CLIP), I32),
        "cxs": ((2, 16, CLIP), BF),
        "cxr": ((2, 16, CLIP), BF),
        "fcs": ((2, 8, CLIP), F32),
        "fcr": ((2, 8, CLIP), F32),
        "ent": ((2, 2, 8, CLIP), F32),
        "cvec": ((2, 16, CLIP), BF),
        "hb": ((CLIP, D), F32),
        "bo": ((2 * CLIP, D), BF),
        "m8": ((16, FF), BF),
        "pgt": ((D, 128), F32),
        "q8": ((2, 8, 768), F32),
        "q0": ((8, 768), F32),
        "qs1": ((8, 768), F32),
        "qz": ((3, 8, 768), F32),
        "qs2": ((8, 768), F32),
        "qx": ((3, 8, 768), F32),
        "qs3": ((8, 768), F32),
        "qy": ((8, 768), F32),
        "qs4": ((8, 768), F32),
        "qg": ((8, 768), F32),
        "avi": ((8, 4 * D + FF), F32),
        "avd": ((32, D), F32),
        "gob": ((CLIP, D), BF),
        "xh1": ((2, CLIP, D), F32),
        "xh2": ((2, CLIP, D), F32),
        "r1": ((2, CLIP, 1), F32),
        "r2": ((2, CLIP, 1), F32),
        "a1": ((2, CLIP, D), BF),
        "a2": ((2, CLIP, D), BF),
        "qkv": ((2, CLIP, 3 * D), BF),
        "prob": ((2, CLIP, D), F32),
        "att": ((2, CLIP, D), BF),
        "act": ((2, CLIP, FF), BF),
        "gel": ((2, CLIP, FF), BF),
        "gy": ((2, CLIP, D), BF),
        "eb": ((2, CLIP, D), BF),
        "acc_dn": ((FF, D), F32),
        "acc_up": ((D, FF), F32),
        "acc_qkv": ((D, 3 * D), F32),
        "acc_out": ((D, D), F32),
        "s_acc": ((4, 8, 2, 8, 128), F32),
        "gacc": ((2, 8, D), F32),
        "s0": ((4, 8, 8, 128), F32),
        "s1": ((3, 8, 8, 128), F32),
        "s2": ((7, 8, 128), F32),
    }
    for k, (rows, w) in CHUNKS.items():
        h = w // 2
        shapes["sb0" + k] = ((4, 4, 2, rows, w), BF)
        shapes["r0" + k] = ((4, 4, 2, rows, w), BF)
        for ax in "zx":
            for slot in "012":
                shapes["q" + slot + ax + k] = ((2, 4, rows, h), BF)
            shapes["p" + ax + k] = ((7, rows, h), BF)
    return shapes


SHAPES = ten_shapes()
N_SEM = 200


class Refs:
    pass


def mega(
    x_hbm, win_hbm, wdn_hbm, gains_ref, proj_ref, book_ref, codes_ref, grids_ref, orders_ref,
    avgin_hbm, avgdn_hbm,
    bout_hbm, gin_ref, gdn_ref, small_ref, ain_ref, adn_ref,
    *scratch,
):
    s = Refs()
    for name, ref in zip(SHAPES, scratch):
        setattr(s, name, ref)
    send_sems, recv_sems, load_sems = scratch[len(SHAPES):]

    sec = lax.axis_index("section")
    dp = lax.axis_index("dp")
    core = dp % 2
    yh = (dp // 2) % 2
    x = (dp // 4) % 4
    z = dp // 16
    is_e = sec == 0
    is_d = sec == 1

    def place(zz, xx, yy, cc):
        return (sec, ((zz * 4 + xx) * 2 + yy) * 2 + cc)

    core_dev = place(z, x, yh, 1 - core)
    y_dev = place(z, x, 1 - yh, core)
    def flips(v):
        return {1: v + 1 - 2 * (v % 2), 2: (v + 2) % 4, 3: 3 - v}

    z_flip, x_flip = flips(z), flips(x)
    z_dev = [place((z + d) % 4, x, yh, core) for d in (1, 2, 3)]
    x_dev = [place(z, (x + d) % 4, yh, core) for d in (1, 2, 3)]
    sec_dev = (1 - sec, dp)
    sec_core_dev = (1 - sec, dp + 1 - 2 * core)
    around = [(2, 1), (1, 1), (3, 1), (0, 1), (2, 0), (1, 0), (3, 0)]
    zy_dev = [place((z + d) % 4, x, (yh + y) % 2, core) for d, y in around]
    xy_dev = [place(z, (x + d) % 4, (yh + y) % 2, core) for d, y in around]

    counter = [0]
    slots = {}

    def rcopy(key, src, dst, dev):
        if key not in slots:
            slots[key] = counter[0]
            counter[0] += 1
        i = slots[key]
        return pltpu.make_async_remote_copy(
            src_ref=src, dst_ref=dst, send_sem=send_sems.at[i], recv_sem=recv_sems.at[i],
            device_id=dev, device_id_type=MESH,
        )

    def bout_copy(c):
        rows = pl.ds(c * CLIP, CLIP)
        return pltpu.make_async_copy(s.bo.at[rows], bout_hbm.at[0, rows], load_sems.at[5 + c])

    barrier = pltpu.get_barrier_semaphore()
    far = [(i, j, y) for i in range(4) for j in range(4) for y in range(2) if i + j + y > 0]
    far.sort(key=lambda p: -(min(p[0], 4 - p[0]) + min(p[1], 4 - p[1]) + 2 * p[2]))
    wide = [n for n, (i, j, y) in enumerate(far) if i > 0 and j > 0]
    far_dev = [place((z + i) % 4, (x + j) % 4, (yh + y) % 2, core) for i, j, y in far]
    plane_dev = [dev for n, dev in enumerate(far_dev) if n not in wide]
    near_dev = [sec_core_dev, sec_dev, core_dev]
    @pl.when(is_d)
    def _():
        for n in wide:
            pl.semaphore_signal(barrier, inc=1, device_id=far_dev[n], device_id_type=MESH)

    for dev in plane_dev + near_dev:
        pl.semaphore_signal(barrier, inc=1, device_id=dev, device_id_type=MESH)

    loads = [
        pltpu.make_async_copy(x_hbm.at[0, pl.ds(0, CLIP)], s.xs.at[0], load_sems.at[0]),
        pltpu.make_async_copy(win_hbm.at[0, :, pl.ds(0, 3 * D)], s.win.at[:, pl.ds(0, 3 * D)], load_sems.at[1]),
        pltpu.make_async_copy(
            win_hbm.at[0, :, pl.ds(3 * D, D + FF)], s.win.at[:, pl.ds(3 * D, D + FF)], load_sems.at[2]
        ),
        pltpu.make_async_copy(wdn_hbm.at[0], s.wdn, load_sems.at[3]),
        pltpu.make_async_copy(x_hbm.at[0, pl.ds(CLIP, CLIP)], s.xs.at[1], load_sems.at[4]),
    ]
    averages = [
        pltpu.make_async_copy(avgin_hbm.at[0], s.avi, load_sems.at[7]),
        pltpu.make_async_copy(avgdn_hbm.at[0], s.avd, load_sems.at[8]),
    ]
    for load in loads + averages:
        load.start()

    rows_i = iota((256, 256), 0)
    cols_i = iota((256, 256), 1)
    same = ((rows_i >> 6) == (cols_i >> 6)).astype(F32)
    s.bdf[...] = same * SCALE
    s.bd1[...] = same.astype(BF)
    s.bds[...] = (same * SCALE).astype(BF)
    for c in range(2):
        code_row = jnp.concatenate([codes_ref[4 * c + k : 4 * c + k + 1, :] for k in range(4)], axis=1)
        s.cds[c] = jnp.broadcast_to(code_row, (8, CLIP))

    proj_t = proj_ref[...]
    gain_one = gains_ref[0, 0:1, :].astype(F32)
    gain_two = gains_ref[0, 1:2, :].astype(F32)
    book = book_ref[...].astype(F32)
    empty = jnp.zeros((8, 64), F32)
    s.pre[sec, core] = jnp.where(
        is_e, jnp.concatenate([book, empty], axis=1), jnp.concatenate([empty, book], axis=1)
    )
    s.gacc[...] = jnp.zeros((2, 8, D), F32)
    s.s_acc[...] = jnp.zeros((4, 8, 2, 8, 128), F32)

    def book_start():
        pl.semaphore_wait(barrier, len(plane_dev + near_dev) + sec * len(wide))
        mine = s.pre.at[sec, core]

        @pl.when(is_e)
        def _():
            rcopy("ag0", mine, mine, sec_dev).start()
            rcopy("ag1", mine, mine, sec_core_dev).start()

        @pl.when(is_d)
        def _():
            rcopy("ag2", mine, mine, core_dev).start()

    def gather_book_start():
        chip = dp // 2
        rcopy("ag0", s.pre.at[0, core], s.pre.at[0, core], sec_dev).wait_recv()
        rcopy("ag1", s.pre.at[0, 1 - core], s.pre.at[0, 1 - core], sec_core_dev).wait_recv()
        rcopy("ag2", s.pre.at[1, 1 - core], s.pre.at[1, 1 - core], core_dev).wait_recv()
        s.tbl[chip] = jnp.concatenate([s.pre[0, 0] + s.pre[1, 0], s.pre[0, 1] + s.pre[1, 1]], axis=0).astype(BF)
        part = s.tbl.at[chip]
        for n in range(31):
            rcopy("ag3%d" % n, part, part, far_dev[n]).start()

    def gather_book_wait():
        for n, (i, j, y) in enumerate(far):
            part = s.tbl.at[(((z + 4 - i) % 4) * 4 + (x + 4 - j) % 4) * 2 + (yh + 2 - y) % 2]
            rcopy("ag3%d" % n, part, part, far_dev[n]).wait_recv()

    def book_finish():
        mine = s.pre.at[sec, core]

        @pl.when(is_e)
        def _():
            rcopy("ag0", mine, mine, sec_dev).wait_send()
            rcopy("ag1", mine, mine, sec_core_dev).wait_send()

        @pl.when(is_d)
        def _():
            rcopy("ag2", mine, mine, core_dev).wait_send()
            part = s.tbl.at[dp // 2]
            for n in range(31):
                rcopy("ag3%d" % n, part, part, far_dev[n]).wait_send()

    def onehots(c, half, shift):
        code_row = s.cds[c][0:1, :] - half * HALF
        hi = code_row >> 6
        lo = code_row & 63
        lo_one = (iota((128, CLIP), 0) == lo + shift).astype(F32).astype(BF)
        hi_mask = (iota((CLIP, CLIP), 0) >> 3) == hi
        return lo_one, hi_mask

    def entries(c):
        for half in range(2):
            lo_one, hi_mask = onehots(c, half, 64 * half)
            table = s.tbl[...].reshape(CLIP, 128)
            picked = jnp.where(hi_mask, nn(table, lo_one), 0.0)
            s.ent[c, half] = jnp.sum(picked.reshape(64, 8, CLIP), axis=0)

    def total(parts):
        parts = [v.astype(F32) for v in parts]
        while len(parts) > 1:
            parts = [a + b for a, b in zip(parts[::2], parts[1::2])] + parts[len(parts) // 2 * 2 :]
        return parts[0]

    def pad16(v):
        return jnp.concatenate([v, jnp.zeros((8, v.shape[1]), F32)], axis=0).astype(BF)

    def book_proj_terms(c, code_grad, wide_rows, narrow):
        lo_one, hi_mask = onehots(c, sec, 0)
        spread = jnp.broadcast_to(code_grad[None], (64, 8, CLIP)).reshape(CLIP, CLIP)
        left = jnp.where(hi_mask, spread, 0.0).astype(BF)
        total = nt(left, lo_one)
        narrow_wide = jnp.concatenate(
            [jnp.zeros((64, CLIP), F32), narrow, jnp.zeros((56, CLIP), F32)], axis=0
        ).astype(BF)
        total = total + tt(wide_rows, narrow_wide)
        s.s_acc[...] += total.reshape(4, 8, 2, 8, 128)

    def norm_qkv(c, parts):
        halves = [slice(0, 256), slice(256, 512)]
        a = []
        for rows, h in zip(halves, parts):
            s.hb[rows] = h
            xh, r = normed(h)
            s.xh1[c, rows] = xh
            s.r1[c, rows] = r
            a.append((xh * gain_one).astype(BF))
            s.a1[c, rows] = a[-1]
        for j in range(3):
            for rows, v in zip(halves, a):
                s.qkv[c, rows, 512 * j : 512 * j + 512] = nn(v, s.win[:, 512 * j : 512 * j + 512]).astype(BF)

    def feed_forward(c, put, ahead=False):
        m = s.hb[...] + nn(s.att[c], s.win[:, 1536:2048])
        xh, r = normed(m)
        s.xh2[c] = xh
        s.r2[c] = r
        a = (xh * gain_two).astype(BF)
        s.a2[c] = a
        acc = m
        nxt = nn(a, s.win[:, 2048:2304])
        for j in range(8):
            cols = slice(256 * j, 256 * j + 256)
            u = nxt
            if j < 7:
                nxt = nn(a, s.win[:, 2304 + 256 * j : 2560 + 256 * j])
            value, slope = gelu_pair(u.astype(BF))
            s.act[c, :, cols] = value
            s.gel[c, :, cols] = s.gel[c, :, cols] * slope if ahead else slope
            acc = acc + nn(value, s.wdn[cols, :])
        put(acc)

    def units(c, w, count):
        out = []
        for n in range(count):
            rows = pl.ds((w * count + n) * WINDOW, WINDOW)
            for quad in range(2):
                out.append((rows, 256 * quad))
        return out

    def widened(v, mask):
        return jnp.concatenate([v] * 4, axis=0) * mask

    def heads_of(wide):
        return (wide[0:64] + wide[64:128]) + (wide[128:192] + wide[192:256])

    def window_forward(c, w):
        if True:
            us = units(c, w, WB)
            bds = s.bds[...]
            bdf = s.bdf[...]
            q = [s.qkv[c, r, o : o + 256] for r, o in us]
            k = [s.qkv[c, r, 512 + o : 768 + o] for r, o in us]
            v = [s.qkv[c, r, 1024 + o : 1280 + o] for r, o in us]
            scores = [nt(kk, widened(qq, bds)) for kk, qq in zip(k, q)]
            e = [jnp.exp(x - jnp.max(x, axis=0, keepdims=True)) for x in scores]
            p = [x * (1.0 / jnp.sum(x, axis=0, keepdims=True)) for x in e]
            wide = [tn(x.astype(BF), vv) for x, vv in zip(p, v)]
            att = [(heads_of(x * bdf) * (1.0 / SCALE)).astype(BF) for x in wide]
            for (r, o), pp, aa in zip(us, p, att):
                s.prob[c, r, o : o + 256] = pp
                s.att[c, r, o : o + 256] = aa

    def window_backward(c, w):
        if True:
            us = units(c, w, WB)
            bds = s.bds[...]
            bd1 = s.bd1[...]
            bdf = s.bdf[...]
            q = [s.qkv[c, r, o : o + 256] for r, o in us]
            k = [s.qkv[c, r, 512 + o : 768 + o] for r, o in us]
            v = [s.qkv[c, r, 1024 + o : 1280 + o] for r, o in us]
            go = [widened(s.gob[r, o : o + 256], bd1) for r, o in us]
            p = [s.prob[c, r, o : o + 256] for r, o in us]
            gp = [nt(vv, gg) for vv, gg in zip(v, go)]
            gv = [nn(pp.astype(BF), gg).astype(BF) for pp, gg in zip(p, go)]
            gs = [
                (pp * (x - jnp.sum(x * pp, axis=0, keepdims=True))).astype(BF)
                for pp, x in zip(p, gp)
            ]
            gk = [nn(x, widened(qq, bds)).astype(BF) for x, qq in zip(gs, q)]
            gq = [heads_of(tn(x, kk) * bdf).astype(BF) for x, kk in zip(gs, k)]
            for (r, o), a, b, d in zip(us, gq, gk, gv):
                s.qkv[c, r, o : o + 256] = a
                s.qkv[c, r, 512 + o : 768 + o] = b
                s.qkv[c, r, 1024 + o : 1280 + o] = d

    def head_sums(v):
        return nn(v, s.bd1[...])

    CR = 256

    def frames_forward(c):
        late0 = orders_ref[c, 0] > orders_ref[c, 1]
        sign = jnp.where(late0, 1.0, -1.0).astype(F32)
        r0 = slice(0, GRID)
        r1 = slice(GRID, CLIP)
        for quad in range(2):
            qc = slice(256 * quad, 256 * quad + 256)
            kc = slice(512 + 256 * quad, 768 + 256 * quad)
            vc = slice(1024 + 256 * quad, 1280 + 256 * quad)
            q_late = jnp.where(late0, s.qkv[c, r0, qc], s.qkv[c, r1, qc])
            k_diff = s.qkv[c, r1, kc] - s.qkv[c, r0, kc]
            v0 = s.qkv[c, r0, vc]
            v1 = s.qkv[c, r1, vc]
            d = head_sums(q_late * k_diff) * (sign * SCALE)
            e = jnp.exp(-jnp.abs(d))
            big = 1.0 / (1.0 + e)
            small = e * big
            p_other = jnp.where(d > 0.0, big, small)
            p_self = jnp.where(d > 0.0, small, big)
            s.prob[c, r0, qc] = p_other
            s.prob[c, r1, qc] = p_self
            p0 = jnp.where(late0, p_self, p_other).astype(BF)
            p1 = jnp.where(late0, p_other, p_self).astype(BF)
            mix = (p0.astype(F32) * v0.astype(F32) + p1.astype(F32) * v1.astype(F32)).astype(BF)
            s.att[c, r0, qc] = jnp.where(late0, mix, v0)
            s.att[c, r1, qc] = jnp.where(late0, v1, mix)

    def frames_backward(c):
        late0 = orders_ref[c, 0] > orders_ref[c, 1]
        r0 = slice(0, GRID)
        r1 = slice(GRID, CLIP)
        for quad in range(2):
            qc = slice(256 * quad, 256 * quad + 256)
            kc = slice(512 + 256 * quad, 768 + 256 * quad)
            vc = slice(1024 + 256 * quad, 1280 + 256 * quad)
            q_late = jnp.where(late0, s.qkv[c, r0, qc], s.qkv[c, r1, qc])
            k_diff = s.qkv[c, r1, kc] - s.qkv[c, r0, kc]
            v_diff = s.qkv[c, r1, vc] - s.qkv[c, r0, vc]
            go0 = s.gob[r0, qc]
            go1 = s.gob[r1, qc]
            go_late = jnp.where(late0, go0, go1)
            go_early = jnp.where(late0, go1, go0)
            p_other = s.prob[c, r0, qc]
            p_self = s.prob[c, r1, qc]
            gs = (p_other * p_self * head_sums(go_late * v_diff)).astype(BF).astype(F32) * SCALE
            gq = (gs * k_diff.astype(F32)).astype(BF)
            gk = gs * q_late.astype(F32)
            late32 = go_late.astype(F32)
            gv_late = (p_self.astype(BF).astype(F32) * late32).astype(BF)
            gv_early = (go_early.astype(F32) + p_other.astype(BF).astype(F32) * late32).astype(BF)
            none = jnp.zeros_like(gq)
            s.qkv[c, r0, qc] = jnp.where(late0, gq, none)
            s.qkv[c, r1, qc] = jnp.where(late0, none, gq)
            s.qkv[c, r0, kc] = (-gk).astype(BF)
            s.qkv[c, r1, kc] = gk.astype(BF)
            s.qkv[c, r0, vc] = jnp.where(late0, gv_late, gv_early)
            s.qkv[c, r1, vc] = jnp.where(late0, gv_early, gv_late)

    def gain_terms(which, grad, xhat):
        part = jnp.sum((grad * xhat).reshape(-1, 8, D), axis=0)
        s.gacc[which] += part

    def back_down_codes(c):
        twice = jnp.concatenate([s.cvec[c][0:8].astype(F32)] * 2, axis=0).astype(BF)
        for j in range(4):
            cols = slice(512 * j, 512 * j + 512)
            s.gel[c, :, cols] = (tn(twice, s.m8[:, cols]) * s.gel[c, :, cols].astype(F32)).astype(BF)

    def back_up(c, grad_of):
        acc = None
        for j in range(4):
            term = nt(s.gel[c, :, 512 * j : 512 * j + 512], s.win[:, 2048 + 512 * j : 2560 + 512 * j])
            acc = term if acc is None else acc + term
        xh = s.xh2[c]
        gain_terms(1, acc, xh)
        gm = grad_of() + normed_back(acc, xh, s.r2[c], gain_two)
        s.hb[...] = gm
        gy = gm.astype(BF)
        s.gy[c] = gy
        s.gob[...] = nt(gy, s.win[:, 1536:2048]).astype(BF)

    def back_in(c):
        acc = None
        for j in range(3):
            cols = slice(512 * j, 512 * j + 512)
            term = nt(s.qkv[c, :, cols], s.win[:, cols])
            acc = term if acc is None else acc + term
        xh = s.xh1[c]
        gain_terms(0, acc, xh)
        return s.hb[...] + normed_back(acc, xh, s.r1[c], gain_one)

    def add_into(ref, rows, cols, c, value):
        ref[rows, cols] = jnp.where(c == 0, value, ref[rows, cols] + value)

    def grad_down(c):
        for j in range(4):
            cols = slice(512 * j, 512 * j + 512)
            add_into(s.acc_dn, cols, slice(None), c, tn(s.act[c, :, cols], s.xs[c]))

    def grad_down_codes(c):
        code = s.cvec[c][0:8].astype(F32)
        wide = jnp.concatenate([jnp.zeros((80, CLIP), F32)] + [code] * 4 + [jnp.zeros((16, CLIP), F32)], axis=0)
        wide = wide.astype(BF)
        lanes = (iota((8, 128), 1) >> 3) - 10
        for j in range(4):
            v = tt(s.act[c, :, 512 * j : 512 * j + 512], wide).reshape(16, 4, 8, 128)
            picked = [jnp.where(lanes == m, v[:, m], 0.0) for m in range(4)]
            s.s_acc[j] += total(picked).reshape(8, 2, 8, 128)

    def grad_qkv_codes(c):
        norm_row = jnp.transpose(jnp.broadcast_to(s.r1[c], (CLIP, 128)))[0:1, :]
        part = nn(pad16(s.cvec[c][0:8].astype(F32) * norm_row), s.qkv[c])[0:8]
        for half in range(2):
            v = part[:, 768 * half : 768 * half + 768]
            s.q8[half] = jnp.where(c == 0, v, s.q8[half] + v)

    def grad_up(c):
        for j in range(4):
            cols = slice(512 * j, 512 * j + 512)
            add_into(s.acc_up, slice(None), cols, c, tn(s.a2[c], s.gel[c, :, cols]))

    def grad_out(c):
        add_into(s.acc_out, slice(None), slice(None), c, tn(s.att[c], s.gy[c]))

    def grad_attn(c):
        for j in range(3):
            cols = slice(512 * j, 512 * j + 512)
            add_into(s.acc_qkv, slice(None), cols, c, tn(s.a1[c], s.qkv[c, :, cols]))

    def share(k, i, to_core):
        n = 2 * i + to_core
        if k == "a":
            return s.acc_dn[pl.ds(pl.multiple_of(n * 32, 32), 32), :]
        rows = pl.ds(pl.multiple_of(n * 8, 8), 8)
        ref, w = {"b": (s.acc_up, 1024), "c": (s.acc_qkv, 768), "o": (s.acc_out, 256)}[k]
        return jnp.concatenate([ref[rows, 0:w], ref[rows, w : 2 * w]], axis=0)

    def buf(name, k):
        return getattr(s, name + k)

    def copies(k, step):
        if k == "s":
            if step == 0:
                return [rcopy("s0", s.s_acc.at[:, :, 1 - core], s.s0, core_dev)]
            if step == 1:
                return [rcopy("s1%d" % i, s.s0.at[(z + 1 + i) % 4], s.s1.at[i], z_dev[i]) for i in range(3)]
            return [
                rcopy(
                    "s2%d" % i, s.s0.at[z, 2 * ((x + d) % 4) + (yh + y) % 2], s.s2.at[i], xy_dev[i]
                )
                for i, (d, y) in enumerate(around)
            ]
        if k == "q":
            if step == 0:
                return [rcopy("q0", s.q8.at[1 - core], s.q0, core_dev)]
            if step == 1:
                return [rcopy("q1%d" % i, s.qs1, s.qz.at[i], z_dev[i]) for i in range(3)]
            if step == 2:
                return [rcopy("q2%d" % i, s.qs2, s.qx.at[i], x_dev[i]) for i in range(3)]
            if step == 3:
                return [rcopy("q3", s.qs3, s.qy, y_dev)]
            return [rcopy("q4", s.qs4, s.qg, core_dev)]
        rows, w = CHUNKS[k]
        h = w // 2
        r0 = buf("r0", k)
        if step == 0:
            return [rcopy(k + "0", buf("sb0", k), r0, core_dev)]
        lo, hi = pl.ds(0, h), pl.ds(h, h)
        out = []
        if step == 4:
            for i, (d, y) in enumerate(around):
                out.append(
                    rcopy(
                        "%s4x%d" % (k, i), r0.at[z, (x + d) % 4, (yh + y) % 2, :, lo],
                        buf("px", k).at[i], xy_dev[i],
                    )
                )
                out.append(
                    rcopy(
                        "%s4z%d" % (k, i), r0.at[(z + d) % 4, x, (yh + y) % 2, :, hi],
                        buf("pz", k).at[i], zy_dev[i],
                    )
                )
            return out
        for y in range(2):
            first, second = ((1, 3), (3, 1))[y]
            hop = second if step == 3 else first
            block = {1: 2, 2: first, 3: second}[step]
            slot = {1: "q1", 2: "q0", 3: "q2"}[step]
            out.append(
                rcopy(
                    "%s%dz%d" % (k, step, y), r0.at[z_flip[block], :, y, :, lo],
                    buf(slot + "z", k).at[y], place(z_flip[hop], x, yh, core),
                )
            )
            out.append(
                rcopy(
                    "%s%dx%d" % (k, step, y), r0.at[:, x_flip[block], y, :, hi],
                    buf(slot + "x", k).at[y], place(z, x_flip[hop], yh, core),
                )
            )
        return out

    def arrived(k, step):
        for cp in copies(k, step):
            cp.wait_recv()

    def send(k, step):
        for cp in copies(k, step):
            cp.start()

    def put_down(mine):
        gdn_ref[0] = mine
        piece = s.wdn[pl.ds(dp * 32, 32), :].astype(F32)
        adn_ref[0] = AVG_DECAY * s.avd[...] + (1.0 - AVG_DECAY) * (piece - LEARN_RATE * mine)

    def reduce_step(k, step):
        if k == "s":
            if step > 0:
                arrived(k, step - 1)
            if step == 1:
                s.s0[...] += s.s_acc[:, :, core]
            elif step == 2:
                s.s0[z] += (s.s1[0] + s.s1[1]) + s.s1[2]
            elif step == 3:
                small = total([s.s0[z, 2 * x + yh]] + [s.s2[i] for i in range(7)])
                small_ref[...] = small

                @pl.when(is_e)
                def _():
                    narrow = proj_t.astype(F32)
                    shares = [
                        total([small[:, n : n + 1] * narrow[n % 8 : n % 8 + 1, :] for n in range(80 + 8 * m, 88 + 8 * m)])
                        for m in range(4)
                    ]
                    put_down(jnp.concatenate(shares, axis=0))

                return
            send(k, step)
            return
        if k == "q":
            if step > 0:
                arrived(k, step - 1)
            if step == 1:
                s.qs1[...] = s.q8[core] + s.q0[...]
            elif step == 2:
                s.qs2[...] = total([s.qs1[...]] + [s.qz[i] for i in range(3)])
            elif step == 3:
                s.qs3[...] = total([s.qs2[...]] + [s.qx[i] for i in range(3)])
            elif step == 4:
                s.qs4[...] = s.qs3[...] + s.qy[...]
            elif step == 5:
                mine, other = s.qs4[...], s.qg[...]
                narrow = s.pgt[pl.ds(pl.multiple_of(dp * 8, 8), 8), :]
                for half, v in enumerate((jnp.where(core == 0, mine, other), jnp.where(core == 0, other, mine))):
                    gin_ref[0, :, 768 * half : 768 * half + 768] = total(
                        [narrow[:, n : n + 1] * v[n : n + 1, :] for n in range(8)]
                    )
                return
            send(k, step)
            return
        rows, w = CHUNKS[k]
        h = w // 2
        r0 = buf("r0", k)
        lo, hi = pl.ds(0, h), pl.ds(h, h)
        if step == 0:
            sb0 = buf("sb0", k)

            def body(i, carry):
                for y in range(2):
                    sb0[i // 4, i % 4, y] = share(k, 2 * i + y, 1 - core).astype(BF)
                return carry

            lax.fori_loop(0, 16, body, 0)
            send(k, 0)
        elif step == 1:
            arrived(k, 0)

            def body(i, carry):
                for y in range(2):
                    r0[i // 4, i % 4, y] = total([share(k, 2 * i + y, core), r0[i // 4, i % 4, y]]).astype(BF)
                return carry

            lax.fori_loop(0, 16, body, 0)
            send(k, 1)
            send(k, 2)
        elif step == 2:
            arrived(k, 1)
            for y in range(2):
                second = (3, 1)[y]
                zb, xb = z_flip[second], x_flip[second]
                r0[zb, :, y, :, lo] = total([r0[zb, :, y, :, lo], buf("q1z", k)[y]]).astype(BF)
                r0[:, xb, y, :, hi] = total([r0[:, xb, y, :, hi], buf("q1x", k)[y]]).astype(BF)
            send(k, 3)
        elif step == 3:
            arrived(k, 2)
            arrived(k, 3)
            for y in range(2):
                r0[z, :, y, :, lo] = total(
                    [r0[z, :, y, :, lo], buf("q0z", k)[y], buf("q2z", k)[y]]
                ).astype(BF)
                r0[:, x, y, :, hi] = total(
                    [r0[:, x, y, :, hi], buf("q0x", k)[y], buf("q2x", k)[y]]
                ).astype(BF)
            send(k, 4)
        else:
            arrived(k, 4)
            left = total([r0[z, x, yh, :, lo]] + [buf("px", k)[i] for i in range(7)])
            right = total([r0[z, x, yh, :, hi]] + [buf("pz", k)[i] for i in range(7)])
            mine = jnp.concatenate([left, right], axis=1)
            if k == "a":
                put_down(mine)
            else:
                first = {"b": 2048, "c": 0, "o": 1536}[k]
                gin_ref[0, :, first : first + w] = mine[0:8]
                gin_ref[0, :, first + w : first + 2 * w] = mine[8:16]

    def add_gains():
        sums = jnp.concatenate(
            [
                jnp.sum(s.gacc[0], axis=0, keepdims=True),
                jnp.sum(s.gacc[1], axis=0, keepdims=True),
                jnp.zeros((6, D), F32),
            ],
            axis=0,
        )
        wide_sums = jnp.concatenate([jnp.zeros((72, D), F32), sums, jnp.zeros((48, D), F32)], axis=0)
        s.s_acc[...] += jnp.transpose(wide_sums).reshape(4, 8, 2, 8, 128)

    def code_copy(c):
        return pltpu.make_async_remote_copy(
            src_ref=s.fcs.at[c], dst_ref=s.fcr.at[c], send_sem=send_sems.at[N_SEM - 2 + c],
            recv_sem=recv_sems.at[N_SEM - 2 + c], device_id=sec_dev, device_id_type=MESH,
        )

    def grad_copy(c):
        return pltpu.make_async_remote_copy(
            src_ref=s.cxs.at[c], dst_ref=s.cxr.at[c], send_sem=send_sems.at[N_SEM - 4 + c],
            recv_sem=recv_sems.at[N_SEM - 4 + c], device_id=sec_dev, device_id_type=MESH,
        )

    @pl.when(is_e)
    def _():
        for c in range(2):
            grid_now = grids_ref[c]
            width = jnp.where(grid_now == 0, 16, jnp.where(grid_now == 1, 32, 8)).astype(I32)
            log_across = jnp.where(grid_now == 0, 1, jnp.where(grid_now == 1, 2, 0)).astype(I32)
            across_mask = jnp.where(grid_now == 0, 1, jnp.where(grid_now == 1, 3, 0)).astype(I32)
            window_no = rows_i >> 6
            inner = rows_i & 63
            source = (
                ((window_no >> log_across) * 8 + (inner >> 3)) * width
                + (window_no & across_mask) * 8
                + (inner & 7)
            )
            s.perm[c] = (source == cols_i).astype(F32).astype(BF)
        loads[0].wait()
        loads[1].wait()

        def forward(c, carry):
            @pl.when(c == 1)
            def _():
                loads[4].wait()

            raster = [s.xs[c, 0:GRID], s.xs[c, GRID:CLIP]]
            @pl.when(c == 0)
            def _():
                book_start()

            norm_qkv(c, [nn(s.perm[c], v) for v in raster])

            window_forward(c, 0)
            window_forward(c, 1)

            @pl.when(c == 0)
            def _():
                loads[2].wait()
                loads[3].wait()

            def put(acc):
                s.eb[c] = acc.astype(BF)

            feed_forward(c, put)
            vec = nt(proj_t, s.eb[c])
            hi = vec.astype(BF).astype(F32)
            mid = (vec - hi).astype(BF).astype(F32)
            parts = jnp.concatenate([hi, mid, vec - hi - mid, jnp.zeros((8, CLIP), F32)], axis=0).astype(BF)
            for f in range(2):
                cols = slice(GRID * f, GRID * f + GRID)
                moved = nn(parts[:, cols], s.perm[c])
                s.fcs[c, :, cols] = (moved[0:8] + moved[8:16]) + moved[16:24]
            code_copy(c).start()
            return carry

        lax.fori_loop(0, 2, forward, 0)
        for j in range(4):
            cols = slice(512 * j, 512 * j + 512)
            m = nt(proj_t, s.wdn[cols, :])
            hi = m.astype(BF).astype(F32)
            s.m8[:, cols] = jnp.concatenate([hi, m - hi], axis=0).astype(BF)

    @pl.when(is_d)
    def _():
        book_start()
        gather_book_start()
        for load in loads:
            load.wait()

        def ahead(c, carry):
            for j in range(4):
                cols = slice(512 * j, 512 * j + 512)
                s.gel[c, :, cols] = nt(s.xs[c], s.wdn[cols, :]).astype(BF)
            return carry

        lax.fori_loop(0, 2, ahead, 0)
        narrow = proj_t.astype(F32)
        narrow = (narrow - jnp.mean(narrow, axis=-1, keepdims=True)) * gain_one
        s.pgt[...] = jnp.transpose(jnp.concatenate([narrow, jnp.zeros((120, D), F32)], axis=0))
        gather_book_wait()

        def both(c, carry):
            entries(c)
            code_copy(c).wait_recv()
            sent = (s.fcr[c] + s.ent[c, 0]).astype(BF).astype(F32)
            s.cvec[c] = pad16(sent + s.ent[c, 1])
            norm_qkv(c, [tn(s.cvec[c][0:8, 0:256], proj_t), tn(s.cvec[c][0:8, 256:512], proj_t)])
            frames_forward(c)

            def put(acc):
                s.bo[pl.ds(c * CLIP, CLIP), :] = acc.astype(BF)

            feed_forward(c, put, ahead=True)
            bout_copy(c).start()
            back_up(c, lambda: s.xs[c].astype(F32))
            frames_backward(c)
            s.eb[c] = back_in(c).astype(BF)
            s.cxs[c] = pad16(nt(proj_t, s.eb[c]))
            grad_copy(c).start()
            return carry

        lax.fori_loop(0, 2, both, 0)

        def downs(c, carry):
            grad_down(c)
            return carry

        def ups(c, carry):
            grad_up(c)
            return carry

        def outs(c, carry):
            grad_out(c)
            return carry

        def codes_of(c, carry):
            grad_qkv_codes(c)
            return carry

        def books(c):
            book_proj_terms(c, s.cxs[c][0:8].astype(F32), s.eb[c], s.cvec[c][0:8].astype(F32))

        lax.fori_loop(0, 2, downs, 0)
        reduce_step("a", 0)
        lax.fori_loop(0, 2, ups, 0)
        reduce_step("b", 0)
        reduce_step("a", 1)
        lax.fori_loop(0, 2, outs, 0)
        reduce_step("o", 0)
        books(0)
        reduce_step("o", 1)
        reduce_step("b", 1)
        books(1)
        reduce_step("a", 2)
        add_gains()
        lax.fori_loop(0, 2, codes_of, 0)
        for load in averages:
            load.wait()
        for item in ["q0", "s0", "q1", "b2", "o2", "a3", "s1", "q2", "b3", "o3", "s2", "q3", "a4", "q4", "o4", "s3", "b4", "q5"]:
            reduce_step(item[0], int(item[1]))

    @pl.when(is_e)
    def _():
        def backward(c, carry):
            grad_copy(c).wait_recv()
            for f in range(2):
                cols = slice(GRID * f, GRID * f + GRID)
                s.cvec[c, :, cols] = nt(s.cxr[c, :, cols], s.perm[c]).astype(BF)
            g = tn(s.cvec[c][0:8], proj_t)
            s.hb[...] = g
            back_down_codes(c)
            grad_up(c)

            @pl.when(c == 1)
            def _():
                reduce_step("b", 0)

            back_up(c, lambda: s.hb[...])
            window_backward(c, 0)

            @pl.when(c == 1)
            def _():
                reduce_step("b", 1)

            window_backward(c, 1)
            grad_attn(c)

            @pl.when(c == 1)
            def _():
                reduce_step("c", 0)
                reduce_step("b", 2)

            grad_out(c)

            @pl.when(c == 1)
            def _():
                reduce_step("o", 0)
                reduce_step("c", 1)

            s.a2[c] = back_in(c).astype(BF)
            return carry

        lax.fori_loop(0, 2, backward, 0)
        reduce_step("o", 1)

        def leave(c, carry):
            for f in range(2):
                back = tn(s.perm[c], s.a2[c, GRID * f : GRID * f + GRID])
                s.bo[pl.ds(c * CLIP + GRID * f, GRID), :] = back.astype(BF)
            bout_copy(c).start()
            book_proj_terms(c, s.cxr[c][0:8].astype(F32), s.eb[c], s.cvec[c][0:8].astype(F32))
            return carry

        lax.fori_loop(0, 2, leave, 0)
        reduce_step("c", 2)
        reduce_step("b", 3)

        def downs(c, carry):
            grad_down_codes(c)
            return carry

        lax.fori_loop(0, 2, downs, 0)
        add_gains()
        for load in averages:
            load.wait()
        for item in ["o2", "s0", "s1", "c3", "o3", "s2", "c4", "b4", "o4", "s3"]:
            reduce_step(item[0], int(item[1]))

    half_rows = s.win[pl.ds(16 * (dp // 2), 16), :].astype(F32)
    piece = jnp.where(core == 0, half_rows[0:8], half_rows[8:16])
    ain_ref[0] = AVG_DECAY * s.avi[...] + (1.0 - AVG_DECAY) * (piece - LEARN_RATE * gin_ref[0])

    for c in range(2):
        bout_copy(c).wait()

        @pl.when(is_e)
        def _():
            code_copy(c).wait_send()

        @pl.when(is_d)
        def _():
            grad_copy(c).wait_send()

    book_finish()
    def finish(chunks):
        for k in chunks:
            for step in {"s": (0, 1, 2)}.get(k, (0, 1, 2, 3, 4)):
                for cp in copies(k, step):
                    cp.wait_send()

    @pl.when(is_e)
    def _():
        finish("bcos")

    @pl.when(is_d)
    def _():
        finish("abosq")


def body(
    boundary, in_weights, down_weight, gains, proj, codebook, codes, grids, orders, avg_in, avg_down
):
    vmem = pl.BlockSpec(memory_space=pltpu.VMEM)
    smem = pl.BlockSpec(memory_space=pltpu.SMEM)
    hbm = pl.BlockSpec(memory_space=pl.ANY)
    outs = (
        jax.ShapeDtypeStruct(boundary.shape, BF),
        jax.ShapeDtypeStruct(avg_in.shape, F32),
        jax.ShapeDtypeStruct(avg_down.shape, F32),
        jax.ShapeDtypeStruct((8, 128), F32),
        jax.ShapeDtypeStruct(avg_in.shape, F32),
        jax.ShapeDtypeStruct(avg_down.shape, F32),
    )
    scratch = [pltpu.VMEM(shape, dtype) for shape, dtype in SHAPES.values()]
    scratch += [pltpu.SemaphoreType.DMA((N_SEM,)), pltpu.SemaphoreType.DMA((N_SEM,)), pltpu.SemaphoreType.DMA((9,))]
    made = pl.pallas_call(
        mega,
        out_shape=outs,
        in_specs=[hbm, hbm, hbm, vmem, vmem, vmem, vmem, smem, smem, hbm, hbm],
        out_specs=[hbm] + [vmem] * 5,
        scratch_shapes=scratch,
        compiler_params=pltpu.CompilerParams(
            collective_id=0, has_side_effects=True, vmem_limit_bytes=63 << 20
        ),
        name="both_sections",
    )(
        boundary, in_weights, down_weight, gains, proj[0].T, codebook, codes.reshape(8, 128), grids, orders,
        avg_in, avg_down,
    )
    return pl.pallas_call(
        split_outputs,
        out_shape=(
            outs[0], outs[1], outs[2],
            jax.ShapeDtypeStruct((1, 2, 8), F32),
            jax.ShapeDtypeStruct((1, 8, 8), F32),
            jax.ShapeDtypeStruct(codebook.shape, F32),
            outs[4], outs[5],
        ),
        in_specs=[vmem] * 6,
        out_specs=[vmem] * 8,
        name="split_outputs",
    )(*made)


def split_outputs(
    bout_in, gin_in, gdn_in, small_in, ain_in, adn_in,
    bout, gin, gdn, ggain, gproj, gbook, ain, adn,
):
    bout[...] = bout_in[...]
    gin[...] = gin_in[...]
    gdn[...] = gdn_in[...]
    ain[...] = ain_in[...]
    adn[...] = adn_in[...]
    small = small_in[...]
    gbook[...] = small[:, 0:64]
    gproj[0] = small[:, 64:72]
    ggain[0] = jnp.transpose(jnp.concatenate([small] * 16, axis=0))[72:74, 0:8]


def solution(mesh):
    placed = (
        P("section", "dp", None),
        P("section", None, None),
        P("section", None, None),
        P("section", None, None),
        P("section", None, None),
        P(None, ("section", "dp")),
        P("dp"),
        P("dp"),
        P("dp", None),
        P("section", "dp", None),
        P("section", "dp", None),
    )
    return jax.shard_map(
        body,
        mesh=mesh,
        in_specs=placed,
        out_specs=(
            P("section", "dp", None),
            P("section", "dp", None),
            P("section", "dp", None),
            P("section", None, "dp"),
            P("section", "dp", None),
            P(None, ("section", "dp")),
            P("section", "dp", None),
            P("section", "dp", None),
        ),
        check_vma=False,
    )
```

```python
import functools

import jax
import jax.numpy as jnp
from jax import lax
from jax.experimental import pallas as pl
from jax.experimental.pallas import tpu as pltpu
from jax.sharding import PartitionSpec as P

BF = jnp.bfloat16
F32 = jnp.float32
I32 = jnp.int32
MESH = pl.DeviceIdType.MESH

D = 512
FF = 2048
CLIP = 512
GRID = 256
WINDOW = 64
HALF = 4096
NORM_EPS = 1e-05
AVG_DECAY = 0.9
LEARN_RATE = 0.0005
SCALE = 0.125
WB = 4

CHUNKS = {"a": (32, 512), "b": (16, 1024), "c": (16, 768), "o": (16, 256)}


def nn(left, right):
    return lax.dot_general(left, right, (((1,), (0,)), ((), ())), preferred_element_type=F32)


def nt(left, right):
    return lax.dot_general(left, right, (((1,), (1,)), ((), ())), preferred_element_type=F32)


def tn(left, right):
    return lax.dot_general(left, right, (((0,), (0,)), ((), ())), preferred_element_type=F32)


def tt(left, right):
    return lax.dot_general(left, right, (((0,), (1,)), ((), ())), preferred_element_type=F32)


def iota(shape, axis):
    return lax.broadcasted_iota(I32, shape, axis)


def normed(h):
    mean = jnp.mean(h, axis=-1, keepdims=True)
    c = h - mean
    var = jnp.mean(c * c, axis=-1, keepdims=True)
    r = lax.rsqrt(var + NORM_EPS)
    return c * r, r


def normed_back(grad, xhat, r, gain):
    t = grad * gain
    m1 = jnp.mean(t, axis=-1, keepdims=True)
    m2 = jnp.mean(t * xhat, axis=-1, keepdims=True)
    return r * (t - m1 - xhat * m2)


def gelu_pair(u):
    c0 = 0.7978845608028654
    c1 = 0.7978845608028654 * 0.044715
    m = c1 * (u * u)
    half = 0.5 + 0.5 * jnp.tanh(u * (c0 + m))
    value = u * half
    slope = half + (value - value * half) * (2.0 * c0 + 6.0 * m)
    return value, slope


def ten_shapes():
    shapes = {
        "xs": ((2, CLIP, D), BF),
        "win": ((D, 4 * D + FF), BF),
        "wdn": ((FF, D), BF),
        "perm": ((2, GRID, GRID), BF),
        "bd1": ((256, 256), BF),
        "bds": ((256, 256), BF),
        "bdf": ((256, 256), F32),
        "tbl": ((32, 16, 128), BF),
        "pre": ((2, 2, 8, 128), F32),
        "cds": ((2, 8, CLIP), I32),
        "cxs": ((2, 16, CLIP), BF),
        "cxr": ((2, 16, CLIP), BF),
        "fcs": ((2, 8, CLIP), F32),
        "fcr": ((2, 8, CLIP), F32),
        "ent": ((2, 2, 8, CLIP), F32),
        "cvec": ((2, 16, CLIP), BF),
        "hb": ((CLIP, D), F32),
        "bo": ((2 * CLIP, D), BF),
        "m8": ((16, FF), BF),
        "pgt": ((D, 128), F32),
        "q8": ((2, 8, 768), F32),
        "q0": ((8, 768), F32),
        "qs1": ((8, 768), F32),
        "qz": ((3, 8, 768), F32),
        "qs2": ((8, 768), F32),
        "qx": ((3, 8, 768), F32),
        "qs3": ((8, 768), F32),
        "qy": ((8, 768), F32),
        "qs4": ((8, 768), F32),
        "qg": ((8, 768), F32),
        "avi": ((8, 4 * D + FF), F32),
        "avd": ((32, D), F32),
        "gob": ((CLIP, D), BF),
        "xh1": ((2, CLIP, D), F32),
        "xh2": ((2, CLIP, D), F32),
        "r1": ((2, CLIP, 1), F32),
        "r2": ((2, CLIP, 1), F32),
        "a1": ((2, CLIP, D), BF),
        "a2": ((2, CLIP, D), BF),
        "qkv": ((2, CLIP, 3 * D), BF),
        "prob": ((2, CLIP, D), F32),
        "att": ((2, CLIP, D), BF),
        "act": ((2, CLIP, FF), BF),
        "gel": ((2, CLIP, FF), BF),
        "gy": ((2, CLIP, D), BF),
        "eb": ((2, CLIP, D), BF),
        "acc_dn": ((FF, D), F32),
        "acc_up": ((D, FF), F32),
        "acc_qkv": ((D, 3 * D), F32),
        "acc_out": ((D, D), F32),
        "s_acc": ((4, 8, 2, 8, 128), F32),
        "gacc": ((2, 8, D), F32),
        "s0": ((4, 8, 8, 128), F32),
        "s1": ((3, 8, 8, 128), F32),
        "s2": ((7, 8, 128), F32),
    }
    for k, (rows, w) in CHUNKS.items():
        h = w // 2
        shapes["sb0" + k] = ((4, 4, 2, rows, w), BF)
        shapes["r0" + k] = ((4, 4, 2, rows, w), BF)
        for ax in "zx":
            for slot in "012":
                shapes["q" + slot + ax + k] = ((2, 4, rows, h), BF)
            shapes["p" + ax + k] = ((7, rows, h), BF)
    return shapes


SHAPES = ten_shapes()
N_SEM = 200


class Refs:
    pass


def mega(
    x_hbm, win_hbm, wdn_hbm, gains_ref, proj_ref, book_ref, codes_ref, grids_ref, orders_ref,
    avgin_hbm, avgdn_hbm,
    bout_hbm, gin_ref, gdn_ref, small_ref, ain_ref, adn_ref,
    *scratch,
):
    s = Refs()
    for name, ref in zip(SHAPES, scratch):
        setattr(s, name, ref)
    send_sems, recv_sems, load_sems = scratch[len(SHAPES):]

    sec = lax.axis_index("section")
    dp = lax.axis_index("dp")
    core = dp % 2
    yh = (dp // 2) % 2
    x = (dp // 4) % 4
    z = dp // 16
    is_e = sec == 0
    is_d = sec == 1

    def place(zz, xx, yy, cc):
        return (sec, ((zz * 4 + xx) * 2 + yy) * 2 + cc)

    core_dev = place(z, x, yh, 1 - core)
    y_dev = place(z, x, 1 - yh, core)
    def flips(v):
        return {1: v + 1 - 2 * (v % 2), 2: (v + 2) % 4, 3: 3 - v}

    z_flip, x_flip = flips(z), flips(x)
    z_dev = [place((z + d) % 4, x, yh, core) for d in (1, 2, 3)]
    x_dev = [place(z, (x + d) % 4, yh, core) for d in (1, 2, 3)]
    sec_dev = (1 - sec, dp)
    sec_core_dev = (1 - sec, dp + 1 - 2 * core)
    around = [(2, 1), (1, 1), (3, 1), (0, 1), (2, 0), (1, 0), (3, 0)]
    zy_dev = [place((z + d) % 4, x, (yh + y) % 2, core) for d, y in around]
    xy_dev = [place(z, (x + d) % 4, (yh + y) % 2, core) for d, y in around]

    counter = [0]
    slots = {}

    def rcopy(key, src, dst, dev):
        if key not in slots:
            slots[key] = counter[0]
            counter[0] += 1
        i = slots[key]
        return pltpu.make_async_remote_copy(
            src_ref=src, dst_ref=dst, send_sem=send_sems.at[i], recv_sem=recv_sems.at[i],
            device_id=dev, device_id_type=MESH,
        )

    def bout_copy(c):
        rows = pl.ds(c * CLIP, CLIP)
        return pltpu.make_async_copy(s.bo.at[rows], bout_hbm.at[0, rows], load_sems.at[5 + c])

    barrier = pltpu.get_barrier_semaphore()
    far = [(i, j, y) for i in range(4) for j in range(4) for y in range(2) if i + j + y > 0]
    far.sort(key=lambda p: -(min(p[0], 4 - p[0]) + min(p[1], 4 - p[1]) + 2 * p[2]))
    wide = [n for n, (i, j, y) in enumerate(far) if i > 0 and j > 0]
    far_dev = [place((z + i) % 4, (x + j) % 4, (yh + y) % 2, core) for i, j, y in far]
    plane_dev = [dev for n, dev in enumerate(far_dev) if n not in wide]
    near_dev = [sec_core_dev, sec_dev, core_dev]
    @pl.when(is_d)
    def _():
        for n in wide:
            pl.semaphore_signal(barrier, inc=1, device_id=far_dev[n], device_id_type=MESH)

    for dev in plane_dev + near_dev:
        pl.semaphore_signal(barrier, inc=1, device_id=dev, device_id_type=MESH)

    loads = [
        pltpu.make_async_copy(x_hbm.at[0, pl.ds(0, CLIP)], s.xs.at[0], load_sems.at[0]),
        pltpu.make_async_copy(win_hbm.at[0, :, pl.ds(0, 3 * D)], s.win.at[:, pl.ds(0, 3 * D)], load_sems.at[1]),
        pltpu.make_async_copy(
            win_hbm.at[0, :, pl.ds(3 * D, D + FF)], s.win.at[:, pl.ds(3 * D, D + FF)], load_sems.at[2]
        ),
        pltpu.make_async_copy(wdn_hbm.at[0], s.wdn, load_sems.at[3]),
        pltpu.make_async_copy(x_hbm.at[0, pl.ds(CLIP, CLIP)], s.xs.at[1], load_sems.at[4]),
    ]
    averages = [
        pltpu.make_async_copy(avgin_hbm.at[0], s.avi, load_sems.at[7]),
        pltpu.make_async_copy(avgdn_hbm.at[0], s.avd, load_sems.at[8]),
    ]
    for load in loads + averages:
        load.start()

    rows_i = iota((256, 256), 0)
    cols_i = iota((256, 256), 1)
    same = ((rows_i >> 6) == (cols_i >> 6)).astype(F32)
    s.bdf[...] = same * SCALE
    s.bd1[...] = same.astype(BF)
    s.bds[...] = (same * SCALE).astype(BF)
    for c in range(2):
        code_row = jnp.concatenate([codes_ref[4 * c + k : 4 * c + k + 1, :] for k in range(4)], axis=1)
        s.cds[c] = jnp.broadcast_to(code_row, (8, CLIP))

    proj_t = proj_ref[...]
    gain_one = gains_ref[0, 0:1, :].astype(F32)
    gain_two = gains_ref[0, 1:2, :].astype(F32)
    book = book_ref[...].astype(F32)
    empty = jnp.zeros((8, 64), F32)
    s.pre[sec, core] = jnp.where(
        is_e, jnp.concatenate([book, empty], axis=1), jnp.concatenate([empty, book], axis=1)
    )
    s.gacc[...] = jnp.zeros((2, 8, D), F32)
    s.s_acc[...] = jnp.zeros((4, 8, 2, 8, 128), F32)

    def book_start():
        pl.semaphore_wait(barrier, len(plane_dev + near_dev) + sec * len(wide))
        mine = s.pre.at[sec, core]

        @pl.when(is_e)
        def _():
            rcopy("ag0", mine, mine, sec_dev).start()
            rcopy("ag1", mine, mine, sec_core_dev).start()

        @pl.when(is_d)
        def _():
            rcopy("ag2", mine, mine, core_dev).start()

    def gather_book_start():
        chip = dp // 2
        rcopy("ag0", s.pre.at[0, core], s.pre.at[0, core], sec_dev).wait_recv()
        rcopy("ag1", s.pre.at[0, 1 - core], s.pre.at[0, 1 - core], sec_core_dev).wait_recv()
        rcopy("ag2", s.pre.at[1, 1 - core], s.pre.at[1, 1 - core], core_dev).wait_recv()
        s.tbl[chip] = jnp.concatenate([s.pre[0, 0] + s.pre[1, 0], s.pre[0, 1] + s.pre[1, 1]], axis=0).astype(BF)
        part = s.tbl.at[chip]
        for n in range(31):
            rcopy("ag3%d" % n, part, part, far_dev[n]).start()

    def gather_book_wait():
        for n, (i, j, y) in enumerate(far):
            part = s.tbl.at[(((z + 4 - i) % 4) * 4 + (x + 4 - j) % 4) * 2 + (yh + 2 - y) % 2]
            rcopy("ag3%d" % n, part, part, far_dev[n]).wait_recv()

    def book_finish():
        mine = s.pre.at[sec, core]

        @pl.when(is_e)
        def _():
            rcopy("ag0", mine, mine, sec_dev).wait_send()
            rcopy("ag1", mine, mine, sec_core_dev).wait_send()

        @pl.when(is_d)
        def _():
            rcopy("ag2", mine, mine, core_dev).wait_send()
            part = s.tbl.at[dp // 2]
            for n in range(31):
                rcopy("ag3%d" % n, part, part, far_dev[n]).wait_send()

    def onehots(c, half, shift):
        code_row = s.cds[c][0:1, :] - half * HALF
        hi = code_row >> 6
        lo = code_row & 63
        lo_one = (iota((128, CLIP), 0) == lo + shift).astype(F32).astype(BF)
        hi_mask = (iota((CLIP, CLIP), 0) >> 3) == hi
        return lo_one, hi_mask

    def entries(c):
        for half in range(2):
            lo_one, hi_mask = onehots(c, half, 64 * half)
            table = s.tbl[...].reshape(CLIP, 128)
            picked = jnp.where(hi_mask, nn(table, lo_one), 0.0)
            s.ent[c, half] = jnp.sum(picked.reshape(64, 8, CLIP), axis=0)

    def total(parts):
        parts = [v.astype(F32) for v in parts]
        while len(parts) > 1:
            parts = [a + b for a, b in zip(parts[::2], parts[1::2])] + parts[len(parts) // 2 * 2 :]
        return parts[0]

    def pad16(v):
        return jnp.concatenate([v, jnp.zeros((8, v.shape[1]), F32)], axis=0).astype(BF)

    def book_proj_terms(c, code_grad, wide_rows, narrow):
        lo_one, hi_mask = onehots(c, sec, 0)
        spread = jnp.broadcast_to(code_grad[None], (64, 8, CLIP)).reshape(CLIP, CLIP)
        left = jnp.where(hi_mask, spread, 0.0).astype(BF)
        total = nt(left, lo_one)
        narrow_wide = jnp.concatenate(
            [jnp.zeros((64, CLIP), F32), narrow, jnp.zeros((56, CLIP), F32)], axis=0
        ).astype(BF)
        total = total + tt(wide_rows, narrow_wide)
        s.s_acc[...] += total.reshape(4, 8, 2, 8, 128)

    def norm_qkv(c, parts):
        halves = [slice(0, 256), slice(256, 512)]
        a = []
        for rows, h in zip(halves, parts):
            s.hb[rows] = h
            xh, r = normed(h)
            s.xh1[c, rows] = xh
            s.r1[c, rows] = r
            a.append((xh * gain_one).astype(BF))
            s.a1[c, rows] = a[-1]
        for j in range(3):
            for rows, v in zip(halves, a):
                s.qkv[c, rows, 512 * j : 512 * j + 512] = nn(v, s.win[:, 512 * j : 512 * j + 512]).astype(BF)

    def feed_forward(c, put, ahead=False):
        m = s.hb[...] + nn(s.att[c], s.win[:, 1536:2048])
        xh, r = normed(m)
        s.xh2[c] = xh
        s.r2[c] = r
        a = (xh * gain_two).astype(BF)
        s.a2[c] = a
        acc = m
        nxt = nn(a, s.win[:, 2048:2304])
        for j in range(8):
            cols = slice(256 * j, 256 * j + 256)
            u = nxt
            if j < 7:
                nxt = nn(a, s.win[:, 2304 + 256 * j : 2560 + 256 * j])
            value, slope = gelu_pair(u.astype(BF))
            s.act[c, :, cols] = value
            s.gel[c, :, cols] = s.gel[c, :, cols] * slope if ahead else slope
            acc = acc + nn(value, s.wdn[cols, :])
        put(acc)

    def units(c, w, count):
        out = []
        for n in range(count):
            rows = pl.ds((w * count + n) * WINDOW, WINDOW)
            for quad in range(2):
                out.append((rows, 256 * quad))
        return out

    def widened(v, mask):
        return jnp.concatenate([v] * 4, axis=0) * mask

    def heads_of(wide):
        return (wide[0:64] + wide[64:128]) + (wide[128:192] + wide[192:256])

    def window_forward(c, w):
        if True:
            us = units(c, w, WB)
            bds = s.bds[...]
            bdf = s.bdf[...]
            q = [s.qkv[c, r, o : o + 256] for r, o in us]
            k = [s.qkv[c, r, 512 + o : 768 + o] for r, o in us]
            v = [s.qkv[c, r, 1024 + o : 1280 + o] for r, o in us]
            scores = [nt(kk, widened(qq, bds)) for kk, qq in zip(k, q)]
            e = [jnp.exp(x - jnp.max(x, axis=0, keepdims=True)) for x in scores]
            p = [x * (1.0 / jnp.sum(x, axis=0, keepdims=True)) for x in e]
            wide = [tn(x.astype(BF), vv) for x, vv in zip(p, v)]
            att = [(heads_of(x * bdf) * (1.0 / SCALE)).astype(BF) for x in wide]
            for (r, o), pp, aa in zip(us, p, att):
                s.prob[c, r, o : o + 256] = pp
                s.att[c, r, o : o + 256] = aa

    def window_backward(c, w):
        if True:
            us = units(c, w, WB)
            bds = s.bds[...]
            bd1 = s.bd1[...]
            bdf = s.bdf[...]
            q = [s.qkv[c, r, o : o + 256] for r, o in us]
            k = [s.qkv[c, r, 512 + o : 768 + o] for r, o in us]
            v = [s.qkv[c, r, 1024 + o : 1280 + o] for r, o in us]
            go = [widened(s.gob[r, o : o + 256], bd1) for r, o in us]
            p = [s.prob[c, r, o : o + 256] for r, o in us]
            gp = [nt(vv, gg) for vv, gg in zip(v, go)]
            gv = [nn(pp.astype(BF), gg).astype(BF) for pp, gg in zip(p, go)]
            gs = [
                (pp * (x - jnp.sum(x * pp, axis=0, keepdims=True))).astype(BF)
                for pp, x in zip(p, gp)
            ]
            gk = [nn(x, widened(qq, bds)).astype(BF) for x, qq in zip(gs, q)]
            gq = [heads_of(tn(x, kk) * bdf).astype(BF) for x, kk in zip(gs, k)]
            for (r, o), a, b, d in zip(us, gq, gk, gv):
                s.qkv[c, r, o : o + 256] = a
                s.qkv[c, r, 512 + o : 768 + o] = b
                s.qkv[c, r, 1024 + o : 1280 + o] = d

    def head_sums(v):
        return nn(v, s.bd1[...])

    CR = 256

    def frames_forward(c):
        late0 = orders_ref[c, 0] > orders_ref[c, 1]
        sign = jnp.where(late0, 1.0, -1.0).astype(F32)
        r0 = slice(0, GRID)
        r1 = slice(GRID, CLIP)
        for quad in range(2):
            qc = slice(256 * quad, 256 * quad + 256)
            kc = slice(512 + 256 * quad, 768 + 256 * quad)
            vc = slice(1024 + 256 * quad, 1280 + 256 * quad)
            q_late = jnp.where(late0, s.qkv[c, r0, qc], s.qkv[c, r1, qc])
            k_diff = s.qkv[c, r1, kc] - s.qkv[c, r0, kc]
            v0 = s.qkv[c, r0, vc]
            v1 = s.qkv[c, r1, vc]
            d = head_sums(q_late * k_diff) * (sign * SCALE)
            e = jnp.exp(-jnp.abs(d))
            big = 1.0 / (1.0 + e)
            small = e * big
            p_other = jnp.where(d > 0.0, big, small)
            p_self = jnp.where(d > 0.0, small, big)
            s.prob[c, r0, qc] = p_other
            s.prob[c, r1, qc] = p_self
            p0 = jnp.where(late0, p_self, p_other).astype(BF)
            p1 = jnp.where(late0, p_other, p_self).astype(BF)
            mix = (p0.astype(F32) * v0.astype(F32) + p1.astype(F32) * v1.astype(F32)).astype(BF)
            s.att[c, r0, qc] = jnp.where(late0, mix, v0)
            s.att[c, r1, qc] = jnp.where(late0, v1, mix)

    def frames_backward(c):
        late0 = orders_ref[c, 0] > orders_ref[c, 1]
        r0 = slice(0, GRID)
        r1 = slice(GRID, CLIP)
        for quad in range(2):
            qc = slice(256 * quad, 256 * quad + 256)
            kc = slice(512 + 256 * quad, 768 + 256 * quad)
            vc = slice(1024 + 256 * quad, 1280 + 256 * quad)
            q_late = jnp.where(late0, s.qkv[c, r0, qc], s.qkv[c, r1, qc])
            k_diff = s.qkv[c, r1, kc] - s.qkv[c, r0, kc]
            v_diff = s.qkv[c, r1, vc] - s.qkv[c, r0, vc]
            go0 = s.gob[r0, qc]
            go1 = s.gob[r1, qc]
            go_late = jnp.where(late0, go0, go1)
            go_early = jnp.where(late0, go1, go0)
            p_other = s.prob[c, r0, qc]
            p_self = s.prob[c, r1, qc]
            gs = (p_other * p_self * head_sums(go_late * v_diff)).astype(BF).astype(F32) * SCALE
            gq = (gs * k_diff.astype(F32)).astype(BF)
            gk = gs * q_late.astype(F32)
            late32 = go_late.astype(F32)
            gv_late = (p_self.astype(BF).astype(F32) * late32).astype(BF)
            gv_early = (go_early.astype(F32) + p_other.astype(BF).astype(F32) * late32).astype(BF)
            none = jnp.zeros_like(gq)
            s.qkv[c, r0, qc] = jnp.where(late0, gq, none)
            s.qkv[c, r1, qc] = jnp.where(late0, none, gq)
            s.qkv[c, r0, kc] = (-gk).astype(BF)
            s.qkv[c, r1, kc] = gk.astype(BF)
            s.qkv[c, r0, vc] = jnp.where(late0, gv_late, gv_early)
            s.qkv[c, r1, vc] = jnp.where(late0, gv_early, gv_late)

    def gain_terms(which, grad, xhat):
        part = jnp.sum((grad * xhat).reshape(-1, 8, D), axis=0)
        s.gacc[which] += part

    def back_down_codes(c):
        twice = jnp.concatenate([s.cvec[c][0:8].astype(F32)] * 2, axis=0).astype(BF)
        for j in range(4):
            cols = slice(512 * j, 512 * j + 512)
            s.gel[c, :, cols] = (tn(twice, s.m8[:, cols]) * s.gel[c, :, cols].astype(F32)).astype(BF)

    def back_up(c, grad_of):
        acc = None
        for j in range(4):
            term = nt(s.gel[c, :, 512 * j : 512 * j + 512], s.win[:, 2048 + 512 * j : 2560 + 512 * j])
            acc = term if acc is None else acc + term
        xh = s.xh2[c]
        gain_terms(1, acc, xh)
        gm = grad_of() + normed_back(acc, xh, s.r2[c], gain_two)
        s.hb[...] = gm
        gy = gm.astype(BF)
        s.gy[c] = gy
        s.gob[...] = nt(gy, s.win[:, 1536:2048]).astype(BF)

    def back_in(c):
        acc = None
        for j in range(3):
            cols = slice(512 * j, 512 * j + 512)
            term = nt(s.qkv[c, :, cols], s.win[:, cols])
            acc = term if acc is None else acc + term
        xh = s.xh1[c]
        gain_terms(0, acc, xh)
        return s.hb[...] + normed_back(acc, xh, s.r1[c], gain_one)

    def add_into(ref, rows, cols, c, value):
        ref[rows, cols] = jnp.where(c == 0, value, ref[rows, cols] + value)

    def grad_down(c):
        for j in range(4):
            cols = slice(512 * j, 512 * j + 512)
            add_into(s.acc_dn, cols, slice(None), c, tn(s.act[c, :, cols], s.xs[c]))

    def grad_down_codes(c):
        code = s.cvec[c][0:8].astype(F32)
        wide = jnp.concatenate([jnp.zeros((80, CLIP), F32)] + [code] * 4 + [jnp.zeros((16, CLIP), F32)], axis=0)
        wide = wide.astype(BF)
        lanes = (iota((8, 128), 1) >> 3) - 10
        for j in range(4):
            v = tt(s.act[c, :, 512 * j : 512 * j + 512], wide).reshape(16, 4, 8, 128)
            picked = [jnp.where(lanes == m, v[:, m], 0.0) for m in range(4)]
            s.s_acc[j] += total(picked).reshape(8, 2, 8, 128)

    def grad_qkv_codes(c):
        norm_row = jnp.transpose(jnp.broadcast_to(s.r1[c], (CLIP, 128)))[0:1, :]
        part = nn(pad16(s.cvec[c][0:8].astype(F32) * norm_row), s.qkv[c])[0:8]
        for half in range(2):
            v = part[:, 768 * half : 768 * half + 768]
            s.q8[half] = jnp.where(c == 0, v, s.q8[half] + v)

    def grad_up(c):
        for j in range(4):
            cols = slice(512 * j, 512 * j + 512)
            add_into(s.acc_up, slice(None), cols, c, tn(s.a2[c], s.gel[c, :, cols]))

    def grad_out(c):
        add_into(s.acc_out, slice(None), slice(None), c, tn(s.att[c], s.gy[c]))

    def grad_attn(c):
        for j in range(3):
            cols = slice(512 * j, 512 * j + 512)
            add_into(s.acc_qkv, slice(None), cols, c, tn(s.a1[c], s.qkv[c, :, cols]))

    def share(k, i, to_core):
        n = 2 * i + to_core
        if k == "a":
            return s.acc_dn[pl.ds(pl.multiple_of(n * 32, 32), 32), :]
        rows = pl.ds(pl.multiple_of(n * 8, 8), 8)
        ref, w = {"b": (s.acc_up, 1024), "c": (s.acc_qkv, 768), "o": (s.acc_out, 256)}[k]
        return jnp.concatenate([ref[rows, 0:w], ref[rows, w : 2 * w]], axis=0)

    def buf(name, k):
        return getattr(s, name + k)

    def copies(k, step):
        if k == "s":
            if step == 0:
                return [rcopy("s0", s.s_acc.at[:, :, 1 - core], s.s0, core_dev)]
            if step == 1:
                return [rcopy("s1%d" % i, s.s0.at[(z + 1 + i) % 4], s.s1.at[i], z_dev[i]) for i in range(3)]
            return [
                rcopy(
                    "s2%d" % i, s.s0.at[z, 2 * ((x + d) % 4) + (yh + y) % 2], s.s2.at[i], xy_dev[i]
                )
                for i, (d, y) in enumerate(around)
            ]
        if k == "q":
            if step == 0:
                return [rcopy("q0", s.q8.at[1 - core], s.q0, core_dev)]
            if step == 1:
                return [rcopy("q1%d" % i, s.qs1, s.qz.at[i], z_dev[i]) for i in range(3)]
            if step == 2:
                return [rcopy("q2%d" % i, s.qs2, s.qx.at[i], x_dev[i]) for i in range(3)]
            if step == 3:
                return [rcopy("q3", s.qs3, s.qy, y_dev)]
            return [rcopy("q4", s.qs4, s.qg, core_dev)]
        rows, w = CHUNKS[k]
        h = w // 2
        r0 = buf("r0", k)
        if step == 0:
            return [rcopy(k + "0", buf("sb0", k), r0, core_dev)]
        lo, hi = pl.ds(0, h), pl.ds(h, h)
        out = []
        if step == 4:
            for i, (d, y) in enumerate(around):
                out.append(
                    rcopy(
                        "%s4x%d" % (k, i), r0.at[z, (x + d) % 4, (yh + y) % 2, :, lo],
                        buf("px", k).at[i], xy_dev[i],
                    )
                )
                out.append(
                    rcopy(
                        "%s4z%d" % (k, i), r0.at[(z + d) % 4, x, (yh + y) % 2, :, hi],
                        buf("pz", k).at[i], zy_dev[i],
                    )
                )
            return out
        for y in range(2):
            first, second = ((1, 3), (3, 1))[y]
            hop = second if step == 3 else first
            block = {1: 2, 2: first, 3: second}[step]
            slot = {1: "q1", 2: "q0", 3: "q2"}[step]
            out.append(
                rcopy(
                    "%s%dz%d" % (k, step, y), r0.at[z_flip[block], :, y, :, lo],
                    buf(slot + "z", k).at[y], place(z_flip[hop], x, yh, core),
                )
            )
            out.append(
                rcopy(
                    "%s%dx%d" % (k, step, y), r0.at[:, x_flip[block], y, :, hi],
                    buf(slot + "x", k).at[y], place(z, x_flip[hop], yh, core),
                )
            )
        return out

    def arrived(k, step):
        for cp in copies(k, step):
            cp.wait_recv()

    def send(k, step):
        for cp in copies(k, step):
            cp.start()

    def put_down(mine):
        gdn_ref[0] = mine
        piece = s.wdn[pl.ds(dp * 32, 32), :].astype(F32)
        adn_ref[0] = AVG_DECAY * s.avd[...] + (1.0 - AVG_DECAY) * (piece - LEARN_RATE * mine)

    def reduce_step(k, step):
        if k == "s":
            if step > 0:
                arrived(k, step - 1)
            if step == 1:
                s.s0[...] += s.s_acc[:, :, core]
            elif step == 2:
                s.s0[z] += (s.s1[0] + s.s1[1]) + s.s1[2]
            elif step == 3:
                small = total([s.s0[z, 2 * x + yh]] + [s.s2[i] for i in range(7)])
                small_ref[...] = small

                @pl.when(is_e)
                def _():
                    narrow = proj_t.astype(F32)
                    shares = [
                        total([small[:, n : n + 1] * narrow[n % 8 : n % 8 + 1, :] for n in range(80 + 8 * m, 88 + 8 * m)])
                        for m in range(4)
                    ]
                    put_down(jnp.concatenate(shares, axis=0))

                return
            send(k, step)
            return
        if k == "q":
            if step > 0:
                arrived(k, step - 1)
            if step == 1:
                s.qs1[...] = s.q8[core] + s.q0[...]
            elif step == 2:
                s.qs2[...] = total([s.qs1[...]] + [s.qz[i] for i in range(3)])
            elif step == 3:
                s.qs3[...] = total([s.qs2[...]] + [s.qx[i] for i in range(3)])
            elif step == 4:
                s.qs4[...] = s.qs3[...] + s.qy[...]
            elif step == 5:
                mine, other = s.qs4[...], s.qg[...]
                narrow = s.pgt[pl.ds(pl.multiple_of(dp * 8, 8), 8), :]
                for half, v in enumerate((jnp.where(core == 0, mine, other), jnp.where(core == 0, other, mine))):
                    gin_ref[0, :, 768 * half : 768 * half + 768] = total(
                        [narrow[:, n : n + 1] * v[n : n + 1, :] for n in range(8)]
                    )
                return
            send(k, step)
            return
        rows, w = CHUNKS[k]
        h = w // 2
        r0 = buf("r0", k)
        lo, hi = pl.ds(0, h), pl.ds(h, h)
        if step == 0:
            sb0 = buf("sb0", k)

            def body(i, carry):
                for y in range(2):
                    sb0[i // 4, i % 4, y] = share(k, 2 * i + y, 1 - core).astype(BF)
                return carry

            lax.fori_loop(0, 16, body, 0)
            send(k, 0)
        elif step == 1:
            arrived(k, 0)

            def body(i, carry):
                for y in range(2):
                    r0[i // 4, i % 4, y] = total([share(k, 2 * i + y, core), r0[i // 4, i % 4, y]]).astype(BF)
                return carry

            lax.fori_loop(0, 16, body, 0)
            send(k, 1)
            send(k, 2)
        elif step == 2:
            arrived(k, 1)
            for y in range(2):
                second = (3, 1)[y]
                zb, xb = z_flip[second], x_flip[second]
                r0[zb, :, y, :, lo] = total([r0[zb, :, y, :, lo], buf("q1z", k)[y]]).astype(BF)
                r0[:, xb, y, :, hi] = total([r0[:, xb, y, :, hi], buf("q1x", k)[y]]).astype(BF)
            send(k, 3)
        elif step == 3:
            arrived(k, 2)
            arrived(k, 3)
            for y in range(2):
                r0[z, :, y, :, lo] = total(
                    [r0[z, :, y, :, lo], buf("q0z", k)[y], buf("q2z", k)[y]]
                ).astype(BF)
                r0[:, x, y, :, hi] = total(
                    [r0[:, x, y, :, hi], buf("q0x", k)[y], buf("q2x", k)[y]]
                ).astype(BF)
            send(k, 4)
        else:
            arrived(k, 4)
            left = total([r0[z, x, yh, :, lo]] + [buf("px", k)[i] for i in range(7)])
            right = total([r0[z, x, yh, :, hi]] + [buf("pz", k)[i] for i in range(7)])
            mine = jnp.concatenate([left, right], axis=1)
            if k == "a":
                put_down(mine)
            else:
                first = {"b": 2048, "c": 0, "o": 1536}[k]
                gin_ref[0, :, first : first + w] = mine[0:8]
                gin_ref[0, :, first + w : first + 2 * w] = mine[8:16]

    def add_gains():
        sums = jnp.concatenate(
            [
                jnp.sum(s.gacc[0], axis=0, keepdims=True),
                jnp.sum(s.gacc[1], axis=0, keepdims=True),
                jnp.zeros((6, D), F32),
            ],
            axis=0,
        )
        wide_sums = jnp.concatenate([jnp.zeros((72, D), F32), sums, jnp.zeros((48, D), F32)], axis=0)
        s.s_acc[...] += jnp.transpose(wide_sums).reshape(4, 8, 2, 8, 128)

    def code_copy(c):
        return pltpu.make_async_remote_copy(
            src_ref=s.fcs.at[c], dst_ref=s.fcr.at[c], send_sem=send_sems.at[N_SEM - 2 + c],
            recv_sem=recv_sems.at[N_SEM - 2 + c], device_id=sec_dev, device_id_type=MESH,
        )

    def grad_copy(c):
        return pltpu.make_async_remote_copy(
            src_ref=s.cxs.at[c], dst_ref=s.cxr.at[c], send_sem=send_sems.at[N_SEM - 4 + c],
            recv_sem=recv_sems.at[N_SEM - 4 + c], device_id=sec_dev, device_id_type=MESH,
        )

    @pl.when(is_e)
    def _():
        for c in range(2):
            grid_now = grids_ref[c]
            width = jnp.where(grid_now == 0, 16, jnp.where(grid_now == 1, 32, 8)).astype(I32)
            log_across = jnp.where(grid_now == 0, 1, jnp.where(grid_now == 1, 2, 0)).astype(I32)
            across_mask = jnp.where(grid_now == 0, 1, jnp.where(grid_now == 1, 3, 0)).astype(I32)
            window_no = rows_i >> 6
            inner = rows_i & 63
            source = (
                ((window_no >> log_across) * 8 + (inner >> 3)) * width
                + (window_no & across_mask) * 8
                + (inner & 7)
            )
            s.perm[c] = (source == cols_i).astype(F32).astype(BF)
        loads[0].wait()
        loads[1].wait()

        def forward(c, carry):
            @pl.when(c == 1)
            def _():
                loads[4].wait()

            raster = [s.xs[c, 0:GRID], s.xs[c, GRID:CLIP]]
            @pl.when(c == 0)
            def _():
                book_start()

            norm_qkv(c, [nn(s.perm[c], v) for v in raster])

            window_forward(c, 0)
            window_forward(c, 1)

            @pl.when(c == 0)
            def _():
                loads[2].wait()
                loads[3].wait()

            def put(acc):
                s.eb[c] = acc.astype(BF)

            feed_forward(c, put)
            vec = nt(proj_t, s.eb[c])
            hi = vec.astype(BF).astype(F32)
            mid = (vec - hi).astype(BF).astype(F32)
            parts = jnp.concatenate([hi, mid, vec - hi - mid, jnp.zeros((8, CLIP), F32)], axis=0).astype(BF)
            for f in range(2):
                cols = slice(GRID * f, GRID * f + GRID)
                moved = nn(parts[:, cols], s.perm[c])
                s.fcs[c, :, cols] = (moved[0:8] + moved[8:16]) + moved[16:24]
            code_copy(c).start()
            return carry

        lax.fori_loop(0, 2, forward, 0)
        for j in range(4):
            cols = slice(512 * j, 512 * j + 512)
            m = nt(proj_t, s.wdn[cols, :])
            hi = m.astype(BF).astype(F32)
            s.m8[:, cols] = jnp.concatenate([hi, m - hi], axis=0).astype(BF)

    @pl.when(is_d)
    def _():
        book_start()
        gather_book_start()
        for load in loads:
            load.wait()

        def ahead(c, carry):
            for j in range(4):
                cols = slice(512 * j, 512 * j + 512)
                s.gel[c, :, cols] = nt(s.xs[c], s.wdn[cols, :]).astype(BF)
            return carry

        lax.fori_loop(0, 2, ahead, 0)
        narrow = proj_t.astype(F32)
        narrow = (narrow - jnp.mean(narrow, axis=-1, keepdims=True)) * gain_one
        s.pgt[...] = jnp.transpose(jnp.concatenate([narrow, jnp.zeros((120, D), F32)], axis=0))
        gather_book_wait()

        def both(c, carry):
            entries(c)
            code_copy(c).wait_recv()
            sent = (s.fcr[c] + s.ent[c, 0]).astype(BF).astype(F32)
            s.cvec[c] = pad16(sent + s.ent[c, 1])
            norm_qkv(c, [tn(s.cvec[c][0:8, 0:256], proj_t), tn(s.cvec[c][0:8, 256:512], proj_t)])
            frames_forward(c)

            def put(acc):
                s.bo[pl.ds(c * CLIP, CLIP), :] = acc.astype(BF)

            feed_forward(c, put, ahead=True)
            bout_copy(c).start()
            back_up(c, lambda: s.xs[c].astype(F32))
            frames_backward(c)
            s.eb[c] = back_in(c).astype(BF)
            s.cxs[c] = pad16(nt(proj_t, s.eb[c]))
            grad_copy(c).start()
            return carry

        lax.fori_loop(0, 2, both, 0)

        def downs(c, carry):
            grad_down(c)
            return carry

        def ups(c, carry):
            grad_up(c)
            return carry

        def outs(c, carry):
            grad_out(c)
            return carry

        def codes_of(c, carry):
            grad_qkv_codes(c)
            return carry

        def books(c):
            book_proj_terms(c, s.cxs[c][0:8].astype(F32), s.eb[c], s.cvec[c][0:8].astype(F32))

        lax.fori_loop(0, 2, downs, 0)
        reduce_step("a", 0)
        lax.fori_loop(0, 2, ups, 0)
        reduce_step("b", 0)
        reduce_step("a", 1)
        lax.fori_loop(0, 2, outs, 0)
        reduce_step("o", 0)
        books(0)
        reduce_step("o", 1)
        reduce_step("b", 1)
        books(1)
        reduce_step("a", 2)
        add_gains()
        lax.fori_loop(0, 2, codes_of, 0)
        for load in averages:
            load.wait()
        for item in ["q0", "s0", "q1", "b2", "o2", "a3", "s1", "q2", "b3", "o3", "s2", "q3", "a4", "q4", "o4", "s3", "b4", "q5"]:
            reduce_step(item[0], int(item[1]))

    @pl.when(is_e)
    def _():
        def leave(c):
            for f in range(2):
                back = tn(s.perm[c], s.a2[c, GRID * f : GRID * f + GRID])
                s.bo[pl.ds(c * CLIP + GRID * f, GRID), :] = back.astype(BF)
            bout_copy(c).start()
            book_proj_terms(c, s.cxr[c][0:8].astype(F32), s.eb[c], s.cvec[c][0:8].astype(F32))

        def backward(c, carry):
            grad_copy(c).wait_recv()
            for f in range(2):
                cols = slice(GRID * f, GRID * f + GRID)
                s.cvec[c, :, cols] = nt(s.cxr[c, :, cols], s.perm[c]).astype(BF)
            g = tn(s.cvec[c][0:8], proj_t)
            s.hb[...] = g
            back_down_codes(c)
            grad_up(c)

            @pl.when(c == 1)
            def _():
                reduce_step("b", 0)

            back_up(c, lambda: s.hb[...])
            window_backward(c, 0)

            @pl.when(c == 1)
            def _():
                reduce_step("b", 1)

            window_backward(c, 1)
            grad_attn(c)

            @pl.when(c == 1)
            def _():
                reduce_step("c", 0)

            grad_out(c)

            @pl.when(c == 1)
            def _():
                reduce_step("o", 0)
                leave(0)
                reduce_step("b", 2)
                reduce_step("c", 1)

            s.a2[c] = back_in(c).astype(BF)
            return carry

        lax.fori_loop(0, 2, backward, 0)
        reduce_step("o", 1)

        leave(1)
        reduce_step("c", 2)
        reduce_step("b", 3)

        def downs(c, carry):
            grad_down_codes(c)
            return carry

        lax.fori_loop(0, 2, downs, 0)
        add_gains()
        for load in averages:
            load.wait()
        for item in ["o2", "s0", "s1", "c3", "o3", "s2", "c4", "b4", "o4", "s3"]:
            reduce_step(item[0], int(item[1]))

    half_rows = s.win[pl.ds(16 * (dp // 2), 16), :].astype(F32)
    piece = jnp.where(core == 0, half_rows[0:8], half_rows[8:16])
    ain_ref[0] = AVG_DECAY * s.avi[...] + (1.0 - AVG_DECAY) * (piece - LEARN_RATE * gin_ref[0])

    for c in range(2):
        bout_copy(c).wait()

        @pl.when(is_e)
        def _():
            code_copy(c).wait_send()

        @pl.when(is_d)
        def _():
            grad_copy(c).wait_send()

    book_finish()
    def finish(chunks):
        for k in chunks:
            for step in {"s": (0, 1, 2)}.get(k, (0, 1, 2, 3, 4)):
                for cp in copies(k, step):
                    cp.wait_send()

    @pl.when(is_e)
    def _():
        finish("bcos")

    @pl.when(is_d)
    def _():
        finish("abosq")


def body(
    boundary, in_weights, down_weight, gains, proj, codebook, codes, grids, orders, avg_in, avg_down
):
    vmem = pl.BlockSpec(memory_space=pltpu.VMEM)
    smem = pl.BlockSpec(memory_space=pltpu.SMEM)
    hbm = pl.BlockSpec(memory_space=pl.ANY)
    outs = (
        jax.ShapeDtypeStruct(boundary.shape, BF),
        jax.ShapeDtypeStruct(avg_in.shape, F32),
        jax.ShapeDtypeStruct(avg_down.shape, F32),
        jax.ShapeDtypeStruct((8, 128), F32),
        jax.ShapeDtypeStruct(avg_in.shape, F32),
        jax.ShapeDtypeStruct(avg_down.shape, F32),
    )
    scratch = [pltpu.VMEM(shape, dtype) for shape, dtype in SHAPES.values()]
    scratch += [pltpu.SemaphoreType.DMA((N_SEM,)), pltpu.SemaphoreType.DMA((N_SEM,)), pltpu.SemaphoreType.DMA((9,))]
    made = pl.pallas_call(
        mega,
        out_shape=outs,
        in_specs=[hbm, hbm, hbm, vmem, vmem, vmem, vmem, smem, smem, hbm, hbm],
        out_specs=[hbm] + [vmem] * 5,
        scratch_shapes=scratch,
        compiler_params=pltpu.CompilerParams(
            collective_id=0, has_side_effects=True, vmem_limit_bytes=63 << 20
        ),
        name="both_sections",
    )(
        boundary, in_weights, down_weight, gains, proj[0].T, codebook, codes.reshape(8, 128), grids, orders,
        avg_in, avg_down,
    )
    return pl.pallas_call(
        split_outputs,
        out_shape=(
            outs[0], outs[1], outs[2],
            jax.ShapeDtypeStruct((1, 2, 8), F32),
            jax.ShapeDtypeStruct((1, 8, 8), F32),
            jax.ShapeDtypeStruct(codebook.shape, F32),
            outs[4], outs[5],
        ),
        in_specs=[vmem] * 6,
        out_specs=[vmem] * 8,
        name="split_outputs",
    )(*made)


def split_outputs(
    bout_in, gin_in, gdn_in, small_in, ain_in, adn_in,
    bout, gin, gdn, ggain, gproj, gbook, ain, adn,
):
    bout[...] = bout_in[...]
    gin[...] = gin_in[...]
    gdn[...] = gdn_in[...]
    ain[...] = ain_in[...]
    adn[...] = adn_in[...]
    small = small_in[...]
    gbook[...] = small[:, 0:64]
    gproj[0] = small[:, 64:72]
    ggain[0] = jnp.transpose(jnp.concatenate([small] * 16, axis=0))[72:74, 0:8]


def solution(mesh):
    placed = (
        P("section", "dp", None),
        P("section", None, None),
        P("section", None, None),
        P("section", None, None),
        P("section", None, None),
        P(None, ("section", "dp")),
        P("dp"),
        P("dp"),
        P("dp", None),
        P("section", "dp", None),
        P("section", "dp", None),
    )
    return jax.shard_map(
        body,
        mesh=mesh,
        in_specs=placed,
        out_specs=(
            P("section", "dp", None),
            P("section", "dp", None),
            P("section", "dp", None),
            P("section", None, "dp"),
            P("section", "dp", None),
            P(None, ("section", "dp")),
            P("section", "dp", None),
            P("section", "dp", None),
        ),
        check_vma=False,
    )
```
